512 devices in a mesh: replica: 4 (over y), context: 16 (over x, z_hi), tensor: 8 (over z_lo, core).
Axes of the slice: x: 4, y: 4, z: 16 (z_hi: 4, z_lo: 4; z = z_hi * 4 + z_lo), core: 2. Of those that a mesh axis runs over, the one named last changes fastest.
Arguments:
- hidden: bfloat16 [4, 2048, 7168], P('replica', 'context', 'tensor'), may hold values from -40 to 40
- q_nope: bfloat16 [4, 2048, 8192], P('replica', 'context', 'tensor'), may hold values from -6 to 6
- q_rope: bfloat16 [4, 2048, 4096], P('replica', 'context', 'tensor'), may hold values from -8 to 8
- w_latent: bfloat16 [7168, 512], P('tensor'), may hold values from -5 to 5
- w_krope: bfloat16 [7168, 64], P('tensor'), may hold values from -0.0625 to 0.0625
- kv_gain: float32 [512], replicated, may hold values from 0.1 to 1.9
- w_uk: bfloat16 [64, 128, 512], P('tensor'), may hold values from -0.5 to 0.5
- w_uv: bfloat16 [64, 512, 128], P('tensor'), may hold values from -1 to 1
- prefix_latent: bfloat16 [4, 1024, 512], P('replica', 'context'), may hold values from -6 to 6
- prefix_rope: bfloat16 [4, 1024, 64], P('replica', 'context'), may hold values from -8 to 8
- prefix_lengths: int32 [4], P('replica'), may hold values from 2 to 1024
- placements: int32 [16, 8], P('context'), may hold values from 0 to 7, each once within a row
Outputs:
- attention: bfloat16 [4, 2048, 8192], P('replica', 'context', 'tensor')
- cache_latent: bfloat16 [4, 32, 32768], P('replica', 'context')
- cache_rope: bfloat16 [4, 32, 4096], P('replica', 'context')
- cache_scale: bfloat16 [4, 32, 256], P('replica', 'context')
The draws below stay inside these ranges and needn't reach their ends.
Inputs may be any that keep to these rules, and one draw needn't show every extreme that they name: `placements`: each row names every owner slot exactly once.
All inputs are finite; a program needn't handle non-finite values.
Results may differ from the reference program's by a relative error of at most 0.0091.
Values may be sent and summed in bfloat16 or wider, within the bound.
A program may use at most 64 MiB of HBM per device.

```python
import math
import jax
import jax.numpy as jnp
from jax import lax

D = 7168
HEADS = 64
NOPE = 128
ROPE = 64
LAT = 512
VDIM = 128
TOK_DEV = 128
PRE_DEV = 64
BLOCK = 64
TILES = 4
SPAN = 2048
PREFIX = 1024
BLK_DEV = 2
N_REPLICA = 4
N_CONTEXT = 16


def draw_prefix_rope(key, part):
    key = jax.random.fold_in(key, 3)
    shape = (N_REPLICA, PREFIX, ROPE)
    entries = jnp.clip(jax.random.normal(key, shape, jnp.float32), -4.0, 4.0)
    return entries.astype(jnp.bfloat16)


def draw_q_rope(key, part):
    key = jax.random.fold_in(key, 4)
    shape = (N_REPLICA, SPAN, HEADS * ROPE)
    entries = jnp.clip(jax.random.normal(key, shape, jnp.float32), -4.0, 4.0)
    return entries.astype(jnp.bfloat16)


def draw_hidden(key, part):
    key = jax.random.fold_in(key, 5)
    scale_key, entry_key = jax.random.split(key, 2)
    shape = (N_REPLICA, SPAN, D)
    row_scale = jnp.exp(jax.random.uniform(scale_key, (N_REPLICA, SPAN, 1), jnp.float32, 0.0, math.log(10.0)))
    entries = jnp.clip(jax.random.normal(entry_key, shape, jnp.float32), -4.0, 4.0)
    return (entries * row_scale).astype(jnp.bfloat16)


def draw_w_latent(key, part):
    key = jax.random.fold_in(key, 6)
    column_key, entry_key = jax.random.split(key, 2)
    column_scale = jnp.exp(jax.random.uniform(column_key, (1, LAT), jnp.float32, 0.0, math.log(10.0)))
    entries = jnp.clip(jax.random.normal(entry_key, (D, LAT), jnp.float32), -4.0, 4.0)
    return (entries * column_scale / math.sqrt(D)).astype(jnp.bfloat16)


def touch_ends(values, stream_key, least, high):
    dims = values.shape
    spot = [jax.random.randint(jax.random.fold_in(stream_key, axis), (), 0, dims[axis]) for axis in range(len(dims))]
    values = values.at[tuple(spot)].set(least)
    longest = dims.index(max(dims))
    spot[longest] = (spot[longest] + 1) % dims[longest]
    return values.at[tuple(spot)].set(high)


def block_levels(own_key, extent, cuts, least, largest):
    def one(position, parts):
        steps = jax.random.uniform(jax.random.fold_in(jax.random.fold_in(own_key, 6), position), (parts,), jnp.float32, least / len(cuts), largest / len(cuts))
        return jnp.repeat(jnp.exp(steps), extent[position] // parts).reshape((-1,) + (1,) * (len(extent) - position - 1))

    loudness = one(*cuts[0])
    for cut in cuts[1:]:
        loudness = loudness * one(*cut)
    return loudness


def normal_values(stream_key, dims, deviation, limit, shards=(), kind=jnp.bfloat16):
    values = deviation * jax.random.normal(stream_key, dims, jnp.float32)
    if shards:
        values = values * block_levels(stream_key, dims, shards, -0.22, 0.18)
    return jnp.clip(values, -limit, limit).astype(kind)


def setup_inputs(seed: int = 0) -> dict:
    arg_keys = jax.random.split(jax.random.key(seed), 13)
    return {
        "hidden": draw_hidden(jax.random.fold_in(arg_keys[12], 71), 0),
        "q_nope": normal_values(arg_keys[1], (N_REPLICA, SPAN, HEADS * NOPE), 1.0, 6.0, ((0, 4), (1, 16), (2, 8))),
        "q_rope": draw_q_rope(jax.random.fold_in(arg_keys[12], 71), 0),
        "w_latent": draw_w_latent(jax.random.fold_in(arg_keys[12], 71), 0),
        "w_krope": normal_values(arg_keys[4], (D, ROPE), D ** -0.5, 0.0625, ((0, 8),)),
        "kv_gain": jnp.clip(1.0 + 0.18 * jax.random.normal(arg_keys[5], (LAT,), jnp.float32), 0.1, 1.9),
        "w_uk": normal_values(arg_keys[6], (HEADS, NOPE, LAT), NOPE ** -0.5, 0.5, ((0, 8),)),
        "w_uv": normal_values(arg_keys[7], (HEADS, LAT, VDIM), (LAT // 16) ** -0.5, 1.0, ((0, 8),)),
        "prefix_latent": normal_values(arg_keys[8], (N_REPLICA, PREFIX, LAT), 1.0, 6.0, ((0, 4), (1, 16))),
        "prefix_rope": draw_prefix_rope(jax.random.fold_in(arg_keys[12], 71), 0),
        "prefix_lengths": touch_ends(jax.random.randint(arg_keys[10], (N_REPLICA,), 2, PREFIX + 1), jax.random.fold_in(arg_keys[10], 1), 2, PREFIX).astype(jnp.int32),
        "placements": jax.vmap(lambda own: jax.random.permutation(own, N_REPLICA * BLK_DEV))(jax.random.split(arg_keys[11], N_CONTEXT)).reshape((N_CONTEXT, N_REPLICA * BLK_DEV)).astype(jnp.int32),
    }


rope_theta = 50000.0
norm_eps = 1e-06
scale_eps = 1e-06
masked_score = -1e+30

def rotate(entries, positions):
    half_width = entries.shape[1] // 2
    frequency = rope_theta ** (-(jnp.arange(half_width, dtype=jnp.float32) * 2.0) / entries.shape[1])
    angles = positions.astype(jnp.float32)[:, None] * frequency[None, :]
    cosine_part = jnp.cos(angles)
    sine_part = jnp.sin(angles)
    leading = entries[:, :half_width]
    trailing = entries[:, half_width:]
    return jnp.concatenate([leading * cosine_part - trailing * sine_part, trailing * cosine_part + leading * sine_part], axis=1)

def finish(lat_sum, rope_sum, kv_gain, positions):
    mean_square = lax.optimization_barrier(jnp.mean(lat_sum * lat_sum, axis=1, keepdims=True))
    key_latent = (lat_sum * lax.rsqrt(mean_square + norm_eps) * kv_gain).astype(jnp.bfloat16)
    return (key_latent, rotate(rope_sum, positions).astype(jnp.bfloat16))

def quantize(key_latent, tile_count):
    row_count = key_latent.shape[0]
    entries = key_latent.astype(jnp.float32).reshape(row_count, tile_count, key_latent.shape[1] // tile_count)
    tile_scale = (lax.optimization_barrier(jnp.max(jnp.abs(entries), axis=2)) + scale_eps).astype(jnp.bfloat16)
    scale_back = lax.optimization_barrier(tile_scale).astype(jnp.float32)
    stored = (entries / scale_back[:, :, None]).astype(jnp.bfloat16).reshape(row_count, key_latent.shape[1])
    return (stored, tile_scale)

def reference(hidden, q_nope, q_rope, w_latent, w_krope, kv_gain, w_uk, w_uv, prefix_latent, prefix_rope, prefix_lengths, placements):
    score_scale = (NOPE + ROPE) ** (-0.5)
    blk_dev = TOK_DEV // BLOCK
    span_rows = TOK_DEV * N_CONTEXT
    prefix_rows = PRE_DEV * N_CONTEXT
    results = []
    latent_blocks = []
    rope_blocks = []
    scale_blocks = []
    for replica in range(N_REPLICA):
        lat_sum = jnp.dot(hidden[replica], w_latent, preferred_element_type=jnp.float32)
        rope_sum = jnp.dot(hidden[replica], w_krope, preferred_element_type=jnp.float32)
        length = prefix_lengths[replica]
        positions = length + jnp.arange(span_rows, dtype=jnp.int32)
        key_latent, key_rope = finish(lat_sum, rope_sum, kv_gain, positions)
        all_lat = jnp.concatenate([prefix_latent[replica], key_latent], axis=0)
        all_rope = jnp.concatenate([prefix_rope[replica], key_rope], axis=0)
        key_index = jnp.arange(prefix_rows + span_rows, dtype=jnp.int32)
        query_index = jnp.arange(span_rows, dtype=jnp.int32)
        visible = jnp.where(key_index[None, :] < prefix_rows, key_index[None, :] < length, key_index[None, :] - prefix_rows <= query_index[:, None])
        nope_heads = jnp.transpose(q_nope[replica].reshape(span_rows, HEADS, NOPE), (1, 0, 2))
        rope_heads = jnp.transpose(q_rope[replica].reshape(span_rows, HEADS, ROPE), (1, 0, 2))

        def one_head(operands):
            query_nope, query_rope, absorb, expand = operands
            absorbed = jnp.dot(query_nope, absorb, preferred_element_type=jnp.float32).astype(jnp.bfloat16)
            scores = jnp.dot(absorbed, all_lat.T, preferred_element_type=jnp.float32)
            scores = (scores + jnp.dot(query_rope, all_rope.T, preferred_element_type=jnp.float32)) * score_scale
            scores = jnp.where(visible, scores, masked_score)
            row_max = lax.optimization_barrier(jnp.max(scores, axis=1, keepdims=True))
            exponents = jnp.where(visible, jnp.exp(scores - row_max), 0.0)
            row_sum = lax.optimization_barrier(jnp.sum(exponents, axis=1, keepdims=True))
            weights = exponents.astype(jnp.bfloat16)
            latent_out = (jnp.dot(weights, all_lat, preferred_element_type=jnp.float32) / row_sum).astype(jnp.bfloat16)
            return jnp.dot(latent_out, expand, preferred_element_type=jnp.float32).astype(jnp.bfloat16)
        per_head = lax.map(one_head, (nope_heads, rope_heads, w_uk, w_uv))
        results.append(jnp.transpose(per_head, (1, 0, 2)).reshape(span_rows, HEADS * VDIM))
        stored, tile_scale = quantize(key_latent, TILES)
        latent_blocks.append(stored.reshape(span_rows // BLOCK, BLOCK * LAT))
        rope_blocks.append(key_rope.reshape(span_rows // BLOCK, BLOCK * ROPE))
        scale_blocks.append(tile_scale.reshape(span_rows // BLOCK, BLOCK * TILES))

    def route_blocks(blocks):
        row_width = blocks.shape[-1]
        grouped = jnp.transpose(blocks.reshape(N_REPLICA, N_CONTEXT, blk_dev, row_width), (1, 0, 2, 3)).reshape(N_CONTEXT, N_REPLICA * blk_dev, row_width)
        context_rows = jnp.arange(N_CONTEXT, dtype=jnp.int32)[:, None]
        placed = jnp.zeros_like(grouped).at[context_rows, placements].set(grouped)
        return jnp.transpose(placed.reshape(N_CONTEXT, N_REPLICA, blk_dev, row_width), (1, 0, 2, 3)).reshape(N_REPLICA, N_CONTEXT * blk_dev, row_width)
    attention = jnp.stack(results, axis=0)
    cache_latent = route_blocks(jnp.stack(latent_blocks, axis=0))
    cache_rope = route_blocks(jnp.stack(rope_blocks, axis=0))
    cache_scale = route_blocks(jnp.stack(scale_blocks, axis=0))
    return (attention, cache_latent, cache_rope, cache_scale)
```

```python
import functools
import math

import jax
import jax.numpy as jnp
import numpy as np
from jax import lax
from jax.experimental import pallas as pl
from jax.experimental.pallas import tpu as pltpu
from jax.sharding import PartitionSpec as P

MESH = pl.DeviceIdType.MESH
BLOCK = 64
TILES = 4
PIECE = 16
COLUMNS = 512
ROPE_THETA = 50000.0
NORM_EPS = 1e-06
SCALE_EPS = 1e-06
MASKED = -1e30
FLOOR = -1e29
FAR = 1 << 20


def when(condition, action):
    if isinstance(condition, bool):
        if condition:
            action()
    else:
        pl.when(condition)(action)


def both(*conditions):
    static = [c for c in conditions if isinstance(c, bool)]
    traced = [c for c in conditions if not isinstance(c, bool)]
    if not all(static):
        return False
    if not traced:
        return True
    out = traced[0]
    for c in traced[1:]:
        out = jnp.logical_and(out, c)
    return out


def sine_cosine(angle):
    turns = jnp.floor(angle * np.float32(1.0 / (2.0 * math.pi)) + 0.5)
    high = 6.28125
    middle = float(np.float32(0.0019350051879882812))
    low = 2.0 * math.pi - high - middle
    r = angle - turns * np.float32(high)
    r = r - turns * np.float32(middle)
    r = r - turns * np.float32(low)
    square = r * r
    sine = jnp.full_like(r, 1.0 / math.factorial(17))
    for n in (15, 13, 11, 9, 7, 5, 3, 1):
        sign = -1.0 if (n // 2) % 2 else 1.0
        sine = sine * square + sign / math.factorial(n)
    cosine = jnp.full_like(r, 1.0 / math.factorial(16))
    for n in (14, 12, 10, 8, 6, 4, 2, 0):
        sign = -1.0 if (n // 2) % 2 else 1.0
        cosine = cosine * square + sign / math.factorial(n)
    return sine * r, cosine


def kernel(
    shape,
    length_ref,
    places_ref,
    frequency_ref,
    gain_ref,
    hidden_hbm,
    q_nope_hbm,
    q_rope_hbm,
    w_latent_hbm,
    w_krope_hbm,
    w_uk_hbm,
    w_uv_hbm,
    pre_lat_hbm,
    pre_rope_hbm,
    out_ref,
    cache_lat_ref,
    cache_rope_ref,
    cache_scale_ref,
    hidden,
    q_nope,
    q_rope,
    w_latent,
    w_krope,
    w_uk,
    w_uv,
    pre_lat,
    pre_rope,
    partial,
    partner_part,
    chip_sum,
    group_part,
    keys,
    blocks,
    queries,
    total,
    top,
    weight_sum,
    in_sem,
    ra_send,
    ra_recv,
    rb_send,
    rb_recv,
    px_send,
    px_recv,
    pz_send,
    pz_recv,
    pd_send,
    pd_recv,
    nx_send,
    nx_recv,
    no_send,
    no_recv,
    nz_send,
    nz_recv,
    nd_send,
    nd_recv,
    y_send,
    y_recv,
    yd_send,
    yd_recv,
):
    n_rep, n_x, n_hi, n_lo = shape
    n_z = n_hi * n_lo
    half = n_z // 2
    heads, nope, lat = w_uk.shape
    rope = pre_rope.shape[1]
    width = keys.shape[-1]
    value = w_uv.shape[2]
    tok = hidden.shape[0]

    replica = lax.axis_index("replica")
    context = lax.axis_index("context")
    tensor = lax.axis_index("tensor")
    x = lax.div(context, n_hi)
    z_hi = lax.rem(context, n_hi)
    z_lo = lax.div(tensor, 2)
    core = lax.rem(tensor, 2)
    other = 1 - core
    z = z_hi * n_lo + z_lo
    sign = 1 - 2 * core

    def wrap(place):
        return lax.rem(place + 2 * n_z, n_z)

    def at_z(place):
        return {
            "context": x * n_hi + lax.div(place, n_lo),
            "tensor": lax.rem(place, n_lo) * 2 + core,
        }

    def at_x(place):
        return {"context": place * n_hi + z_hi}

    def x_plus(step):
        return lax.rem(x + step, n_x)

    def r_plus(step):
        return lax.rem(replica + step, n_rep)

    partner = {"tensor": z_lo * 2 + other}
    z_next = at_z(wrap(z + sign))
    z_behind = at_z(wrap(z - sign))

    peers = [z_next, z_behind, partner]
    peers += [at_x(x_plus(d)) for d in range(1, n_x)]
    peers += [{"tensor": lax.rem(z_lo + d, n_lo) * 2 + core} for d in range(1, n_lo)]
    peers += [{"replica": r_plus(d)} for d in range(1, n_rep)]
    barrier = pltpu.get_barrier_semaphore()
    for peer in peers:
        pl.semaphore_signal(barrier, inc=1, device_id=peer, device_id_type=MESH)

    own_pre = pl.multiple_of(z_lo * PIECE, PIECE)
    loads = [
        (hidden_hbm, hidden),
        (w_latent_hbm, w_latent),
        (w_krope_hbm, w_krope),
        (pre_lat_hbm.at[pl.ds(own_pre, PIECE)], pre_lat),
        (pre_rope_hbm.at[pl.ds(own_pre, PIECE)], pre_rope),
        (q_nope_hbm, q_nope),
        (q_rope_hbm, q_rope),
        (w_uk_hbm, w_uk),
        (w_uv_hbm, w_uv),
    ]
    loads = [
        pltpu.make_async_copy(source, target, in_sem.at[i])
        for i, (source, target) in enumerate(loads)
    ]
    for load in loads:
        load.start()

    def send(source, target, send_sem, recv_sem, device):
        return pltpu.make_async_remote_copy(
            src_ref=source,
            dst_ref=target,
            send_sem=send_sem,
            recv_sem=recv_sem,
            device_id=device,
            device_id_type=MESH,
        )

    def same(ref, send_sem, recv_sem, device):
        return send(ref, ref, send_sem, recv_sem, device)

    def ra_copy():
        return send(partial.at[other], partner_part, ra_send, ra_recv, partner)

    def rb_copy(d):
        to = lax.rem(z_lo + d, n_lo)
        return send(
            chip_sum.at[to],
            group_part.at[d - 1],
            rb_send.at[d - 1],
            rb_recv.at[d - 1],
            {"tensor": to * 2 + core},
        )

    def pz_copy(p):
        return same(
            keys.at[0, wrap(z - sign * (p - 1)), x], pz_send.at[p], pz_recv.at[p], z_next
        )

    def pz_arrival(p):
        return same(keys.at[0, wrap(z - sign * p), x], pz_send.at[p], pz_recv.at[p], z_next)

    def px_copy(p, d):
        return same(
            keys.at[0, wrap(z - sign * p), x],
            px_send.at[p, d - 1],
            px_recv.at[p, d - 1],
            at_x(x_plus(d)),
        )

    def px_arrival(p, d):
        return same(
            keys.at[0, wrap(z - sign * p), x_plus(n_x - d)],
            px_send.at[p, d - 1],
            px_recv.at[p, d - 1],
            partner,
        )

    def pd_copy(p):
        return same(keys.at[0, wrap(z - sign * p)], pd_send.at[p], pd_recv.at[p], partner)

    def pd_arrival(p):
        return same(keys.at[0, wrap(z + sign * p)], pd_send.at[p], pd_recv.at[p], partner)

    def prefix_step(p):
        def first():
            pz_arrival(p).wait_recv()
            when(p < half, lambda: pz_copy(p + 1).start())
            for d in range(1, n_x):
                px_copy(p, d).start()

        def second():
            for d in range(1, n_x):
                px_arrival(p - 1, d).wait_recv()
            when(both(p - 1 >= 1, p - 1 < half), lambda: pd_copy(p - 1).start())

        def third():
            pd_arrival(p - 2).wait_recv()

        when(p <= half, first)
        when(p - 1 <= half, second)
        when(both(p - 2 >= 1, p - 2 < half), third)

    own_kind = 1 + core

    def nx_copy(d):
        return same(
            keys.at[own_kind, z, x], nx_send.at[d - 1], nx_recv.at[d - 1], at_x(x_plus(d))
        )

    def nx_arrival(d):
        return same(
            keys.at[own_kind, z, x_plus(n_x - d)],
            nx_send.at[d - 1],
            nx_recv.at[d - 1],
            partner,
        )

    def no_copy():
        return same(keys.at[own_kind, z], no_send, no_recv, partner)

    def no_arrival():
        return same(keys.at[2 - core, z], no_send, no_recv, partner)

    def half_x(who):
        return pl.ds(who * (n_x // 2), n_x // 2)

    def nz_copy(kind, s):
        return same(
            keys.at[kind, wrap(z - sign * (s - 1))],
            nz_send.at[kind - 1, s],
            nz_recv.at[kind - 1, s],
            z_next,
        )

    def nz_arrival(kind, s):
        return same(
            keys.at[kind, wrap(z - sign * s)],
            nz_send.at[kind - 1, s],
            nz_recv.at[kind - 1, s],
            z_next,
        )

    def nz_last_copy(kind):
        return same(
            keys.at[kind, wrap(z - sign * (half - 1)), half_x(core)],
            nz_send.at[kind - 1, half],
            nz_recv.at[kind - 1, half],
            z_next,
        )

    def nz_last_arrival(kind):
        return same(
            keys.at[kind, wrap(z + half), half_x(core)],
            nz_send.at[kind - 1, half],
            nz_recv.at[kind - 1, half],
            z_next,
        )

    def nd_copy(kind, s):
        return same(
            keys.at[kind, wrap(z - sign * s)],
            nd_send.at[kind - 1, s],
            nd_recv.at[kind - 1, s],
            partner,
        )

    def nd_arrival(kind, s):
        return same(
            keys.at[kind, wrap(z + sign * s)],
            nd_send.at[kind - 1, s],
            nd_recv.at[kind - 1, s],
            partner,
        )

    def nd_last_copy(kind):
        return same(
            keys.at[kind, wrap(z + half), half_x(core)],
            nd_send.at[kind - 1, half],
            nd_recv.at[kind - 1, half],
            partner,
        )

    def nd_last_arrival(kind):
        return same(
            keys.at[kind, wrap(z + half), half_x(other)],
            nd_send.at[kind - 1, half],
            nd_recv.at[kind - 1, half],
            partner,
        )

    def new_step(s):
        def middle():
            for kind in (1, 2):
                nz_arrival(kind, s).wait_recv()
                when(s + 1 < half, lambda: nz_copy(kind, s + 1).start())
                when(s + 1 == half, lambda: nz_last_copy(kind).start())
                nd_copy(kind, s).start()

        def last():
            for kind in (1, 2):
                nz_last_arrival(kind).wait_recv()
                nd_last_copy(kind).start()

        when(s < half, middle)
        when(s == half, last)

    def y_copy(d):
        return send(
            keys.at[own_kind, pl.ds(z_hi * n_lo, n_lo), x],
            blocks.at[core, pl.ds(replica * n_lo, n_lo)],
            y_send.at[d - 1],
            y_recv.at[d - 1],
            {"replica": r_plus(d)},
        )

    def y_arrival(d):
        return send(
            keys.at[own_kind, pl.ds(z_hi * n_lo, n_lo), x],
            blocks.at[core, pl.ds(r_plus(n_rep - d) * n_lo, n_lo)],
            y_send.at[d - 1],
            y_recv.at[d - 1],
            partner,
        )

    def yd_copy():
        return same(blocks.at[core], yd_send, yd_recv, partner)

    def yd_arrival():
        return same(blocks.at[other], yd_send, yd_recv, partner)

    loads[0].wait()
    loads[1].wait()
    loads[2].wait()
    lat_term = jnp.dot(hidden[...], w_latent[...], preferred_element_type=jnp.float32)
    rope_term = lax.dot_general(
        hidden[...], w_krope[...], (((1,), (1,)), ((), ())), preferred_element_type=jnp.float32
    )
    rope_term = jnp.concatenate(
        [rope_term, jnp.zeros((tok, width - lat - rope), jnp.float32)], axis=1
    )
    for place in range(n_lo):
        for who in range(2):
            first = (place * 2 + who) * PIECE
            partial[who, place, :, :lat] = lat_term[first : first + PIECE]
            partial[who, place, :, lat:] = rope_term[first : first + PIECE]
    loads[3].wait()
    loads[4].wait()
    keys[0, z, x, :, :lat] = pre_lat[...]
    keys[0, z, x, :, lat:] = jnp.concatenate(
        [pre_rope[...], jnp.zeros((PIECE, width - lat - rope), pre_rope.dtype)], axis=1
    )

    pl.semaphore_wait(barrier, len(peers))
    ra_copy().start()
    pz_copy(1).start()
    for d in range(1, n_x):
        px_copy(0, d).start()

    loads[5].wait()
    loads[6].wait()
    loads[7].wait()
    lanes = lax.broadcasted_iota(jnp.int32, (tok, width - lat), 1)

    def absorb(first, last):
        for head in range(first, last):
            columns = pl.ds(head * tok, tok)
            absorbed = jnp.dot(
                q_nope[:, head * nope : (head + 1) * nope],
                w_uk[head],
                preferred_element_type=jnp.float32,
            )
            queries[:lat, columns] = absorbed.T.astype(jnp.bfloat16)
            pair = q_rope[:, (head // 2) * 2 * rope : (head // 2 + 1) * 2 * rope]
            pair = pair.astype(jnp.float32)
            if head % 2:
                pair = pltpu.roll(pair, rope, 1)
            queries[lat:, columns] = jnp.where(lanes < rope, pair, 0.0).T.astype(jnp.bfloat16)

    absorb(0, heads // 2)

    ra_copy().wait_recv()
    chip_sum[...] = partial[core] + partner_part[...]
    for d in range(1, n_lo):
        rb_copy(d).start()

    if half >= 1:
        prefix_step(1)
    absorb(heads // 2, heads)

    length = length_ref[0]
    position = (
        length
        + context * tok
        + tensor * PIECE
        + lax.broadcasted_iota(jnp.int32, (PIECE, width - lat), 0)
    )
    sine, cosine = sine_cosine(position.astype(jnp.float32) * frequency_ref[...])
    piece_lanes = lax.broadcasted_iota(jnp.int32, (PIECE, width - lat), 1)
    sine = jnp.where(piece_lanes < rope // 2, -sine, sine)
    sine = jnp.where(piece_lanes < rope, sine, 0.0)

    top[...] = jnp.full_like(top, FLOOR)
    weight_sum[...] = jnp.zeros_like(weight_sum)
    total[...] = jnp.zeros_like(total)

    for d in range(1, n_lo):
        rb_copy(d).wait_recv()
    summed = chip_sum[z_lo]
    for d in range(1, n_lo):
        summed = summed + group_part[d - 1]
    lat_sum = summed[:, :lat]
    mean_square = jnp.mean(lat_sum * lat_sum, axis=1, keepdims=True)
    keys[own_kind, z, x, :, :lat] = (
        lat_sum * lax.rsqrt(mean_square + NORM_EPS) * gain_ref[...]
    ).astype(jnp.bfloat16)
    rope_sum = summed[:, lat:]
    swapped = jnp.where(
        piece_lanes < rope // 2,
        pltpu.roll(rope_sum, width - lat - rope // 2, 1),
        pltpu.roll(rope_sum, rope // 2, 1),
    )
    keys[own_kind, z, x, :, lat:] = (rope_sum * cosine + swapped * sine).astype(jnp.bfloat16)

    for d in range(1, n_x):
        nx_copy(d).start()
    prefix_step(2)
    for d in range(1, n_x):
        nx_arrival(d).wait_recv()
    no_copy().start()

    def start_ring(kind):
        if half > 1:
            nz_copy(kind, 1).start()
        else:
            nz_last_copy(kind).start()

    pl.when(core == 0)(lambda: start_ring(1))
    pl.when(core == 1)(lambda: start_ring(2))
    prefix_step(3)
    no_arrival().wait_recv()
    pl.when(core == 1)(lambda: start_ring(1))
    pl.when(core == 0)(lambda: start_ring(2))

    score_scale = float((nope + rope) ** (-0.5) * math.log2(math.e))

    def attend(slots, spread, limit):
        block = n_x * PIECE
        count = len(slots) * block
        row = lax.broadcasted_iota(jnp.int32, (block, tok), 0)
        within = lax.div(row, PIECE) * spread + lax.rem(row, PIECE)
        bias = jnp.concatenate(
            [jnp.where(within <= limit - start, 0.0, MASKED) for _, _, start in slots], axis=0
        )
        key_rows = jnp.concatenate(
            [keys[kind, place].reshape(block, width) for kind, place, _ in slots], axis=0
        )
        latents = key_rows[:, :lat].T
        at_once = min(COLUMNS, heads * tok)
        bias = jnp.concatenate([bias] * (at_once // tok), axis=1)
        for first in range(0, heads * tok, at_once):
            columns = pl.ds(first, at_once)
            scores = jnp.dot(
                key_rows, queries[:, columns], preferred_element_type=jnp.float32
            )
            scores = scores * score_scale + bias
            old_top = top[:, columns]
            new_top = jnp.maximum(old_top, jnp.max(scores, axis=0, keepdims=True))
            top[:, columns] = new_top
            rescale = jnp.exp2(old_top - new_top)
            exponents = jnp.exp2(scores - new_top)
            weight_sum[:, columns] = weight_sum[:, columns] * rescale + jnp.sum(
                exponents, axis=0, keepdims=True
            )
            total[:, columns] = total[:, columns] * rescale + jnp.dot(
                latents, exponents.astype(jnp.bfloat16), preferred_element_type=jnp.float32
            )

    pre_dev = n_lo * PIECE

    def prefix_slot(place):
        return (0, place, lax.div(place, n_lo) * pre_dev + lax.rem(place, n_lo) * PIECE)

    def new_slot(kind, place, push=0):
        start = lax.div(place, n_lo) * tok + lax.rem(place, n_lo) * 2 * PIECE
        return (kind, place, start + (kind - 1) * PIECE + push)

    prefix_limit = length - 1
    new_limit = context * tok + lax.broadcasted_iota(jnp.int32, (n_x * PIECE, tok), 1)

    def iteration(s, carry):
        new_step(s)
        prefix_step(s + 3)

        def from_partner():
            for kind in (1, 2):
                nd_arrival(kind, s - 1).wait_recv()

        pl.when(s > 1)(from_partner)

        def to_owners():
            for place in range(n_lo):
                blocks[core, replica * n_lo + place] = keys[own_kind, z_hi * n_lo + place, x]
            for d in range(1, n_rep):
                y_copy(d).start()

        pl.when(s == n_lo)(to_owners)

        def owners_done():
            for d in range(1, n_rep):
                y_arrival(d).wait_recv()
            yd_copy().start()

        pl.when(s == half)(owners_done)

        def attend_prefix():
            last = jnp.where(s + 1 == half, z, wrap(z - (s + 1)))
            attend(
                [
                    prefix_slot(wrap(z - s)),
                    prefix_slot(wrap(z + s)),
                    prefix_slot(wrap(z + s + 1)),
                    prefix_slot(last),
                ],
                n_hi * pre_dev,
                prefix_limit,
            )

        pl.when(lax.rem(s, 2) == 1)(attend_prefix)
        push = jnp.where(s == 1, FAR, 0)
        before, after = wrap(z - (s - 1)), wrap(z + (s - 1))
        attend(
            [
                new_slot(1, before),
                new_slot(2, before),
                new_slot(1, after, push),
                new_slot(2, after, push),
            ],
            n_hi * tok,
            new_limit,
        )
        return carry

    lax.fori_loop(1, half + 1, iteration, 0)
    for kind in (1, 2):
        nd_last_arrival(kind).wait_recv()
    far = wrap(z + half)
    attend([new_slot(1, far), new_slot(2, far)], n_hi * tok, new_limit)

    loads[8].wait()
    for head in range(heads):
        columns = pl.ds(head * tok, tok)
        latent_out = (total[:, columns] / weight_sum[:, columns]).astype(jnp.bfloat16)
        out_ref[:, head * value : (head + 1) * value] = jnp.dot(
            latent_out.T, w_uv[head], preferred_element_type=jnp.float32
        ).astype(jnp.bfloat16)

    yd_arrival().wait_recv()
    tile = lat // TILES
    per_block = BLOCK // (2 * PIECE)
    stored, ropes, flat_scales = [], [], []
    scale_row = lax.broadcasted_iota(jnp.int32, (BLOCK, BLOCK * TILES), 0)
    scale_lane = lax.broadcasted_iota(jnp.int32, (BLOCK, BLOCK * TILES), 1)
    rope_lane = lax.broadcasted_iota(jnp.int32, (BLOCK, 2 * rope), 1)
    for slot in range(2):
        source = jnp.int32(0)
        for candidate in range(n_rep * 2):
            source = jnp.where(
                places_ref[0, candidate] == replica * 2 + slot, candidate, source
            )
        rows = jnp.concatenate(
            [
                blocks[who, source * per_block + place]
                for place in range(per_block)
                for who in range(2)
            ],
            axis=0,
        ).astype(jnp.float32)
        flat = jnp.zeros((BLOCK, BLOCK * TILES), jnp.float32)
        tiles = []
        for i in range(TILES):
            entries = rows[:, i * tile : (i + 1) * tile]
            scale = jnp.max(jnp.abs(entries), axis=1, keepdims=True) + SCALE_EPS
            scale = scale.astype(jnp.bfloat16).astype(jnp.float32)
            tiles.append(entries / scale)
            flat = jnp.where(scale_lane == scale_row * TILES + i, scale, flat)
        stored.append(jnp.concatenate(tiles, axis=1))
        flat_scales.append(jnp.sum(flat, axis=0, keepdims=True))
        tail = rows[:, lat : lat + 2 * rope]
        following = pltpu.roll(pltpu.roll(tail, BLOCK - 1, 0), rope, 1)
        ropes.append(jnp.where(rope_lane < rope, tail, following))
    for j in range(BLOCK):
        cache_lat_ref[:, j * lat : (j + 1) * lat] = jnp.concatenate(
            [stored[0][j : j + 1], stored[1][j : j + 1]], axis=0
        ).astype(jnp.bfloat16)
    for j in range(BLOCK // 2):
        cache_rope_ref[:, j * 2 * rope : (j + 1) * 2 * rope] = jnp.concatenate(
            [ropes[0][2 * j : 2 * j + 1], ropes[1][2 * j : 2 * j + 1]], axis=0
        ).astype(jnp.bfloat16)
    cache_scale_ref[...] = jnp.concatenate(flat_scales, axis=0).astype(jnp.bfloat16)

    ra_copy().wait_send()
    for d in range(1, n_lo):
        rb_copy(d).wait_send()
    for d in range(1, n_x):
        nx_copy(d).wait_send()
    for d in range(1, n_rep):
        y_copy(d).wait_send()
    no_copy().wait_send()
    yd_copy().wait_send()

    def sent(s, carry):
        pz_copy(s).wait_send()

        def middle():
            pd_copy(s).wait_send()
            for kind in (1, 2):
                nz_copy(kind, s).wait_send()
                nd_copy(kind, s).wait_send()

        def last():
            for kind in (1, 2):
                nz_last_copy(kind).wait_send()
                nd_last_copy(kind).wait_send()

        pl.when(s < half)(middle)
        pl.when(s == half)(last)
        return carry

    lax.fori_loop(1, half + 1, sent, 0)

    def pushed(p, carry):
        for d in range(1, n_x):
            px_copy(p, d).wait_send()
        return carry

    lax.fori_loop(0, half + 1, pushed, 0)


def per_device(
    shape,
    hidden,
    q_nope,
    q_rope,
    w_latent,
    w_krope,
    kv_gain,
    w_uk,
    w_uv,
    prefix_latent,
    prefix_rope,
    prefix_lengths,
    placements,
):
    n_rep, n_x, n_hi, n_lo = shape
    n_z = n_hi * n_lo
    half = n_z // 2
    tok, depth = hidden.shape[1:]
    heads, nope, lat = w_uk.shape
    rope = w_krope.shape[1]
    value = w_uv.shape[2]
    width = -(-(lat + rope) // 128) * 128
    count = rope // 2
    powers = -(np.arange(count, dtype=np.float32) * np.float32(2.0)) / np.float32(rope)
    frequency = np.power(np.float64(ROPE_THETA), powers.astype(np.float64))
    frequency = np.resize(frequency, (1, width - lat)).astype(np.float32)
    vmem = pl.BlockSpec(memory_space=pltpu.VMEM)
    smem = pl.BlockSpec(memory_space=pltpu.SMEM)
    anywhere = pl.BlockSpec(memory_space=pl.ANY)
    bf16, f32 = jnp.bfloat16, jnp.float32
    dma = pltpu.SemaphoreType.DMA
    out = pl.pallas_call(
        functools.partial(kernel, shape),
        out_shape=(
            jax.ShapeDtypeStruct((tok, heads * value), bf16),
            jax.ShapeDtypeStruct((2, BLOCK * lat), bf16),
            jax.ShapeDtypeStruct((2, BLOCK * rope), bf16),
            jax.ShapeDtypeStruct((2, BLOCK * TILES), bf16),
        ),
        in_specs=[smem, smem, vmem, vmem] + [anywhere] * 9,
        out_specs=(vmem, vmem, vmem, vmem),
        scratch_shapes=[
            pltpu.VMEM((tok, depth), bf16),
            pltpu.VMEM((tok, heads * nope), bf16),
            pltpu.VMEM((tok, heads * rope), bf16),
            pltpu.VMEM((depth, lat), bf16),
            pltpu.VMEM((rope, depth), bf16),
            pltpu.VMEM((heads, nope, lat), bf16),
            pltpu.VMEM((heads, lat, value), bf16),
            pltpu.VMEM((PIECE, lat), bf16),
            pltpu.VMEM((PIECE, rope), bf16),
            pltpu.VMEM((2, n_lo, PIECE, width), f32),
            pltpu.VMEM((n_lo, PIECE, width), f32),
            pltpu.VMEM((n_lo, PIECE, width), f32),
            pltpu.VMEM((max(n_lo - 1, 1), PIECE, width), f32),
            pltpu.VMEM((3, n_z, n_x, PIECE, width), bf16),
            pltpu.VMEM((2, n_rep * n_lo, PIECE, width), bf16),
            pltpu.VMEM((width, heads * tok), bf16),
            pltpu.VMEM((lat, heads * tok), f32),
            pltpu.VMEM((1, heads * tok), f32),
            pltpu.VMEM((1, heads * tok), f32),
            dma((9,)),
            dma,
            dma,
            dma((max(n_lo - 1, 1),)),
            dma((max(n_lo - 1, 1),)),
            dma((half + 1, max(n_x - 1, 1))),
            dma((half + 1, max(n_x - 1, 1))),
            dma((half + 1,)),
            dma((half + 1,)),
            dma((half + 1,)),
            dma((half + 1,)),
            dma((max(n_x - 1, 1),)),
            dma((max(n_x - 1, 1),)),
            dma,
            dma,
            dma((2, half + 1)),
            dma((2, half + 1)),
            dma((2, half + 1)),
            dma((2, half + 1)),
            dma((max(n_rep - 1, 1),)),
            dma((max(n_rep - 1, 1),)),
            dma,
            dma,
        ],
        compiler_params=pltpu.CompilerParams(
            collective_id=0, has_side_effects=True, vmem_limit_bytes=56 * 1024 * 1024
        ),
    )(
        prefix_lengths,
        placements,
        jnp.asarray(frequency),
        kv_gain.reshape(1, lat),
        hidden[0],
        q_nope[0],
        q_rope[0],
        w_latent,
        w_krope.T,
        w_uk,
        w_uv,
        prefix_latent[0],
        prefix_rope[0],
    )
    return tuple(result[None] for result in out)


def program(mesh, shape):
    return jax.shard_map(
        functools.partial(per_device, shape),
        mesh=mesh,
        in_specs=(
            P("replica", "context", "tensor"),
            P("replica", "context", "tensor"),
            P("replica", "context", "tensor"),
            P("tensor", None),
            P("tensor", None),
            P(),
            P("tensor", None, None),
            P("tensor", None, None),
            P("replica", "context", None),
            P("replica", "context", None),
            P("replica"),
            P("context", None),
        ),
        out_specs=(
            P("replica", "context", "tensor"),
            P("replica", "context", None),
            P("replica", "context", None),
            P("replica", "context", None),
        ),
        check_vma=False,
    )


def solution(mesh):
    n_hi = 4
    return program(
        mesh,
        (
            mesh.shape["replica"],
            mesh.shape["context"] // n_hi,
            n_hi,
            mesh.shape["tensor"] // 2,
        ),
    )
```

```python
import functools
import math

import jax
import jax.numpy as jnp
import numpy as np
from jax import lax
from jax.experimental import pallas as pl
from jax.experimental.pallas import tpu as pltpu
from jax.sharding import PartitionSpec as P

MESH = pl.DeviceIdType.MESH
BLOCK = 64
TILES = 4
PIECE = 16
ROWS = 256
ROPE_THETA = 50000.0
NORM_EPS = 1e-06
SCALE_EPS = 1e-06
MASKED = -1e30
FLOOR = -1e28


def sine_cosine(angle):
    turns = jnp.floor(angle * np.float32(1.0 / (2.0 * math.pi)) + 0.5)
    high = 6.28125
    middle = float(np.float32(0.0019350051879882812))
    low = 2.0 * math.pi - high - middle
    r = angle - turns * np.float32(high)
    r = r - turns * np.float32(middle)
    r = r - turns * np.float32(low)
    square = r * r
    sine = jnp.full_like(r, 1.0 / math.factorial(17))
    for n in (15, 13, 11, 9, 7, 5, 3, 1):
        sign = -1.0 if (n // 2) % 2 else 1.0
        sine = sine * square + sign / math.factorial(n)
    cosine = jnp.full_like(r, 1.0 / math.factorial(16))
    for n in (14, 12, 10, 8, 6, 4, 2, 0):
        sign = -1.0 if (n // 2) % 2 else 1.0
        cosine = cosine * square + sign / math.factorial(n)
    return sine * r, cosine


def kernel(
    shape,
    length_ref,
    places_ref,
    frequency_ref,
    gain_ref,
    hidden_hbm,
    q_nope_hbm,
    q_rope_hbm,
    w_latent_hbm,
    w_krope_hbm,
    w_uk_hbm,
    w_uv_hbm,
    pre_lat_hbm,
    pre_rope_hbm,
    out_ref,
    cache_lat_ref,
    cache_rope_ref,
    cache_scale_ref,
    hidden,
    q_nope,
    q_rope,
    w_latent,
    w_krope,
    w_uk,
    w_uv,
    pre_lat,
    pre_rope,
    partial,
    partner_part,
    chip_sum,
    group_part,
    keys,
    marks,
    blocks,
    queries,
    total,
    top,
    weight_sum,
    in_sem,
    ra_send,
    ra_recv,
    rb_send,
    rb_recv,
    z1_send,
    z1_recv,
    z2_send,
    z2_recv,
    x_send,
    x_recv,
    xf_send,
    xf_recv,
    d_send,
    d_recv,
    y_send,
    y_recv,
    yd_send,
    yd_recv,
):
    n_rep, n_x, n_hi, n_lo = shape
    n_z = n_hi * n_lo
    heads, nope, lat = w_uk.shape
    rope = pre_rope.shape[1]
    width = keys.shape[-1]
    value = w_uv.shape[2]
    tok = hidden.shape[0]

    replica = lax.axis_index("replica")
    context = lax.axis_index("context")
    tensor = lax.axis_index("tensor")
    x = lax.div(context, n_hi)
    z_hi = lax.rem(context, n_hi)
    z_lo = lax.div(tensor, 2)
    core = lax.rem(tensor, 2)
    other = 1 - core
    z = z_hi * n_lo + z_lo
    own_kind = 1 + core

    def z_plus(step):
        place = lax.rem(z + step + n_z, n_z)
        return {
            "context": x * n_hi + lax.div(place, n_lo),
            "tensor": lax.rem(place, n_lo) * 2 + core,
        }

    def x_place(step):
        return lax.rem(x + step + n_x, n_x)

    def x_plus(step):
        return {"context": x_place(step) * n_hi + z_hi}

    def hi_place(step):
        return lax.rem(z_hi + step, n_hi)

    def r_plus(step):
        return lax.rem(replica + step, n_rep)

    def group(step):
        return lax.rem(z_lo + step + n_lo, n_lo)

    partner = {"tensor": z_lo * 2 + other}
    two = 2 - 4 * lax.rem(z_lo, 2)

    peers = [partner, z_plus(1), z_plus(-1), z_plus(2), z_plus(-2), x_plus(1), x_plus(-1)]
    peers += [{"context": x * n_hi + hi_place(d)} for d in range(1, n_hi)]
    peers += [{"tensor": group(d) * 2 + core} for d in range(1, n_lo)]
    peers += [{"replica": r_plus(d)} for d in range(1, n_rep)]
    barrier = pltpu.get_barrier_semaphore()
    for peer in peers:
        pl.semaphore_signal(barrier, inc=1, device_id=peer, device_id_type=MESH)

    own_pre = pl.multiple_of(z_lo * PIECE, PIECE)
    loads = [
        (hidden_hbm, hidden),
        (w_latent_hbm, w_latent),
        (w_krope_hbm, w_krope),
        (pre_lat_hbm.at[pl.ds(own_pre, PIECE)], pre_lat),
        (pre_rope_hbm.at[pl.ds(own_pre, PIECE)], pre_rope),
        (q_nope_hbm, q_nope),
        (q_rope_hbm, q_rope),
        (w_uk_hbm, w_uk),
        (w_uv_hbm, w_uv),
    ]
    loads = [
        pltpu.make_async_copy(source, target, in_sem.at[i])
        for i, (source, target) in enumerate(loads)
    ]
    for load in loads:
        load.start()

    def send(source, target, send_sem, recv_sem, device):
        return pltpu.make_async_remote_copy(
            src_ref=source,
            dst_ref=target,
            send_sem=send_sem,
            recv_sem=recv_sem,
            device_id=device,
            device_id_type=MESH,
        )

    def same(ref, send_sem, recv_sem, device):
        return send(ref, ref, send_sem, recv_sem, device)

    def ra_copy():
        return send(partial.at[other], partner_part, ra_send, ra_recv, partner)

    def rb_copy(d):
        to = lax.rem(z_lo + d, n_lo)
        return send(
            chip_sum.at[to],
            group_part.at[d - 1],
            rb_send.at[d - 1],
            rb_recv.at[d - 1],
            {"tensor": to * 2 + core},
        )

    def kind_of(flow):
        return own_kind if flow else 0

    def z1_copy(flow, d):
        return same(
            keys.at[kind_of(flow), z_lo, z_hi, x],
            z1_send.at[flow, d - 1],
            z1_recv.at[flow, d - 1],
            {"context": x * n_hi + hi_place(d)},
        )

    def z1_arrival(flow, d):
        return same(
            keys.at[kind_of(flow), z_lo, hi_place(n_hi - d), x],
            z1_send.at[flow, d - 1],
            z1_recv.at[flow, d - 1],
            partner,
        )

    z2_steps = (1, -1, two)

    def z2_copy(flow, i):
        return same(
            keys.at[kind_of(flow), z_lo, :, x],
            z2_send.at[flow, i],
            z2_recv.at[flow, i],
            z_plus(z2_steps[i]),
        )

    def z2_arrival(flow, i):
        return same(
            keys.at[kind_of(flow), group(-z2_steps[i]), :, x],
            z2_send.at[flow, i],
            z2_recv.at[flow, i],
            partner,
        )

    def x_copy(flow, g, i):
        return same(
            keys.at[kind_of(flow), g, :, x],
            x_send.at[flow, g, i],
            x_recv.at[flow, g, i],
            x_plus(1 - 2 * i),
        )

    def x_arrival(flow, g, i):
        return same(
            keys.at[kind_of(flow), g, :, x_place(2 * i - 1)],
            x_send.at[flow, g, i],
            x_recv.at[flow, g, i],
            partner,
        )

    def xf_copy(flow, g):
        way = 1 - 2 * lax.rem(g, 2)
        return same(
            keys.at[kind_of(flow), g, :, x_place(-way)],
            xf_send.at[flow, g],
            xf_recv.at[flow, g],
            x_plus(way),
        )

    def xf_arrival(flow, g):
        return same(
            keys.at[kind_of(flow), g, :, x_place(2)],
            xf_send.at[flow, g],
            xf_recv.at[flow, g],
            partner,
        )

    def d_copy(flow, g):
        return same(
            keys.at[kind_of(flow), g], d_send.at[flow, g], d_recv.at[flow, g], partner
        )

    def d_arrival(flow, g):
        kind = 2 - core if flow else 0
        return same(keys.at[kind, g], d_send.at[flow, g], d_recv.at[flow, g], partner)

    def push_x(flow, g):
        for i in range(2):
            x_copy(flow, g, i).start()

    def forward_x(flow, g):
        for i in range(2):
            x_arrival(flow, g, i).wait_recv()
        xf_copy(flow, g).start()

    def to_partner(flow, g):
        xf_arrival(flow, g).wait_recv()
        d_copy(flow, g).start()

    match = lax.rem(z_lo, 2) == core
    first_group = jnp.where(match, z_lo, group(-1))

    def mine(i):
        return lax.rem(first_group + 2 * i, n_lo)

    def y_copy(d):
        return send(
            keys.at[own_kind, :, z_hi, x],
            blocks.at[core, pl.ds(replica * n_lo, n_lo)],
            y_send.at[d - 1],
            y_recv.at[d - 1],
            {"replica": r_plus(d)},
        )

    def y_arrival(d):
        return send(
            keys.at[own_kind, :, z_hi, x],
            blocks.at[core, pl.ds(r_plus(n_rep - d) * n_lo, n_lo)],
            y_send.at[d - 1],
            y_recv.at[d - 1],
            partner,
        )

    def yd_copy():
        return same(blocks.at[core], yd_send, yd_recv, partner)

    def yd_arrival():
        return same(blocks.at[other], yd_send, yd_recv, partner)

    loads[0].wait()
    loads[1].wait()
    loads[2].wait()
    lat_term = jnp.dot(hidden[...], w_latent[...], preferred_element_type=jnp.float32)
    rope_term = lax.dot_general(
        hidden[...], w_krope[...], (((1,), (1,)), ((), ())), preferred_element_type=jnp.float32
    )
    rope_term = jnp.concatenate(
        [rope_term, jnp.zeros((tok, width - lat - rope), jnp.float32)], axis=1
    )
    for place in range(n_lo):
        for who in range(2):
            first = (place * 2 + who) * PIECE
            partial[who, place, :, :lat] = lat_term[first : first + PIECE]
            partial[who, place, :, lat:] = rope_term[first : first + PIECE]
    loads[3].wait()
    loads[4].wait()
    keys[0, z_lo, z_hi, x, :, :lat] = pre_lat[...]
    length = length_ref[0]
    n_context = n_x * n_hi
    piece_row = lax.broadcasted_iota(jnp.int32, (PIECE, width - lat), 0)
    piece_lanes = lax.broadcasted_iota(jnp.int32, (PIECE, width - lat), 1)
    pre_place = context * (n_lo * PIECE) + z_lo * PIECE + piece_row
    hidden_key = jnp.logical_and(piece_lanes == rope + n_context, pre_place >= length)
    pre_tail = jnp.concatenate(
        [
            pre_rope[...].astype(jnp.float32),
            jnp.zeros((PIECE, width - lat - rope), jnp.float32),
        ],
        axis=1,
    )
    keys[0, z_lo, z_hi, x, :, lat:] = jnp.where(hidden_key, MASKED, pre_tail).astype(
        jnp.bfloat16
    )

    pl.semaphore_wait(barrier, len(peers))
    ra_copy().start()

    def prefix_z1():
        for d in range(1, n_hi):
            z1_copy(0, d).start()

    pl.when(match)(prefix_z1)

    loads[5].wait()
    loads[6].wait()
    loads[7].wait()
    lanes = lax.broadcasted_iota(jnp.int32, (tok, width - lat), 1)
    later = jnp.logical_and(lanes > rope + context, lanes < rope + n_context)
    masks = jnp.where(later, MASKED, jnp.where(lanes == rope + n_context, 1.0, 0.0))
    query_row = lax.broadcasted_iota(jnp.int32, (tok, tok), 0)
    key_lane = lax.broadcasted_iota(jnp.int32, (tok, tok), 1)
    triangle = jnp.where(key_lane > query_row, MASKED, 0.0).astype(jnp.bfloat16)
    marks[...] = jnp.zeros_like(marks)
    mark_row = lax.broadcasted_iota(jnp.int32, (PIECE, tok), 0)
    mark_lane = lax.broadcasted_iota(jnp.int32, (PIECE, tok), 1)
    for place in range(n_lo):
        for who in range(2):
            first = (place * 2 + who) * PIECE
            marks[1 + who, place, z_hi, x] = jnp.where(
                mark_lane == first + mark_row, 1.0, 0.0
            ).astype(jnp.bfloat16)

    def absorb(first, last):
        for head in range(first, last):
            rows = pl.ds(head * tok, tok)
            queries[rows, :lat] = jnp.dot(
                q_nope[:, head * nope : (head + 1) * nope],
                w_uk[head],
                preferred_element_type=jnp.float32,
            ).astype(jnp.bfloat16)
            pair = q_rope[:, (head // 2) * 2 * rope : (head // 2 + 1) * 2 * rope]
            pair = pair.astype(jnp.float32)
            if head % 2:
                pair = pltpu.roll(pair, rope, 1)
            queries[rows, lat:width] = jnp.where(lanes < rope, pair, masks).astype(jnp.bfloat16)
            queries[rows, width:] = triangle

    absorb(0, heads // 2)

    ra_copy().wait_recv()
    chip_sum[...] = partial[core] + partner_part[...]
    for d in range(1, n_lo):
        rb_copy(d).start()

    def prefix_z2():
        for d in range(1, n_hi):
            z1_arrival(0, d).wait_recv()
        for i in range(3):
            z2_copy(0, i).start()
        push_x(0, z_lo)

    pl.when(match)(prefix_z2)
    absorb(heads // 2, heads)

    position = (
        length
        + context * tok
        + tensor * PIECE
        + piece_row
    )
    sine, cosine = sine_cosine(position.astype(jnp.float32) * frequency_ref[...])
    sine = jnp.where(piece_lanes < rope // 2, -sine, sine)
    sine = jnp.where(piece_lanes < rope, sine, 0.0)

    top[...] = jnp.full_like(top, FLOOR)
    weight_sum[...] = jnp.zeros_like(weight_sum)
    total[...] = jnp.zeros_like(total)

    def prefix_far():
        z2_arrival(0, 2).wait_recv()
        push_x(0, group(2))

    def prefix_near():
        for i in (0, 1):
            z2_arrival(0, i).wait_recv()
            push_x(0, group(-z2_steps[i]))

    pl.when(match)(prefix_far)
    pl.when(jnp.logical_not(match))(prefix_near)

    for d in range(1, n_lo):
        rb_copy(d).wait_recv()
    summed = chip_sum[z_lo]
    for d in range(1, n_lo):
        summed = summed + group_part[d - 1]
    lat_sum = summed[:, :lat]
    mean_square = jnp.mean(lat_sum * lat_sum, axis=1, keepdims=True)
    keys[own_kind, z_lo, z_hi, x, :, :lat] = (
        lat_sum * lax.rsqrt(mean_square + NORM_EPS) * gain_ref[...]
    ).astype(jnp.bfloat16)
    rope_sum = summed[:, lat:]
    swapped = jnp.where(
        piece_lanes < rope // 2,
        pltpu.roll(rope_sum, width - lat - rope // 2, 1),
        pltpu.roll(rope_sum, rope // 2, 1),
    )
    new_tail = rope_sum * cosine + swapped * sine
    keys[own_kind, z_lo, z_hi, x, :, lat:] = jnp.where(
        piece_lanes == rope + context, 1.0, new_tail
    ).astype(jnp.bfloat16)

    for d in range(1, n_hi):
        z1_copy(1, d).start()
    for i in range(2):
        forward_x(0, mine(i))
    for d in range(1, n_hi):
        z1_arrival(1, d).wait_recv()
    for i in range(3):
        z2_copy(1, i).start()
    push_x(1, z_lo)
    for i in range(2):
        to_partner(0, mine(i))

    score_scale = float((nope + rope) ** (-0.5) * math.log2(math.e))

    key_count = n_hi * n_x * PIECE

    def attend(places, first):
        key_rows = jnp.concatenate(
            [
                jnp.concatenate(
                    [
                        keys[kind, g].reshape(key_count, width),
                        marks[kind, g].reshape(key_count, tok),
                    ],
                    axis=1,
                )
                for kind, g in places
            ],
            axis=0,
        )
        tiles = len(places) * key_count // 128
        at_once = min(ROWS, heads * tok // 2)
        for part in range(heads * tok // 2 // at_once):
            rows = pl.ds(pl.multiple_of(first + part * at_once, at_once), at_once)
            scores = lax.dot_general(
                queries[rows, :],
                key_rows,
                (((1,), (1,)), ((), ())),
                preferred_element_type=jnp.float32,
            )
            scores = scores * score_scale
            old_top = top[rows, :]
            new_top = jnp.maximum(old_top, jnp.max(scores, axis=1, keepdims=True))
            top[rows, :] = new_top
            rescale = jnp.exp2(old_top - new_top)
            exponents = [
                jnp.exp2(scores[:, i * 128 : (i + 1) * 128] - new_top) for i in range(tiles)
            ]
            weight_sum[rows, :] = weight_sum[rows, :] * rescale + sum(exponents)
            weights = jnp.concatenate([e.astype(jnp.bfloat16) for e in exponents], axis=1)
            total[rows, :] = total[rows, :] * jnp.concatenate(
                [rescale] * (lat // 128), axis=1
            ) + jnp.dot(weights, key_rows[:, :lat], preferred_element_type=jnp.float32)


    def new_group(i):
        step = jnp.where(i == 1, n_lo - 1, jnp.where(i == 2, 1, jnp.where(i == 3, 2, 0)))
        return lax.rem(z_lo + step, n_lo)

    def second_level():
        for i in range(3):
            z2_arrival(1, i).wait_recv()
            push_x(1, group(-z2_steps[i]))
        for d in range(1, n_rep):
            y_copy(d).start()
        for place in range(n_lo):
            blocks[core, replica * n_lo + place] = keys[own_kind, place, z_hi, x]

    def owners():
        for d in range(1, n_rep):
            y_arrival(d).wait_recv()
        yd_copy().start()

    def step_1():
        forward_x(1, group(0))

    def step_2():
        for i in (1, 3):
            d_arrival(0, lax.rem(first_group + i, n_lo)).wait_recv()
        second_level()

    def step_3():
        to_partner(1, group(0))

    def step_4():
        forward_x(1, group(-1))
        d_arrival(1, group(0)).wait_recv()

    def step_5():
        forward_x(1, group(1))
        to_partner(1, group(-1))

    def step_6():
        forward_x(1, group(2))
        to_partner(1, group(1))
        d_arrival(1, group(-1)).wait_recv()

    def step_7():
        to_partner(1, group(2))
        owners()

    def step_8():
        d_arrival(1, group(1)).wait_recv()

    def step_10():
        d_arrival(1, group(2)).wait_recv()

    actions = {
        1: step_1,
        2: step_2,
        3: step_3,
        4: step_4,
        5: step_5,
        6: step_6,
        7: step_7,
        8: step_8,
        10: step_10,
    }

    def iteration(step, carry):
        for number, action in actions.items():
            pl.when(step == number)(action)
        chunk = lax.div(step, 2)
        is_new = chunk >= 2
        g = new_group(jnp.maximum(chunk - 2, 0))
        pre = lax.rem(first_group + chunk, n_lo)
        attend(
            [
                (jnp.where(is_new, 1, 0), jnp.where(is_new, g, pre)),
                (jnp.where(is_new, 2, 0), jnp.where(is_new, g, lax.rem(pre + 2, n_lo))),
            ],
            lax.rem(step, 2) * (heads * tok // 2),
        )
        return carry

    lax.fori_loop(0, 2 * (2 + n_lo), iteration, 0)

    loads[8].wait()
    for head in range(heads):
        rows = pl.ds(head * tok, tok)
        row_sum = jnp.sum(weight_sum[rows, :], axis=1, keepdims=True)
        latent_out = (total[rows, :] / row_sum).astype(jnp.bfloat16)
        out_ref[:, head * value : (head + 1) * value] = jnp.dot(
            latent_out, w_uv[head], preferred_element_type=jnp.float32
        ).astype(jnp.bfloat16)

    yd_arrival().wait_recv()
    tile = lat // TILES
    per_block = BLOCK // (2 * PIECE)
    stored, ropes, flat_scales = [], [], []
    scale_row = lax.broadcasted_iota(jnp.int32, (BLOCK, BLOCK * TILES), 0)
    scale_lane = lax.broadcasted_iota(jnp.int32, (BLOCK, BLOCK * TILES), 1)
    rope_lane = lax.broadcasted_iota(jnp.int32, (BLOCK, 2 * rope), 1)
    for slot in range(2):
        source = jnp.int32(0)
        for candidate in range(n_rep * 2):
            source = jnp.where(
                places_ref[0, candidate] == replica * 2 + slot, candidate, source
            )
        rows = jnp.concatenate(
            [
                blocks[who, source * per_block + place]
                for place in range(per_block)
                for who in range(2)
            ],
            axis=0,
        ).astype(jnp.float32)
        flat = jnp.zeros((BLOCK, BLOCK * TILES), jnp.float32)
        tiles = []
        for i in range(TILES):
            entries = rows[:, i * tile : (i + 1) * tile]
            scale = jnp.max(jnp.abs(entries), axis=1, keepdims=True) + SCALE_EPS
            scale = scale.astype(jnp.bfloat16).astype(jnp.float32)
            tiles.append(entries / scale)
            flat = jnp.where(scale_lane == scale_row * TILES + i, scale, flat)
        stored.append(jnp.concatenate(tiles, axis=1))
        flat_scales.append(jnp.sum(flat, axis=0, keepdims=True))
        tail = rows[:, lat : lat + 2 * rope]
        following = pltpu.roll(pltpu.roll(tail, BLOCK - 1, 0), rope, 1)
        ropes.append(jnp.where(rope_lane < rope, tail, following))
    for j in range(BLOCK):
        cache_lat_ref[:, j * lat : (j + 1) * lat] = jnp.concatenate(
            [stored[0][j : j + 1], stored[1][j : j + 1]], axis=0
        ).astype(jnp.bfloat16)
    for j in range(BLOCK // 2):
        cache_rope_ref[:, j * 2 * rope : (j + 1) * 2 * rope] = jnp.concatenate(
            [ropes[0][2 * j : 2 * j + 1], ropes[1][2 * j : 2 * j + 1]], axis=0
        ).astype(jnp.bfloat16)
    cache_scale_ref[...] = jnp.concatenate(flat_scales, axis=0).astype(jnp.bfloat16)

    ra_copy().wait_send()
    for d in range(1, n_lo):
        rb_copy(d).wait_send()
    for d in range(1, n_rep):
        y_copy(d).wait_send()
    yd_copy().wait_send()

    def z_sent(flow):
        for d in range(1, n_hi):
            z1_copy(flow, d).wait_send()
        for i in range(3):
            z2_copy(flow, i).wait_send()

    def x_sent(flow, g):
        for i in range(2):
            x_copy(flow, g, i).wait_send()
        xf_copy(flow, g).wait_send()
        d_copy(flow, g).wait_send()

    pl.when(match)(lambda: z_sent(0))
    z_sent(1)
    for i in range(2):
        x_sent(0, mine(i))
    for g in range(n_lo):
        x_sent(1, g)


def per_device(
    shape,
    hidden,
    q_nope,
    q_rope,
    w_latent,
    w_krope,
    kv_gain,
    w_uk,
    w_uv,
    prefix_latent,
    prefix_rope,
    prefix_lengths,
    placements,
):
    n_rep, n_x, n_hi, n_lo = shape
    tok, depth = hidden.shape[1:]
    heads, nope, lat = w_uk.shape
    rope = w_krope.shape[1]
    value = w_uv.shape[2]
    width = -(-(lat + rope) // 128) * 128
    count = rope // 2
    powers = -(np.arange(count, dtype=np.float32) * np.float32(2.0)) / np.float32(rope)
    frequency = np.power(np.float64(ROPE_THETA), powers.astype(np.float64))
    frequency = np.resize(frequency, (1, width - lat)).astype(np.float32)
    vmem = pl.BlockSpec(memory_space=pltpu.VMEM)
    smem = pl.BlockSpec(memory_space=pltpu.SMEM)
    anywhere = pl.BlockSpec(memory_space=pl.ANY)
    bf16, f32 = jnp.bfloat16, jnp.float32
    dma = pltpu.SemaphoreType.DMA
    out = pl.pallas_call(
        functools.partial(kernel, shape),
        out_shape=(
            jax.ShapeDtypeStruct((tok, heads * value), bf16),
            jax.ShapeDtypeStruct((2, BLOCK * lat), bf16),
            jax.ShapeDtypeStruct((2, BLOCK * rope), bf16),
            jax.ShapeDtypeStruct((2, BLOCK * TILES), bf16),
        ),
        in_specs=[smem, smem, vmem, vmem] + [anywhere] * 9,
        out_specs=(vmem, vmem, vmem, vmem),
        scratch_shapes=[
            pltpu.VMEM((tok, depth), bf16),
            pltpu.VMEM((tok, heads * nope), bf16),
            pltpu.VMEM((tok, heads * rope), bf16),
            pltpu.VMEM((depth, lat), bf16),
            pltpu.VMEM((rope, depth), bf16),
            pltpu.VMEM((heads, nope, lat), bf16),
            pltpu.VMEM((heads, lat, value), bf16),
            pltpu.VMEM((PIECE, lat), bf16),
            pltpu.VMEM((PIECE, rope), bf16),
            pltpu.VMEM((2, n_lo, PIECE, width), f32),
            pltpu.VMEM((n_lo, PIECE, width), f32),
            pltpu.VMEM((n_lo, PIECE, width), f32),
            pltpu.VMEM((max(n_lo - 1, 1), PIECE, width), f32),
            pltpu.VMEM((3, n_lo, n_hi, n_x, PIECE, width), bf16),
            pltpu.VMEM((3, n_lo, n_hi, n_x, PIECE, tok), bf16),
            pltpu.VMEM((2, n_rep * n_lo, PIECE, width), bf16),
            pltpu.VMEM((heads * tok, width + tok), bf16),
            pltpu.VMEM((heads * tok, lat), f32),
            pltpu.VMEM((heads * tok, 128), f32),
            pltpu.VMEM((heads * tok, 128), f32),
            dma((9,)),
            dma,
            dma,
            dma((max(n_lo - 1, 1),)),
            dma((max(n_lo - 1, 1),)),
            dma((2, n_hi - 1)),
            dma((2, n_hi - 1)),
            dma((2, 3)),
            dma((2, 3)),
            dma((2, n_lo, 2)),
            dma((2, n_lo, 2)),
            dma((2, n_lo)),
            dma((2, n_lo)),
            dma((2, n_lo)),
            dma((2, n_lo)),
            dma((max(n_rep - 1, 1),)),
            dma((max(n_rep - 1, 1),)),
            dma,
            dma,
        ],
        compiler_params=pltpu.CompilerParams(
            collective_id=0, has_side_effects=True, vmem_limit_bytes=56 * 1024 * 1024
        ),
    )(
        prefix_lengths,
        placements,
        jnp.asarray(frequency),
        kv_gain.reshape(1, lat),
        hidden[0],
        q_nope[0],
        q_rope[0],
        w_latent,
        w_krope.T,
        w_uk,
        w_uv,
        prefix_latent[0],
        prefix_rope[0],
    )
    return tuple(result[None] for result in out)


def program(mesh, shape):
    return jax.shard_map(
        functools.partial(per_device, shape),
        mesh=mesh,
        in_specs=(
            P("replica", "context", "tensor"),
            P("replica", "context", "tensor"),
            P("replica", "context", "tensor"),
            P("tensor", None),
            P("tensor", None),
            P(),
            P("tensor", None, None),
            P("tensor", None, None),
            P("replica", "context", None),
            P("replica", "context", None),
            P("replica"),
            P("context", None),
        ),
        out_specs=(
            P("replica", "context", "tensor"),
            P("replica", "context", None),
            P("replica", "context", None),
            P("replica", "context", None),
        ),
        check_vma=False,
    )


def solution(mesh):
    n_hi = 4
    return program(
        mesh,
        (
            mesh.shape["replica"],
            mesh.shape["context"] // n_hi,
            n_hi,
            mesh.shape["tensor"] // 2,
        ),
    )
```

```python
import functools
import math

import jax
import jax.numpy as jnp
import numpy as np
from jax import lax
from jax.experimental import pallas as pl
from jax.experimental.pallas import tpu as pltpu
from jax.sharding import PartitionSpec as P

MESH = pl.DeviceIdType.MESH
BLOCK = 64
TILES = 4
PIECE = 16
ROWS = 256
ROPE_THETA = 50000.0
NORM_EPS = 1e-06
SCALE_EPS = 1e-06
MASKED = -1e30
FLOOR = -1e28


def sine_cosine(angle):
    turns = jnp.floor(angle * np.float32(1.0 / (2.0 * math.pi)) + 0.5)
    high = 6.28125
    middle = float(np.float32(0.0019350051879882812))
    low = 2.0 * math.pi - high - middle
    r = angle - turns * np.float32(high)
    r = r - turns * np.float32(middle)
    r = r - turns * np.float32(low)
    square = r * r
    sine = jnp.full_like(r, 1.0 / math.factorial(17))
    for n in (15, 13, 11, 9, 7, 5, 3, 1):
        sign = -1.0 if (n // 2) % 2 else 1.0
        sine = sine * square + sign / math.factorial(n)
    cosine = jnp.full_like(r, 1.0 / math.factorial(16))
    for n in (14, 12, 10, 8, 6, 4, 2, 0):
        sign = -1.0 if (n // 2) % 2 else 1.0
        cosine = cosine * square + sign / math.factorial(n)
    return sine * r, cosine


def kernel(
    shape,
    length_ref,
    places_ref,
    frequency_ref,
    gain_ref,
    hidden_hbm,
    q_nope_hbm,
    q_rope_hbm,
    w_latent_hbm,
    w_krope_hbm,
    w_uk_hbm,
    w_uv_hbm,
    pre_lat_hbm,
    pre_rope_hbm,
    out_ref,
    cache_lat_ref,
    cache_rope_ref,
    cache_scale_ref,
    hidden,
    q_nope,
    q_rope,
    w_latent,
    w_krope,
    w_uk,
    w_uv,
    pre_lat,
    pre_rope,
    partial,
    partner_part,
    chip_sum,
    group_part,
    keys,
    marks,
    blocks,
    queries,
    total,
    top,
    weight_sum,
    flat_lat,
    flat_rope,
    in_sem,
    ra_send,
    ra_recv,
    rb_send,
    rb_recv,
    z1_send,
    z1_recv,
    z2_send,
    z2_recv,
    x_send,
    x_recv,
    xf_send,
    xf_recv,
    d_send,
    d_recv,
    y_send,
    y_recv,
    yd_send,
    yd_recv,
):
    n_rep, n_x, n_hi, n_lo = shape
    n_z = n_hi * n_lo
    heads, nope, lat = w_uk.shape
    rope = pre_rope.shape[1]
    width = keys.shape[-1]
    value = w_uv.shape[2]
    tok = hidden.shape[0]

    replica = lax.axis_index("replica")
    context = lax.axis_index("context")
    tensor = lax.axis_index("tensor")
    x = lax.div(context, n_hi)
    z_hi = lax.rem(context, n_hi)
    z_lo = lax.div(tensor, 2)
    core = lax.rem(tensor, 2)
    other = 1 - core
    z = z_hi * n_lo + z_lo
    own_kind = 1 + core

    def z_plus(step):
        place = lax.rem(z + step + n_z, n_z)
        return {
            "context": x * n_hi + lax.div(place, n_lo),
            "tensor": lax.rem(place, n_lo) * 2 + core,
        }

    def x_place(step):
        return lax.rem(x + step + n_x, n_x)

    def x_plus(step):
        return {"context": x_place(step) * n_hi + z_hi}

    def hi_place(step):
        return lax.rem(z_hi + step, n_hi)

    def r_plus(step):
        return lax.rem(replica + step, n_rep)

    def group(step):
        return lax.rem(z_lo + step + n_lo, n_lo)

    partner = {"tensor": z_lo * 2 + other}
    two = 2 - 4 * lax.rem(z_lo, 2)

    peers = [partner, z_plus(1), z_plus(-1), z_plus(2), z_plus(-2), x_plus(1), x_plus(-1)]
    peers += [{"context": x * n_hi + hi_place(d)} for d in range(1, n_hi)]
    peers += [{"tensor": group(d) * 2 + core} for d in range(1, n_lo)]
    peers += [{"replica": r_plus(d)} for d in range(1, n_rep)]
    barrier = pltpu.get_barrier_semaphore()
    for peer in peers:
        pl.semaphore_signal(barrier, inc=1, device_id=peer, device_id_type=MESH)

    own_pre = pl.multiple_of(z_lo * PIECE, PIECE)
    loads = [
        (hidden_hbm, hidden),
        (w_latent_hbm, w_latent),
        (w_krope_hbm, w_krope),
        (pre_lat_hbm.at[pl.ds(own_pre, PIECE)], pre_lat),
        (pre_rope_hbm.at[pl.ds(own_pre, PIECE)], pre_rope),
        (q_nope_hbm, q_nope),
        (q_rope_hbm, q_rope),
        (w_uk_hbm, w_uk),
        (w_uv_hbm, w_uv),
    ]
    loads = [
        pltpu.make_async_copy(source, target, in_sem.at[i])
        for i, (source, target) in enumerate(loads)
    ]
    for load in loads:
        load.start()

    def send(source, target, send_sem, recv_sem, device):
        return pltpu.make_async_remote_copy(
            src_ref=source,
            dst_ref=target,
            send_sem=send_sem,
            recv_sem=recv_sem,
            device_id=device,
            device_id_type=MESH,
        )

    def same(ref, send_sem, recv_sem, device):
        return send(ref, ref, send_sem, recv_sem, device)

    def ra_copy():
        return send(partial.at[other], partner_part, ra_send, ra_recv, partner)

    def rb_copy(d):
        to = lax.rem(z_lo + d, n_lo)
        return send(
            chip_sum.at[to],
            group_part.at[d - 1],
            rb_send.at[d - 1],
            rb_recv.at[d - 1],
            {"tensor": to * 2 + core},
        )

    def kind_of(flow):
        return own_kind if flow else 0

    def z1_copy(flow, d):
        return same(
            keys.at[kind_of(flow), z_lo, z_hi, x],
            z1_send.at[flow, d - 1],
            z1_recv.at[flow, d - 1],
            {"context": x * n_hi + hi_place(d)},
        )

    def z1_arrival(flow, d):
        return same(
            keys.at[kind_of(flow), z_lo, hi_place(n_hi - d), x],
            z1_send.at[flow, d - 1],
            z1_recv.at[flow, d - 1],
            partner,
        )

    z2_steps = (1, -1, two)

    def z2_copy(flow, i):
        return same(
            keys.at[kind_of(flow), z_lo, :, x],
            z2_send.at[flow, i],
            z2_recv.at[flow, i],
            z_plus(z2_steps[i]),
        )

    def z2_arrival(flow, i):
        return same(
            keys.at[kind_of(flow), group(-z2_steps[i]), :, x],
            z2_send.at[flow, i],
            z2_recv.at[flow, i],
            partner,
        )

    def x_copy(flow, g, i):
        return same(
            keys.at[kind_of(flow), g, :, x],
            x_send.at[flow, g, i],
            x_recv.at[flow, g, i],
            x_plus(1 - 2 * i),
        )

    def x_arrival(flow, g, i):
        return same(
            keys.at[kind_of(flow), g, :, x_place(2 * i - 1)],
            x_send.at[flow, g, i],
            x_recv.at[flow, g, i],
            partner,
        )

    def xf_copy(flow, g):
        way = 1 - 2 * lax.rem(g, 2)
        return same(
            keys.at[kind_of(flow), g, :, x_place(-way)],
            xf_send.at[flow, g],
            xf_recv.at[flow, g],
            x_plus(way),
        )

    def xf_arrival(flow, g):
        return same(
            keys.at[kind_of(flow), g, :, x_place(2)],
            xf_send.at[flow, g],
            xf_recv.at[flow, g],
            partner,
        )

    def d_copy(flow, g):
        return same(
            keys.at[kind_of(flow), g], d_send.at[flow, g], d_recv.at[flow, g], partner
        )

    def d_arrival(flow, g):
        kind = 2 - core if flow else 0
        return same(keys.at[kind, g], d_send.at[flow, g], d_recv.at[flow, g], partner)

    def push_x(flow, g):
        for i in range(2):
            x_copy(flow, g, i).start()

    def forward_x(flow, g):
        for i in range(2):
            x_arrival(flow, g, i).wait_recv()
        xf_copy(flow, g).start()

    def to_partner(flow, g):
        xf_arrival(flow, g).wait_recv()
        d_copy(flow, g).start()

    match = lax.rem(z_lo, 2) == core
    first_group = jnp.where(match, z_lo, group(-1))

    def mine(i):
        return lax.rem(first_group + 2 * i, n_lo)

    def y_copy(d):
        return send(
            keys.at[own_kind, :, z_hi, x],
            blocks.at[core, pl.ds(replica * n_lo, n_lo)],
            y_send.at[d - 1],
            y_recv.at[d - 1],
            {"replica": r_plus(d)},
        )

    def y_arrival(d):
        return send(
            keys.at[own_kind, :, z_hi, x],
            blocks.at[core, pl.ds(r_plus(n_rep - d) * n_lo, n_lo)],
            y_send.at[d - 1],
            y_recv.at[d - 1],
            partner,
        )

    def yd_copy():
        return same(blocks.at[core], yd_send, yd_recv, partner)

    def yd_arrival():
        return same(blocks.at[other], yd_send, yd_recv, partner)

    loads[0].wait()
    loads[1].wait()
    loads[2].wait()
    lat_term = jnp.dot(hidden[...], w_latent[...], preferred_element_type=jnp.float32)
    rope_term = lax.dot_general(
        hidden[...], w_krope[...], (((1,), (1,)), ((), ())), preferred_element_type=jnp.float32
    )
    rope_term = jnp.concatenate(
        [rope_term, jnp.zeros((tok, width - lat - rope), jnp.float32)], axis=1
    )
    for place in range(n_lo):
        for who in range(2):
            first = (place * 2 + who) * PIECE
            partial[who, place, :, :lat] = lat_term[first : first + PIECE]
            partial[who, place, :, lat:] = rope_term[first : first + PIECE]
    loads[3].wait()
    loads[4].wait()
    keys[0, z_lo, z_hi, x, :, :lat] = pre_lat[...]
    length = length_ref[0]
    n_context = n_x * n_hi
    piece_row = lax.broadcasted_iota(jnp.int32, (PIECE, width - lat), 0)
    piece_lanes = lax.broadcasted_iota(jnp.int32, (PIECE, width - lat), 1)
    pre_place = context * (n_lo * PIECE) + z_lo * PIECE + piece_row
    hidden_key = jnp.logical_and(piece_lanes == rope + n_context, pre_place >= length)
    pre_tail = jnp.concatenate(
        [
            pre_rope[...].astype(jnp.float32),
            jnp.zeros((PIECE, width - lat - rope), jnp.float32),
        ],
        axis=1,
    )
    keys[0, z_lo, z_hi, x, :, lat:] = jnp.where(hidden_key, MASKED, pre_tail).astype(
        jnp.bfloat16
    )

    pl.semaphore_wait(barrier, len(peers))
    ra_copy().start()

    def prefix_z1():
        for d in range(1, n_hi):
            z1_copy(0, d).start()

    pl.when(match)(prefix_z1)

    loads[5].wait()
    loads[6].wait()
    loads[7].wait()
    lanes = lax.broadcasted_iota(jnp.int32, (tok, width - lat), 1)
    later = jnp.logical_and(lanes > rope + context, lanes < rope + n_context)
    masks = jnp.where(later, MASKED, jnp.where(lanes == rope + n_context, 1.0, 0.0))
    query_row = lax.broadcasted_iota(jnp.int32, (tok, tok), 0)
    key_lane = lax.broadcasted_iota(jnp.int32, (tok, tok), 1)
    triangle = jnp.where(key_lane > query_row, MASKED, 0.0).astype(jnp.bfloat16)
    marks[...] = jnp.zeros_like(marks)
    mark_row = lax.broadcasted_iota(jnp.int32, (PIECE, tok), 0)
    mark_lane = lax.broadcasted_iota(jnp.int32, (PIECE, tok), 1)
    for place in range(n_lo):
        for who in range(2):
            first = (place * 2 + who) * PIECE
            marks[1 + who, place, z_hi, x] = jnp.where(
                mark_lane == first + mark_row, 1.0, 0.0
            ).astype(jnp.bfloat16)

    def absorb(first, last):
        for head in range(first, last):
            rows = pl.ds(head * tok, tok)
            queries[rows, :lat] = jnp.dot(
                q_nope[:, head * nope : (head + 1) * nope],
                w_uk[head],
                preferred_element_type=jnp.float32,
            ).astype(jnp.bfloat16)
            pair = q_rope[:, (head // 2) * 2 * rope : (head // 2 + 1) * 2 * rope]
            pair = pair.astype(jnp.float32)
            if head % 2:
                pair = pltpu.roll(pair, rope, 1)
            queries[rows, lat:width] = jnp.where(lanes < rope, pair, masks).astype(jnp.bfloat16)
            queries[rows, width:] = triangle

    absorb(0, heads // 2)

    ra_copy().wait_recv()
    chip_sum[...] = partial[core] + partner_part[...]
    for d in range(1, n_lo):
        rb_copy(d).start()

    def prefix_z2():
        for d in range(1, n_hi):
            z1_arrival(0, d).wait_recv()
        for i in range(3):
            z2_copy(0, i).start()
        push_x(0, z_lo)

    pl.when(match)(prefix_z2)
    absorb(heads // 2, heads)

    position = (
        length
        + context * tok
        + tensor * PIECE
        + piece_row
    )
    sine, cosine = sine_cosine(position.astype(jnp.float32) * frequency_ref[...])
    sine = jnp.where(piece_lanes < rope // 2, -sine, sine)
    sine = jnp.where(piece_lanes < rope, sine, 0.0)

    top[...] = jnp.full_like(top, FLOOR)
    weight_sum[...] = jnp.zeros_like(weight_sum)
    total[...] = jnp.zeros_like(total)

    def prefix_far():
        z2_arrival(0, 2).wait_recv()
        push_x(0, group(2))

    def prefix_near():
        for i in (0, 1):
            z2_arrival(0, i).wait_recv()
            push_x(0, group(-z2_steps[i]))

    pl.when(match)(prefix_far)
    pl.when(jnp.logical_not(match))(prefix_near)

    for d in range(1, n_lo):
        rb_copy(d).wait_recv()
    summed = chip_sum[z_lo]
    for d in range(1, n_lo):
        summed = summed + group_part[d - 1]
    lat_sum = summed[:, :lat]
    mean_square = jnp.mean(lat_sum * lat_sum, axis=1, keepdims=True)
    keys[own_kind, z_lo, z_hi, x, :, :lat] = (
        lat_sum * lax.rsqrt(mean_square + NORM_EPS) * gain_ref[...]
    ).astype(jnp.bfloat16)
    rope_sum = summed[:, lat:]
    swapped = jnp.where(
        piece_lanes < rope // 2,
        pltpu.roll(rope_sum, width - lat - rope // 2, 1),
        pltpu.roll(rope_sum, rope // 2, 1),
    )
    new_tail = rope_sum * cosine + swapped * sine
    keys[own_kind, z_lo, z_hi, x, :, lat:] = jnp.where(
        piece_lanes == rope + context, 1.0, new_tail
    ).astype(jnp.bfloat16)

    for d in range(1, n_hi):
        z1_copy(1, d).start()
    for i in range(2):
        forward_x(0, mine(i))
    for d in range(1, n_hi):
        z1_arrival(1, d).wait_recv()
    for i in range(3):
        z2_copy(1, i).start()
    push_x(1, z_lo)
    for i in range(2):
        to_partner(0, mine(i))

    score_scale = float((nope + rope) ** (-0.5) * math.log2(math.e))

    key_count = n_hi * n_x * PIECE

    def attend(places, first):
        key_rows = jnp.concatenate(
            [
                jnp.concatenate(
                    [
                        keys[kind, g].reshape(key_count, width),
                        marks[kind, g].reshape(key_count, tok),
                    ],
                    axis=1,
                )
                for kind, g in places
            ],
            axis=0,
        )
        tiles = len(places) * key_count // 128
        at_once = min(ROWS, heads * tok // 2)
        for part in range(heads * tok // 2 // at_once):
            rows = pl.ds(pl.multiple_of(first + part * at_once, at_once), at_once)
            scores = lax.dot_general(
                queries[rows, :],
                key_rows,
                (((1,), (1,)), ((), ())),
                preferred_element_type=jnp.float32,
            )
            scores = scores * score_scale
            old_top = top[rows, :]
            new_top = jnp.maximum(old_top, jnp.max(scores, axis=1, keepdims=True))
            top[rows, :] = new_top
            rescale = jnp.exp2(old_top - new_top)
            exponents = [
                jnp.exp2(scores[:, i * 128 : (i + 1) * 128] - new_top) for i in range(tiles)
            ]
            weight_sum[rows, :] = weight_sum[rows, :] * rescale + sum(exponents)
            weights = jnp.concatenate([e.astype(jnp.bfloat16) for e in exponents], axis=1)
            total[rows, :] = total[rows, :] * jnp.concatenate(
                [rescale] * (lat // 128), axis=1
            ) + jnp.dot(weights, key_rows[:, :lat], preferred_element_type=jnp.float32)


    def new_group(i):
        step = jnp.where(i == 1, n_lo - 1, jnp.where(i == 2, 1, jnp.where(i == 3, 2, 0)))
        return lax.rem(z_lo + step, n_lo)

    def second_level():
        for i in range(3):
            z2_arrival(1, i).wait_recv()
            push_x(1, group(-z2_steps[i]))
        for d in range(1, n_rep):
            y_copy(d).start()
        for place in range(n_lo):
            blocks[core, replica * n_lo + place] = keys[own_kind, place, z_hi, x]

    def owners():
        for d in range(1, n_rep):
            y_arrival(d).wait_recv()
        yd_copy().start()

    def step_1():
        forward_x(1, group(0))

    def step_2():
        for i in (1, 3):
            d_arrival(0, lax.rem(first_group + i, n_lo)).wait_recv()
        second_level()

    def step_3():
        to_partner(1, group(0))

    def step_4():
        forward_x(1, group(-1))
        d_arrival(1, group(0)).wait_recv()

    def step_5():
        forward_x(1, group(1))
        to_partner(1, group(-1))

    def step_6():
        forward_x(1, group(2))
        to_partner(1, group(1))
        d_arrival(1, group(-1)).wait_recv()

    def step_7():
        to_partner(1, group(2))
        owners()

    def step_8():
        d_arrival(1, group(1)).wait_recv()

    def step_10():
        d_arrival(1, group(2)).wait_recv()

    actions = {
        1: step_1,
        2: step_2,
        3: step_3,
        4: step_4,
        5: step_5,
        6: step_6,
        7: step_7,
        8: step_8,
        10: step_10,
    }

    def iteration(step, carry):
        for number, action in actions.items():
            pl.when(step == number)(action)
        chunk = lax.div(step, 2)
        is_new = chunk >= 2
        g = new_group(jnp.maximum(chunk - 2, 0))
        pre = lax.rem(first_group + chunk, n_lo)
        attend(
            [
                (jnp.where(is_new, 1, 0), jnp.where(is_new, g, pre)),
                (jnp.where(is_new, 2, 0), jnp.where(is_new, g, lax.rem(pre + 2, n_lo))),
            ],
            lax.rem(step, 2) * (heads * tok // 2),
        )
        return carry

    lax.fori_loop(0, 2 * (2 + n_lo), iteration, 0)

    loads[8].wait()
    for head in range(heads):
        rows = pl.ds(head * tok, tok)
        row_sum = jnp.sum(weight_sum[rows, :], axis=1, keepdims=True)
        latent_out = (total[rows, :] / row_sum).astype(jnp.bfloat16)
        out_ref[:, head * value : (head + 1) * value] = jnp.dot(
            latent_out, w_uv[head], preferred_element_type=jnp.float32
        ).astype(jnp.bfloat16)

    yd_arrival().wait_recv()
    tile = lat // TILES
    per_block = BLOCK // (2 * PIECE)
    flat_scales = []
    scale_row = lax.broadcasted_iota(jnp.int32, (BLOCK, BLOCK * TILES), 0)
    scale_lane = lax.broadcasted_iota(jnp.int32, (BLOCK, BLOCK * TILES), 1)
    rope_lane = lax.broadcasted_iota(jnp.int32, (BLOCK, 2 * rope), 1)
    for slot in range(2):
        source = jnp.int32(0)
        for candidate in range(n_rep * 2):
            source = jnp.where(
                places_ref[0, candidate] == replica * 2 + slot, candidate, source
            )
        rows = jnp.concatenate(
            [
                blocks[who, source * per_block + place]
                for place in range(per_block)
                for who in range(2)
            ],
            axis=0,
        ).astype(jnp.float32)
        flat = jnp.zeros((BLOCK, BLOCK * TILES), jnp.float32)
        held = pl.ds(slot * BLOCK, BLOCK)
        for i in range(TILES):
            entries = rows[:, i * tile : (i + 1) * tile]
            scale = jnp.max(jnp.abs(entries), axis=1, keepdims=True) + SCALE_EPS
            scale = scale.astype(jnp.bfloat16).astype(jnp.float32)
            flat_lat[i, held, :] = entries / scale
            flat = jnp.where(scale_lane == scale_row * TILES + i, scale, flat)
        flat_scales.append(jnp.sum(flat, axis=0, keepdims=True))
        tail = rows[:, lat : lat + 2 * rope]
        following = pltpu.roll(pltpu.roll(tail, BLOCK - 1, 0), rope, 1)
        flat_rope[held, :] = jnp.where(rope_lane < rope, tail, following)
    for j in range(BLOCK):
        for i in range(TILES):
            first = j * lat + i * tile
            cache_lat_ref[:, first : first + tile] = flat_lat[
                i, pl.ds(j, 2, stride=BLOCK), :
            ].astype(jnp.bfloat16)
    for j in range(BLOCK // 2):
        cache_rope_ref[:, j * 2 * rope : (j + 1) * 2 * rope] = flat_rope[
            pl.ds(2 * j, 2, stride=BLOCK), :
        ].astype(jnp.bfloat16)
    cache_scale_ref[...] = jnp.concatenate(flat_scales, axis=0).astype(jnp.bfloat16)

    ra_copy().wait_send()
    for d in range(1, n_lo):
        rb_copy(d).wait_send()
    for d in range(1, n_rep):
        y_copy(d).wait_send()
    yd_copy().wait_send()

    def z_sent(flow):
        for d in range(1, n_hi):
            z1_copy(flow, d).wait_send()
        for i in range(3):
            z2_copy(flow, i).wait_send()

    def x_sent(flow, g):
        for i in range(2):
            x_copy(flow, g, i).wait_send()
        xf_copy(flow, g).wait_send()
        d_copy(flow, g).wait_send()

    pl.when(match)(lambda: z_sent(0))
    z_sent(1)
    for i in range(2):
        x_sent(0, mine(i))
    for g in range(n_lo):
        x_sent(1, g)


def per_device(
    shape,
    hidden,
    q_nope,
    q_rope,
    w_latent,
    w_krope,
    kv_gain,
    w_uk,
    w_uv,
    prefix_latent,
    prefix_rope,
    prefix_lengths,
    placements,
):
    n_rep, n_x, n_hi, n_lo = shape
    tok, depth = hidden.shape[1:]
    heads, nope, lat = w_uk.shape
    rope = w_krope.shape[1]
    value = w_uv.shape[2]
    width = -(-(lat + rope) // 128) * 128
    count = rope // 2
    powers = -(np.arange(count, dtype=np.float32) * np.float32(2.0)) / np.float32(rope)
    frequency = np.power(np.float64(ROPE_THETA), powers.astype(np.float64))
    frequency = np.resize(frequency, (1, width - lat)).astype(np.float32)
    vmem = pl.BlockSpec(memory_space=pltpu.VMEM)
    smem = pl.BlockSpec(memory_space=pltpu.SMEM)
    anywhere = pl.BlockSpec(memory_space=pl.ANY)
    bf16, f32 = jnp.bfloat16, jnp.float32
    dma = pltpu.SemaphoreType.DMA
    out = pl.pallas_call(
        functools.partial(kernel, shape),
        out_shape=(
            jax.ShapeDtypeStruct((tok, heads * value), bf16),
            jax.ShapeDtypeStruct((2, BLOCK * lat), bf16),
            jax.ShapeDtypeStruct((2, BLOCK * rope), bf16),
            jax.ShapeDtypeStruct((2, BLOCK * TILES), bf16),
        ),
        in_specs=[smem, smem, vmem, vmem] + [anywhere] * 9,
        out_specs=(vmem, vmem, vmem, vmem),
        scratch_shapes=[
            pltpu.VMEM((tok, depth), bf16),
            pltpu.VMEM((tok, heads * nope), bf16),
            pltpu.VMEM((tok, heads * rope), bf16),
            pltpu.VMEM((depth, lat), bf16),
            pltpu.VMEM((rope, depth), bf16),
            pltpu.VMEM((heads, nope, lat), bf16),
            pltpu.VMEM((heads, lat, value), bf16),
            pltpu.VMEM((PIECE, lat), bf16),
            pltpu.VMEM((PIECE, rope), bf16),
            pltpu.VMEM((2, n_lo, PIECE, width), f32),
            pltpu.VMEM((n_lo, PIECE, width), f32),
            pltpu.VMEM((n_lo, PIECE, width), f32),
            pltpu.VMEM((max(n_lo - 1, 1), PIECE, width), f32),
            pltpu.VMEM((3, n_lo, n_hi, n_x, PIECE, width), bf16),
            pltpu.VMEM((3, n_lo, n_hi, n_x, PIECE, tok), bf16),
            pltpu.VMEM((2, n_rep * n_lo, PIECE, width), bf16),
            pltpu.VMEM((heads * tok, width + tok), bf16),
            pltpu.VMEM((heads * tok, lat), f32),
            pltpu.VMEM((heads * tok, 128), f32),
            pltpu.VMEM((heads * tok, 128), f32),
            pltpu.VMEM((TILES, 2 * BLOCK, lat // TILES), f32),
            pltpu.VMEM((2 * BLOCK, 2 * rope), f32),
            dma((9,)),
            dma,
            dma,
            dma((max(n_lo - 1, 1),)),
            dma((max(n_lo - 1, 1),)),
            dma((2, n_hi - 1)),
            dma((2, n_hi - 1)),
            dma((2, 3)),
            dma((2, 3)),
            dma((2, n_lo, 2)),
            dma((2, n_lo, 2)),
            dma((2, n_lo)),
            dma((2, n_lo)),
            dma((2, n_lo)),
            dma((2, n_lo)),
            dma((max(n_rep - 1, 1),)),
            dma((max(n_rep - 1, 1),)),
            dma,
            dma,
        ],
        compiler_params=pltpu.CompilerParams(
            collective_id=0, has_side_effects=True, vmem_limit_bytes=56 * 1024 * 1024
        ),
    )(
        prefix_lengths,
        placements,
        jnp.asarray(frequency),
        kv_gain.reshape(1, lat),
        hidden[0],
        q_nope[0],
        q_rope[0],
        w_latent,
        w_krope.T,
        w_uk,
        w_uv,
        prefix_latent[0],
        prefix_rope[0],
    )
    return tuple(result[None] for result in out)


def program(mesh, shape):
    return jax.shard_map(
        functools.partial(per_device, shape),
        mesh=mesh,
        in_specs=(
            P("replica", "context", "tensor"),
            P("replica", "context", "tensor"),
            P("replica", "context", "tensor"),
            P("tensor", None),
            P("tensor", None),
            P(),
            P("tensor", None, None),
            P("tensor", None, None),
            P("replica", "context", None),
            P("replica", "context", None),
            P("replica"),
            P("context", None),
        ),
        out_specs=(
            P("replica", "context", "tensor"),
            P("replica", "context", None),
            P("replica", "context", None),
            P("replica", "context", None),
        ),
        check_vma=False,
    )


def solution(mesh):
    n_hi = 4
    return program(
        mesh,
        (
            mesh.shape["replica"],
            mesh.shape["context"] // n_hi,
            n_hi,
            mesh.shape["tensor"] // 2,
        ),
    )
```

```python
import functools
import math

import jax
import jax.numpy as jnp
import numpy as np
from jax import lax
from jax.experimental import pallas as pl
from jax.experimental.pallas import tpu as pltpu
from jax.sharding import PartitionSpec as P

MESH = pl.DeviceIdType.MESH
BLOCK = 64
TILES = 4
PIECE = 16
ROWS = 256
ROPE_THETA = 50000.0
NORM_EPS = 1e-06
SCALE_EPS = 1e-06
MASKED = -1e30
FLOOR = -1e28


def when(condition, action):
    if isinstance(condition, bool):
        if condition:
            action()
    else:
        pl.when(condition)(action)


def both(first, second):
    if isinstance(first, bool):
        return first and second
    return jnp.logical_and(first, second)


def sine_cosine(angle):
    turns = jnp.floor(angle * np.float32(1.0 / (2.0 * math.pi)) + 0.5)
    high = 6.28125
    middle = float(np.float32(0.0019350051879882812))
    low = 2.0 * math.pi - high - middle
    r = angle - turns * np.float32(high)
    r = r - turns * np.float32(middle)
    r = r - turns * np.float32(low)
    square = r * r
    sine = jnp.full_like(r, 1.0 / math.factorial(17))
    for n in (15, 13, 11, 9, 7, 5, 3, 1):
        sign = -1.0 if (n // 2) % 2 else 1.0
        sine = sine * square + sign / math.factorial(n)
    cosine = jnp.full_like(r, 1.0 / math.factorial(16))
    for n in (14, 12, 10, 8, 6, 4, 2, 0):
        sign = -1.0 if (n // 2) % 2 else 1.0
        cosine = cosine * square + sign / math.factorial(n)
    return sine * r, cosine


def kernel(
    shape,
    length_ref,
    places_ref,
    frequency_ref,
    gain_ref,
    hidden_hbm,
    q_nope_hbm,
    q_rope_hbm,
    w_latent_hbm,
    w_krope_hbm,
    w_uk_hbm,
    w_uv_hbm,
    pre_lat_hbm,
    pre_rope_hbm,
    out_ref,
    cache_lat_ref,
    cache_rope_ref,
    cache_scale_ref,
    hidden,
    q_nope,
    q_rope,
    w_latent,
    w_krope,
    w_uk,
    w_uv,
    pre_lat,
    pre_rope,
    partial,
    partner_part,
    chip_sum,
    group_part,
    fresh,
    prefix,
    marks,
    blocks,
    queries,
    total,
    top,
    weight_sum,
    flat_rope,
    in_sem,
    ra_send,
    ra_recv,
    rb_send,
    rb_recv,
    own_send,
    own_recv,
    twin_send,
    twin_recv,
    z_send,
    z_recv,
    x_send,
    x_recv,
    d_send,
    d_recv,
    y_send,
    y_recv,
    yd_send,
    yd_recv,
):
    n_rep, n_x, n_hi, n_lo = shape
    n_z = n_hi * n_lo
    half = n_z // 2
    heads, nope, lat = w_uk.shape
    rope = pre_rope.shape[1]
    width = prefix.shape[-1]
    value = w_uv.shape[2]
    tok = hidden.shape[0]

    replica = lax.axis_index("replica")
    context = lax.axis_index("context")
    tensor = lax.axis_index("tensor")
    x = lax.div(context, n_hi)
    z_hi = lax.rem(context, n_hi)
    z_lo = lax.div(tensor, 2)
    core = lax.rem(tensor, 2)
    other = 1 - core
    z = z_hi * n_lo + z_lo
    sign = 1 - 2 * core

    def z_place(step):
        return lax.rem(z + step + n_z, n_z)

    def z_plus(step):
        place = z_place(step)
        return {
            "context": x * n_hi + lax.div(place, n_lo),
            "tensor": lax.rem(place, n_lo) * 2 + core,
        }

    def x_place(step):
        return lax.rem(x + step + n_x, n_x)

    def x_plus(step, who=core):
        return {"context": x_place(step) * n_hi + z_hi, "tensor": z_lo * 2 + who}

    def r_plus(step):
        return lax.rem(replica + step, n_rep)

    def group(step):
        return lax.rem(z_lo + step + n_lo, n_lo)

    partner = {"tensor": z_lo * 2 + other}

    peers = [partner, z_plus(1), z_plus(-1)]
    peers += [x_plus(d, who) for d in range(1, n_x) for who in (core, other)]
    peers += [{"tensor": group(d) * 2 + core} for d in range(1, n_lo)]
    peers += [{"replica": r_plus(d)} for d in range(1, n_rep)]
    barrier = pltpu.get_barrier_semaphore()
    for peer in peers:
        pl.semaphore_signal(barrier, inc=1, device_id=peer, device_id_type=MESH)

    own_pre = pl.multiple_of(z_lo * PIECE, PIECE)
    depth = hidden.shape[1]
    cuts = range(0, depth, 128)
    loads = {
        "prefix": [
            (pre_lat_hbm.at[pl.ds(own_pre, PIECE)], pre_lat),
            (pre_rope_hbm.at[pl.ds(own_pre, PIECE)], pre_rope),
        ],
        "hidden": [(hidden_hbm, hidden), (w_krope_hbm, w_krope)]
        + [
            (w_latent_hbm.at[pl.ds(first, 128)], w_latent.at[pl.ds(first, 128)])
            for first in cuts
        ],
        "query": [(q_nope_hbm, q_nope), (q_rope_hbm, q_rope)]
        + [(w_uk_hbm.at[head], w_uk.at[head]) for head in range(heads)],
        "value": [(w_uv_hbm.at[head], w_uv.at[head]) for head in range(heads)],
    }
    number = 0
    for name, pairs in loads.items():
        copies = []
        for source, target in pairs:
            copies.append(pltpu.make_async_copy(source, target, in_sem.at[number]))
            number += 1
        loads[name] = copies
    for name in ("hidden", "prefix", "query", "value"):
        for load in loads[name]:
            load.start()

    def loaded(name):
        for load in loads[name]:
            load.wait()

    def send(source, target, send_sem, recv_sem, device):
        return pltpu.make_async_remote_copy(
            src_ref=source,
            dst_ref=target,
            send_sem=send_sem,
            recv_sem=recv_sem,
            device_id=device,
            device_id_type=MESH,
        )

    def same(ref, send_sem, recv_sem, device):
        return send(ref, ref, send_sem, recv_sem, device)

    def ra_copy():
        return send(partial.at[other], partner_part, ra_send, ra_recv, partner)

    def rb_copy(d):
        to = lax.rem(z_lo + d, n_lo)
        return send(
            chip_sum.at[to],
            group_part.at[d - 1],
            rb_send.at[d - 1],
            rb_recv.at[d - 1],
            {"tensor": to * 2 + core},
        )

    def slots_of(flow):
        return fresh if flow else prefix

    def own_copies(flow):
        copies = []
        piece = fresh.at[z, x, core] if flow else prefix.at[z, x]
        for d in range(1, n_x):
            for i, who in enumerate((core, other) if flow else (core,)):
                copies.append(
                    same(
                        piece,
                        own_send.at[flow, d - 1, i],
                        own_recv.at[flow, d - 1, core],
                        x_plus(d, who),
                    )
                )
        return copies

    def own_arrival(flow, d, who):
        place = x_place(-d)
        piece = fresh.at[z, place, who] if flow else prefix.at[z, place]
        return same(piece, own_send.at[flow, d - 1, 0], own_recv.at[flow, d - 1, who], partner)

    def own_arrived(flow, d):
        own_arrival(flow, d, core).wait_recv()
        if flow:
            own_arrival(flow, d, other).wait_recv()

    def twin_copy():
        return same(fresh.at[z, x, core], twin_send, twin_recv, partner)

    def twin_arrival():
        return same(fresh.at[z, x, other], twin_send, twin_recv, partner)

    def z_copy(flow, s, i):
        return same(
            slots_of(flow).at[z_place(-sign * (s - 1)), x_place(2 * i)],
            z_send.at[flow, s, i],
            z_recv.at[flow, s, i],
            z_plus(sign),
        )

    def z_arrival(flow, s, i):
        return same(
            slots_of(flow).at[z_place(-sign * s), x_place(2 * i)],
            z_send.at[flow, s, i],
            z_recv.at[flow, s, i],
            partner,
        )

    def x_copy(flow, s, i):
        return same(
            slots_of(flow).at[z_place(-sign * s), x],
            x_send.at[flow, s, i],
            x_recv.at[flow, s, i],
            x_plus(1 - 2 * i),
        )

    def x_arrival(flow, s, i):
        return same(
            slots_of(flow).at[z_place(-sign * s), x_place(2 * i - 1)],
            x_send.at[flow, s, i],
            x_recv.at[flow, s, i],
            partner,
        )

    def d_copy(flow, s):
        return same(
            slots_of(flow).at[z_place(-sign * s)], d_send.at[flow, s], d_recv.at[flow, s], partner
        )

    def d_arrival(flow, s):
        return same(
            slots_of(flow).at[z_place(sign * s)], d_send.at[flow, s], d_recv.at[flow, s], partner
        )

    def come(flow, s):
        z_arrival(flow, s, 0).wait_recv()
        when(s < half, lambda: z_copy(flow, s + 1, 0).start())
        for i in range(2):
            x_copy(flow, s, i).start()
        z_arrival(flow, s, 1).wait_recv()
        when(s < half, lambda: z_copy(flow, s + 1, 1).start())

    def cross(flow, s):
        for i in range(2):
            x_arrival(flow, s, i).wait_recv()
        when(s < half, lambda: d_copy(flow, s).start())

    def stage(flow, s):
        when(s <= half, lambda: come(flow, s))
        when(both(s >= 2, s <= half + 1), lambda: cross(flow, s - 1))
        when(both(s >= 3, s <= half + 1), lambda: d_arrival(flow, s - 2).wait_recv())

    def y_copy(d):
        return send(
            fresh.at[pl.ds(z_hi * n_lo, n_lo), x, core],
            blocks.at[core, pl.ds(replica * n_lo, n_lo)],
            y_send.at[d - 1],
            y_recv.at[d - 1],
            {"replica": r_plus(d)},
        )

    def y_arrival(d):
        return send(
            fresh.at[pl.ds(z_hi * n_lo, n_lo), x, core],
            blocks.at[core, pl.ds(r_plus(n_rep - d) * n_lo, n_lo)],
            y_send.at[d - 1],
            y_recv.at[d - 1],
            partner,
        )

    def yd_copy():
        return same(blocks.at[core], yd_send, yd_recv, partner)

    def yd_arrival():
        return same(blocks.at[other], yd_send, yd_recv, partner)

    loaded("hidden")
    lat_term = jnp.dot(hidden[...], w_latent[...], preferred_element_type=jnp.float32)
    rope_term = lax.dot_general(
        hidden[...], w_krope[...], (((1,), (1,)), ((), ())), preferred_element_type=jnp.float32
    )
    rope_term = jnp.concatenate(
        [rope_term, jnp.zeros((tok, width - lat - rope), jnp.float32)], axis=1
    )
    for place in range(n_lo):
        for who in range(2):
            first = (place * 2 + who) * PIECE
            partial[who, place, :, :lat] = lat_term[first : first + PIECE]
            partial[who, place, :, lat:] = rope_term[first : first + PIECE]
    loaded("prefix")
    prefix[z, x, :, :lat] = pre_lat[...]
    length = length_ref[0]
    n_context = n_x * n_hi
    piece_row = lax.broadcasted_iota(jnp.int32, (PIECE, width - lat), 0)
    piece_lanes = lax.broadcasted_iota(jnp.int32, (PIECE, width - lat), 1)
    pre_place = context * (n_lo * PIECE) + z_lo * PIECE + piece_row
    hidden_key = jnp.logical_and(piece_lanes == rope + n_context, pre_place >= length)
    pre_tail = jnp.concatenate(
        [
            pre_rope[...].astype(jnp.float32),
            jnp.zeros((PIECE, width - lat - rope), jnp.float32),
        ],
        axis=1,
    )
    prefix[z, x, :, lat:] = jnp.where(hidden_key, MASKED, pre_tail).astype(
        jnp.bfloat16
    )

    pl.semaphore_wait(barrier, len(peers))
    ra_copy().start()
    z_copy(0, 1, 0).start()
    for copy in own_copies(0):
        copy.start()

    loaded("query")
    lanes = lax.broadcasted_iota(jnp.int32, (tok, width - lat), 1)
    later = jnp.logical_and(lanes > rope + context, lanes < rope + n_context)
    masks = jnp.where(later, MASKED, jnp.where(lanes == rope + n_context, 1.0, 0.0))
    query_row = lax.broadcasted_iota(jnp.int32, (tok, tok), 0)
    key_lane = lax.broadcasted_iota(jnp.int32, (tok, tok), 1)
    triangle = jnp.where(key_lane > query_row, MASKED, 0.0).astype(jnp.bfloat16)
    marks[...] = jnp.zeros_like(marks)
    mark_row = lax.broadcasted_iota(jnp.int32, (PIECE, tok), 0)
    mark_lane = lax.broadcasted_iota(jnp.int32, (PIECE, tok), 1)
    for place in range(n_lo):
        for who in range(2):
            first = (place * 2 + who) * PIECE
            marks[z_hi * n_lo + place, x, who] = jnp.where(
                mark_lane == first + mark_row, 1.0, 0.0
            ).astype(jnp.bfloat16)

    def absorb(first, last):
        for head in range(first, last):
            rows = pl.ds(head * tok, tok)
            queries[rows, :lat] = jnp.dot(
                q_nope[:, head * nope : (head + 1) * nope],
                w_uk[head],
                preferred_element_type=jnp.float32,
            ).astype(jnp.bfloat16)
            pair = q_rope[:, (head // 2) * 2 * rope : (head // 2 + 1) * 2 * rope]
            pair = pair.astype(jnp.float32)
            if head % 2:
                pair = pltpu.roll(pair, rope, 1)
            queries[rows, lat:width] = jnp.where(lanes < rope, pair, masks).astype(jnp.bfloat16)
            queries[rows, width:] = triangle

    absorb(0, heads // 2)

    ra_copy().wait_recv()
    chip_sum[...] = partial[core] + partner_part[...]
    for d in range(1, n_lo):
        rb_copy(d).start()

    own_arrived(0, 2)
    z_copy(0, 1, 1).start()
    absorb(heads // 2, heads)

    position = (
        length
        + context * tok
        + tensor * PIECE
        + piece_row
    )
    sine, cosine = sine_cosine(position.astype(jnp.float32) * frequency_ref[...])
    sine = jnp.where(piece_lanes < rope // 2, -sine, sine)
    sine = jnp.where(piece_lanes < rope, sine, 0.0)

    top[...] = jnp.full_like(top, FLOOR)
    weight_sum[...] = jnp.zeros_like(weight_sum)
    total[...] = jnp.zeros_like(total)

    stage(0, 1)
    for d in range(1, n_lo):
        rb_copy(d).wait_recv()
    summed = chip_sum[z_lo]
    for d in range(1, n_lo):
        summed = summed + group_part[d - 1]
    lat_sum = summed[:, :lat]
    mean_square = jnp.mean(lat_sum * lat_sum, axis=1, keepdims=True)
    fresh[z, x, core, :, :lat] = (
        lat_sum * lax.rsqrt(mean_square + NORM_EPS) * gain_ref[...]
    ).astype(jnp.bfloat16)
    rope_sum = summed[:, lat:]
    swapped = jnp.where(
        piece_lanes < rope // 2,
        pltpu.roll(rope_sum, width - lat - rope // 2, 1),
        pltpu.roll(rope_sum, rope // 2, 1),
    )
    new_tail = rope_sum * cosine + swapped * sine
    fresh[z, x, core, :, lat:] = jnp.where(
        piece_lanes == rope + context, 1.0, new_tail
    ).astype(jnp.bfloat16)

    twin_copy().start()
    for copy in own_copies(1):
        copy.start()
    stage(0, 2)
    twin_arrival().wait_recv()
    z_copy(1, 1, 0).start()
    own_arrived(1, 2)
    z_copy(1, 1, 1).start()
    for d in (1, 3):
        own_arrived(0, d)
    stage(0, 3)

    score_scale = float((nope + rope) ** (-0.5) * math.log2(math.e))

    zeros = jnp.zeros((n_x * PIECE, tok), jnp.bfloat16)

    def attend(slots):
        count = n_x * PIECE
        parts = []
        for place in slots:
            parts.append((fresh[place].reshape(2 * count, width), marks[place].reshape(2 * count, tok)))
            parts.append((prefix[place].reshape(count, width), zeros))
        key_rows = jnp.concatenate(
            [jnp.concatenate(part, axis=1) for part in parts], axis=0
        )
        tiles = len(slots) * 3 * count // 128
        at_once = min(ROWS, heads * tok)
        for first in range(0, heads * tok, at_once):
            rows = pl.ds(first, at_once)
            scores = lax.dot_general(
                queries[rows, :],
                key_rows,
                (((1,), (1,)), ((), ())),
                preferred_element_type=jnp.float32,
            )
            scores = scores * score_scale
            old_top = top[rows, :]
            new_top = jnp.maximum(old_top, jnp.max(scores, axis=1, keepdims=True))
            top[rows, :] = new_top
            rescale = jnp.exp2(old_top - new_top)
            exponents = [
                jnp.exp2(scores[:, i * 128 : (i + 1) * 128] - new_top) for i in range(tiles)
            ]
            weight_sum[rows, :] = weight_sum[rows, :] * rescale + sum(exponents)
            weights = jnp.concatenate([e.astype(jnp.bfloat16) for e in exponents], axis=1)
            total[rows, :] = total[rows, :] * jnp.concatenate(
                [rescale] * (lat // 128), axis=1
            ) + jnp.dot(weights, key_rows[:, :lat], preferred_element_type=jnp.float32)


    def to_owners():
        for d in range(1, n_rep):
            y_copy(d).start()
        for place in range(n_lo):
            blocks[core, replica * n_lo + place] = fresh[z_hi * n_lo + place, x, core]

    def owners():
        for d in range(1, n_rep):
            y_arrival(d).wait_recv()
        yd_copy().start()

    def own_slot():
        for d in (1, 3):
            own_arrived(1, d)

    def iteration(s, carry):
        stage(1, s)
        stage(0, s + 3)
        pl.when(s == 2)(own_slot)
        pl.when(s == n_lo + 1)(to_owners)
        pl.when(s == half + 1)(owners)
        pl.when(s >= 3)(
            lambda: attend(
                [z_place(s - 2), jnp.where(s == half + 2, z, z_place(2 - s))]
            )
        )
        return carry

    lax.fori_loop(1, half + 3, iteration, 0)

    loaded("value")
    for head in range(heads):
        rows = pl.ds(head * tok, tok)
        row_sum = jnp.sum(weight_sum[rows, :], axis=1, keepdims=True)
        latent_out = (total[rows, :] / row_sum).astype(jnp.bfloat16)
        out_ref[:, head * value : (head + 1) * value] = jnp.dot(
            latent_out, w_uv[head], preferred_element_type=jnp.float32
        ).astype(jnp.bfloat16)

    yd_arrival().wait_recv()
    tile = lat // TILES
    per_block = BLOCK // (2 * PIECE)
    flat_scales = []
    scale_row = lax.broadcasted_iota(jnp.int32, (BLOCK, BLOCK * TILES), 0)
    scale_lane = lax.broadcasted_iota(jnp.int32, (BLOCK, BLOCK * TILES), 1)
    rope_lane = lax.broadcasted_iota(jnp.int32, (BLOCK, 2 * rope), 1)
    for slot in range(2):
        source = jnp.int32(0)
        for candidate in range(n_rep * 2):
            source = jnp.where(
                places_ref[0, candidate] == replica * 2 + slot, candidate, source
            )
        rows = jnp.concatenate(
            [
                blocks[who, source * per_block + place]
                for place in range(per_block)
                for who in range(2)
            ],
            axis=0,
        ).astype(jnp.float32)
        flat = jnp.zeros((BLOCK, BLOCK * TILES), jnp.float32)
        held = pl.ds(slot * BLOCK, BLOCK)
        for i in range(TILES):
            entries = rows[:, i * tile : (i + 1) * tile]
            scale = jnp.max(jnp.abs(entries), axis=1, keepdims=True) + SCALE_EPS
            scale = scale.astype(jnp.bfloat16).astype(jnp.float32)
            cache_lat_ref[slot, :, i * tile : (i + 1) * tile] = (entries / scale).astype(
                jnp.bfloat16
            )
            flat = jnp.where(scale_lane == scale_row * TILES + i, scale, flat)
        flat_scales.append(jnp.sum(flat, axis=0, keepdims=True))
        tail = rows[:, lat : lat + 2 * rope]
        following = pltpu.roll(pltpu.roll(tail, BLOCK - 1, 0), rope, 1)
        flat_rope[held, :] = jnp.where(rope_lane < rope, tail, following)
    for j in range(BLOCK // 2):
        cache_rope_ref[:, j * 2 * rope : (j + 1) * 2 * rope] = flat_rope[
            pl.ds(2 * j, 2, stride=BLOCK), :
        ].astype(jnp.bfloat16)
    cache_scale_ref[...] = jnp.concatenate(flat_scales, axis=0).astype(jnp.bfloat16)

    ra_copy().wait_send()
    for d in range(1, n_lo):
        rb_copy(d).wait_send()
    for d in range(1, n_rep):
        y_copy(d).wait_send()
    yd_copy().wait_send()

    twin_copy().wait_send()
    for flow in range(2):
        for copy in own_copies(flow):
            copy.wait_send()

    def sent(s, carry):
        for flow in range(2):
            for i in range(2):
                z_copy(flow, s, i).wait_send()
                x_copy(flow, s, i).wait_send()
            pl.when(s < half)(lambda: d_copy(flow, s).wait_send())
        return carry

    lax.fori_loop(1, half + 1, sent, 0)


def per_device(
    shape,
    hidden,
    q_nope,
    q_rope,
    w_latent,
    w_krope,
    kv_gain,
    w_uk,
    w_uv,
    prefix_latent,
    prefix_rope,
    prefix_lengths,
    placements,
):
    n_rep, n_x, n_hi, n_lo = shape
    n_z = n_hi * n_lo
    half = n_z // 2
    tok, depth = hidden.shape[1:]
    heads, nope, lat = w_uk.shape
    rope = w_krope.shape[1]
    value = w_uv.shape[2]
    width = -(-(lat + rope) // 128) * 128
    count = rope // 2
    powers = -(np.arange(count, dtype=np.float32) * np.float32(2.0)) / np.float32(rope)
    frequency = np.power(np.float64(ROPE_THETA), powers.astype(np.float64))
    frequency = np.resize(frequency, (1, width - lat)).astype(np.float32)
    vmem = pl.BlockSpec(memory_space=pltpu.VMEM)
    smem = pl.BlockSpec(memory_space=pltpu.SMEM)
    anywhere = pl.BlockSpec(memory_space=pl.ANY)
    bf16, f32 = jnp.bfloat16, jnp.float32
    dma = pltpu.SemaphoreType.DMA
    out = pl.pallas_call(
        functools.partial(kernel, shape),
        out_shape=(
            jax.ShapeDtypeStruct((tok, heads * value), bf16),
            jax.ShapeDtypeStruct((2, BLOCK, lat), bf16),
            jax.ShapeDtypeStruct((2, BLOCK * rope), bf16),
            jax.ShapeDtypeStruct((2, BLOCK * TILES), bf16),
        ),
        in_specs=[smem, smem, vmem, vmem] + [anywhere] * 9,
        out_specs=(vmem, vmem, vmem, vmem),
        scratch_shapes=[
            pltpu.VMEM((tok, depth), bf16),
            pltpu.VMEM((tok, heads * nope), bf16),
            pltpu.VMEM((tok, heads * rope), bf16),
            pltpu.VMEM((depth, lat), bf16),
            pltpu.VMEM((rope, depth), bf16),
            pltpu.VMEM((heads, nope, lat), bf16),
            pltpu.VMEM((heads, lat, value), bf16),
            pltpu.VMEM((PIECE, lat), bf16),
            pltpu.VMEM((PIECE, rope), bf16),
            pltpu.VMEM((2, n_lo, PIECE, width), f32),
            pltpu.VMEM((n_lo, PIECE, width), f32),
            pltpu.VMEM((n_lo, PIECE, width), f32),
            pltpu.VMEM((max(n_lo - 1, 1), PIECE, width), f32),
            pltpu.VMEM((n_z, n_x, 2, PIECE, width), bf16),
            pltpu.VMEM((n_z, n_x, PIECE, width), bf16),
            pltpu.VMEM((n_z, n_x, 2, PIECE, tok), bf16),
            pltpu.VMEM((2, n_rep * n_lo, PIECE, width), bf16),
            pltpu.VMEM((heads * tok, width + tok), bf16),
            pltpu.VMEM((heads * tok, lat), f32),
            pltpu.VMEM((heads * tok, 128), f32),
            pltpu.VMEM((heads * tok, 128), f32),
            pltpu.VMEM((2 * BLOCK, 2 * rope), f32),
            dma((6 + depth // 128 + 2 * heads,)),
            dma,
            dma,
            dma((max(n_lo - 1, 1),)),
            dma((max(n_lo - 1, 1),)),
            dma((2, n_x - 1, 2)),
            dma((2, n_x - 1, 2)),
            dma,
            dma,
            dma((2, half + 1, 2)),
            dma((2, half + 1, 2)),
            dma((2, half + 1, 2)),
            dma((2, half + 1, 2)),
            dma((2, half + 1)),
            dma((2, half + 1)),
            dma((max(n_rep - 1, 1),)),
            dma((max(n_rep - 1, 1),)),
            dma,
            dma,
        ],
        compiler_params=pltpu.CompilerParams(
            collective_id=0, has_side_effects=True, vmem_limit_bytes=56 * 1024 * 1024
        ),
    )(
        prefix_lengths,
        placements,
        jnp.asarray(frequency),
        kv_gain.reshape(1, lat),
        hidden[0],
        q_nope[0],
        q_rope[0],
        w_latent,
        w_krope.T,
        w_uk,
        w_uv,
        prefix_latent[0],
        prefix_rope[0],
    )
    return tuple(result.reshape(1, result.shape[0], -1) for result in out)


def program(mesh, shape):
    return jax.shard_map(
        functools.partial(per_device, shape),
        mesh=mesh,
        in_specs=(
            P("replica", "context", "tensor"),
            P("replica", "context", "tensor"),
            P("replica", "context", "tensor"),
            P("tensor", None),
            P("tensor", None),
            P(),
            P("tensor", None, None),
            P("tensor", None, None),
            P("replica", "context", None),
            P("replica", "context", None),
            P("replica"),
            P("context", None),
        ),
        out_specs=(
            P("replica", "context", "tensor"),
            P("replica", "context", None),
            P("replica", "context", None),
            P("replica", "context", None),
        ),
        check_vma=False,
    )


def solution(mesh):
    n_hi = 4
    return program(
        mesh,
        (
            mesh.shape["replica"],
            mesh.shape["context"] // n_hi,
            n_hi,
            mesh.shape["tensor"] // 2,
        ),
    )
```

```python
import functools
import math

import jax
import jax.numpy as jnp
import numpy as np
from jax import lax
from jax.experimental import pallas as pl
from jax.experimental.pallas import tpu as pltpu
from jax.sharding import PartitionSpec as P

MESH = pl.DeviceIdType.MESH
BLOCK = 64
TILES = 4
PIECE = 16
ROWS = 512
ROPE_THETA = 50000.0
NORM_EPS = 1e-06
SCALE_EPS = 1e-06
MASKED = -1e30
FLOOR = -1e28


def when(condition, action):
    if isinstance(condition, bool):
        if condition:
            action()
    else:
        pl.when(condition)(action)


def both(first, second):
    if isinstance(first, bool):
        return first and second
    return jnp.logical_and(first, second)


def sine_cosine(angle):
    turns = jnp.floor(angle * np.float32(1.0 / (2.0 * math.pi)) + 0.5)
    high = 6.28125
    middle = float(np.float32(0.0019350051879882812))
    low = 2.0 * math.pi - high - middle
    r = angle - turns * np.float32(high)
    r = r - turns * np.float32(middle)
    r = r - turns * np.float32(low)
    square = r * r
    sine = jnp.full_like(r, 1.0 / math.factorial(17))
    for n in (15, 13, 11, 9, 7, 5, 3, 1):
        sign = -1.0 if (n // 2) % 2 else 1.0
        sine = sine * square + sign / math.factorial(n)
    cosine = jnp.full_like(r, 1.0 / math.factorial(16))
    for n in (14, 12, 10, 8, 6, 4, 2, 0):
        sign = -1.0 if (n // 2) % 2 else 1.0
        cosine = cosine * square + sign / math.factorial(n)
    return sine * r, cosine


def kernel(
    shape,
    length_ref,
    places_ref,
    frequency_ref,
    gain_ref,
    hidden_hbm,
    q_nope_hbm,
    q_rope_hbm,
    w_latent_hbm,
    w_krope_hbm,
    w_uk_hbm,
    w_uv_hbm,
    pre_lat_hbm,
    pre_rope_hbm,
    out_ref,
    cache_lat_ref,
    cache_rope_ref,
    cache_scale_ref,
    hidden,
    q_nope,
    q_rope,
    w_latent,
    w_krope,
    w_uk,
    w_uv,
    pre_lat,
    pre_rope,
    partial,
    partner_part,
    chip_sum,
    group_part,
    fresh,
    prefix,
    marks,
    blocks,
    queries,
    total,
    top,
    weight_sum,
    flat_rope,
    in_sem,
    ra_send,
    ra_recv,
    rb_send,
    rb_recv,
    own_send,
    own_recv,
    twin_send,
    twin_recv,
    z_send,
    z_recv,
    x_send,
    x_recv,
    d_send,
    d_recv,
    y_send,
    y_recv,
    yd_send,
    yd_recv,
):
    n_rep, n_x, n_hi, n_lo = shape
    n_z = n_hi * n_lo
    half = n_z // 2
    heads, nope, lat = w_uk.shape
    rope = pre_rope.shape[1]
    width = prefix.shape[-1]
    value = w_uv.shape[2]
    tok = hidden.shape[0]

    replica = lax.axis_index("replica")
    context = lax.axis_index("context")
    tensor = lax.axis_index("tensor")
    x = lax.div(context, n_hi)
    z_hi = lax.rem(context, n_hi)
    z_lo = lax.div(tensor, 2)
    core = lax.rem(tensor, 2)
    other = 1 - core
    z = z_hi * n_lo + z_lo
    sign = 1 - 2 * core

    def z_place(step):
        return lax.rem(z + step + n_z, n_z)

    def z_plus(step):
        place = z_place(step)
        return {
            "context": x * n_hi + lax.div(place, n_lo),
            "tensor": lax.rem(place, n_lo) * 2 + core,
        }

    def x_place(step):
        return lax.rem(x + step + n_x, n_x)

    def x_plus(step, who=core):
        return {"context": x_place(step) * n_hi + z_hi, "tensor": z_lo * 2 + who}

    def r_plus(step):
        return lax.rem(replica + step, n_rep)

    def group(step):
        return lax.rem(z_lo + step + n_lo, n_lo)

    partner = {"tensor": z_lo * 2 + other}

    peers = [partner, z_plus(1), z_plus(-1)]
    peers += [x_plus(d, who) for d in range(1, n_x) for who in (core, other)]
    peers += [{"tensor": group(d) * 2 + core} for d in range(1, n_lo)]
    peers += [{"replica": r_plus(d)} for d in range(1, n_rep)]
    barrier = pltpu.get_barrier_semaphore()
    for peer in peers:
        pl.semaphore_signal(barrier, inc=1, device_id=peer, device_id_type=MESH)

    own_pre = pl.multiple_of(z_lo * PIECE, PIECE)
    depth = hidden.shape[1]
    cuts = range(0, depth, 128)
    loads = {
        "prefix": [
            (pre_lat_hbm.at[pl.ds(own_pre, PIECE)], pre_lat),
            (pre_rope_hbm.at[pl.ds(own_pre, PIECE)], pre_rope),
        ],
        "hidden": [(hidden_hbm, hidden), (w_krope_hbm, w_krope)]
        + [
            (w_latent_hbm.at[pl.ds(first, 128)], w_latent.at[pl.ds(first, 128)])
            for first in cuts
        ],
        "query": [(q_nope_hbm, q_nope), (q_rope_hbm, q_rope)]
        + [(w_uk_hbm.at[head], w_uk.at[head]) for head in range(heads)],
        "value": [(w_uv_hbm.at[head], w_uv.at[head]) for head in range(heads)],
    }
    number = 0
    for name, pairs in loads.items():
        copies = []
        for source, target in pairs:
            copies.append(pltpu.make_async_copy(source, target, in_sem.at[number]))
            number += 1
        loads[name] = copies
    for name in ("hidden", "prefix", "query", "value"):
        for load in loads[name]:
            load.start()

    def loaded(name):
        for load in loads[name]:
            load.wait()

    def send(source, target, send_sem, recv_sem, device):
        return pltpu.make_async_remote_copy(
            src_ref=source,
            dst_ref=target,
            send_sem=send_sem,
            recv_sem=recv_sem,
            device_id=device,
            device_id_type=MESH,
        )

    def same(ref, send_sem, recv_sem, device):
        return send(ref, ref, send_sem, recv_sem, device)

    def ra_copy():
        return send(partial.at[other], partner_part, ra_send, ra_recv, partner)

    def rb_copy(d):
        to = lax.rem(z_lo + d, n_lo)
        return send(
            chip_sum.at[to],
            group_part.at[d - 1],
            rb_send.at[d - 1],
            rb_recv.at[d - 1],
            {"tensor": to * 2 + core},
        )

    def slots_of(flow):
        return fresh if flow else prefix

    def own_copies(flow):
        copies = []
        piece = fresh.at[z, x, core] if flow else prefix.at[z, x]
        for d in range(1, n_x):
            for i, who in enumerate((core, other) if flow else (core,)):
                copies.append(
                    same(
                        piece,
                        own_send.at[flow, d - 1, i],
                        own_recv.at[flow, d - 1, core],
                        x_plus(d, who),
                    )
                )
        return copies

    def own_arrival(flow, d, who):
        place = x_place(-d)
        piece = fresh.at[z, place, who] if flow else prefix.at[z, place]
        return same(piece, own_send.at[flow, d - 1, 0], own_recv.at[flow, d - 1, who], partner)

    def own_arrived(flow, d):
        own_arrival(flow, d, core).wait_recv()
        if flow:
            own_arrival(flow, d, other).wait_recv()

    def twin_copy():
        return same(fresh.at[z, x, core], twin_send, twin_recv, partner)

    def twin_arrival():
        return same(fresh.at[z, x, other], twin_send, twin_recv, partner)

    def z_copy(flow, s, i):
        return same(
            slots_of(flow).at[z_place(-sign * (s - 1)), x_place(2 * i)],
            z_send.at[flow, s, i],
            z_recv.at[flow, s, i],
            z_plus(sign),
        )

    def z_arrival(flow, s, i):
        return same(
            slots_of(flow).at[z_place(-sign * s), x_place(2 * i)],
            z_send.at[flow, s, i],
            z_recv.at[flow, s, i],
            partner,
        )

    def x_copy(flow, s, i):
        return same(
            slots_of(flow).at[z_place(-sign * s), x],
            x_send.at[flow, s, i],
            x_recv.at[flow, s, i],
            x_plus(1 - 2 * i),
        )

    def x_arrival(flow, s, i):
        return same(
            slots_of(flow).at[z_place(-sign * s), x_place(2 * i - 1)],
            x_send.at[flow, s, i],
            x_recv.at[flow, s, i],
            partner,
        )

    def d_copy(flow, s):
        return same(
            slots_of(flow).at[z_place(-sign * s)], d_send.at[flow, s], d_recv.at[flow, s], partner
        )

    def d_arrival(flow, s):
        return same(
            slots_of(flow).at[z_place(sign * s)], d_send.at[flow, s], d_recv.at[flow, s], partner
        )

    def come(flow, s):
        z_arrival(flow, s, 0).wait_recv()
        when(s < half, lambda: z_copy(flow, s + 1, 0).start())
        for i in range(2):
            x_copy(flow, s, i).start()
        z_arrival(flow, s, 1).wait_recv()
        when(s < half, lambda: z_copy(flow, s + 1, 1).start())

    def cross(flow, s):
        for i in range(2):
            x_arrival(flow, s, i).wait_recv()
        when(s < half, lambda: d_copy(flow, s).start())

    def stage(flow, s):
        when(s <= half, lambda: come(flow, s))
        when(both(s >= 2, s <= half + 1), lambda: cross(flow, s - 1))
        when(both(s >= 3, s <= half + 1), lambda: d_arrival(flow, s - 2).wait_recv())

    def y_copy(d):
        return send(
            fresh.at[pl.ds(z_hi * n_lo, n_lo), x, core],
            blocks.at[core, pl.ds(replica * n_lo, n_lo)],
            y_send.at[d - 1],
            y_recv.at[d - 1],
            {"replica": r_plus(d)},
        )

    def y_arrival(d):
        return send(
            fresh.at[pl.ds(z_hi * n_lo, n_lo), x, core],
            blocks.at[core, pl.ds(r_plus(n_rep - d) * n_lo, n_lo)],
            y_send.at[d - 1],
            y_recv.at[d - 1],
            partner,
        )

    def yd_copy():
        return same(blocks.at[core], yd_send, yd_recv, partner)

    def yd_arrival():
        return same(blocks.at[other], yd_send, yd_recv, partner)

    loaded("hidden")
    lat_term = jnp.dot(hidden[...], w_latent[...], preferred_element_type=jnp.float32)
    rope_term = lax.dot_general(
        hidden[...], w_krope[...], (((1,), (1,)), ((), ())), preferred_element_type=jnp.float32
    )
    rope_term = jnp.concatenate(
        [rope_term, jnp.zeros((tok, width - lat - rope), jnp.float32)], axis=1
    )
    for place in range(n_lo):
        for who in range(2):
            first = (place * 2 + who) * PIECE
            partial[who, place, :, :lat] = lat_term[first : first + PIECE]
            partial[who, place, :, lat:] = rope_term[first : first + PIECE]
    loaded("prefix")
    prefix[z, x, :, :lat] = pre_lat[...]
    length = length_ref[0]
    n_context = n_x * n_hi
    piece_row = lax.broadcasted_iota(jnp.int32, (PIECE, width - lat), 0)
    piece_lanes = lax.broadcasted_iota(jnp.int32, (PIECE, width - lat), 1)
    pre_place = context * (n_lo * PIECE) + z_lo * PIECE + piece_row
    hidden_key = jnp.logical_and(piece_lanes == rope + n_context, pre_place >= length)
    pre_tail = jnp.concatenate(
        [
            pre_rope[...].astype(jnp.float32),
            jnp.zeros((PIECE, width - lat - rope), jnp.float32),
        ],
        axis=1,
    )
    prefix[z, x, :, lat:] = jnp.where(hidden_key, MASKED, pre_tail).astype(
        jnp.bfloat16
    )

    pl.semaphore_wait(barrier, len(peers))
    ra_copy().start()
    z_copy(0, 1, 0).start()
    for copy in own_copies(0):
        copy.start()

    loaded("query")
    lanes = lax.broadcasted_iota(jnp.int32, (tok, width - lat), 1)
    later = jnp.logical_and(lanes > rope + context, lanes < rope + n_context)
    masks = jnp.where(later, MASKED, jnp.where(lanes == rope + n_context, 1.0, 0.0))
    query_row = lax.broadcasted_iota(jnp.int32, (tok, tok), 0)
    key_lane = lax.broadcasted_iota(jnp.int32, (tok, tok), 1)
    triangle = jnp.where(key_lane > query_row, MASKED, 0.0).astype(jnp.bfloat16)
    marks[...] = jnp.zeros_like(marks)
    mark_row = lax.broadcasted_iota(jnp.int32, (PIECE, tok), 0)
    mark_lane = lax.broadcasted_iota(jnp.int32, (PIECE, tok), 1)
    for place in range(n_lo):
        for who in range(2):
            first = (place * 2 + who) * PIECE
            marks[z_hi * n_lo + place, x, who] = jnp.where(
                mark_lane == first + mark_row, 1.0, 0.0
            ).astype(jnp.bfloat16)

    def absorb(first, last):
        for head in range(first, last):
            rows = pl.ds(head * tok, tok)
            queries[rows, :lat] = jnp.dot(
                q_nope[:, head * nope : (head + 1) * nope],
                w_uk[head],
                preferred_element_type=jnp.float32,
            ).astype(jnp.bfloat16)
            pair = q_rope[:, (head // 2) * 2 * rope : (head // 2 + 1) * 2 * rope]
            pair = pair.astype(jnp.float32)
            if head % 2:
                pair = pltpu.roll(pair, rope, 1)
            queries[rows, lat:width] = jnp.where(lanes < rope, pair, masks).astype(jnp.bfloat16)
            queries[rows, width:] = triangle

    absorb(0, heads // 2)

    ra_copy().wait_recv()
    chip_sum[...] = partial[core] + partner_part[...]
    for d in range(1, n_lo):
        rb_copy(d).start()

    own_arrived(0, 2)
    z_copy(0, 1, 1).start()
    absorb(heads // 2, heads)

    position = (
        length
        + context * tok
        + tensor * PIECE
        + piece_row
    )
    sine, cosine = sine_cosine(position.astype(jnp.float32) * frequency_ref[...])
    sine = jnp.where(piece_lanes < rope // 2, -sine, sine)
    sine = jnp.where(piece_lanes < rope, sine, 0.0)

    top[...] = jnp.full_like(top, FLOOR)
    weight_sum[...] = jnp.zeros_like(weight_sum)
    total[...] = jnp.zeros_like(total)

    stage(0, 1)
    for d in range(1, n_lo):
        rb_copy(d).wait_recv()
    summed = chip_sum[z_lo]
    for d in range(1, n_lo):
        summed = summed + group_part[d - 1]
    lat_sum = summed[:, :lat]
    mean_square = jnp.mean(lat_sum * lat_sum, axis=1, keepdims=True)
    fresh[z, x, core, :, :lat] = (
        lat_sum * lax.rsqrt(mean_square + NORM_EPS) * gain_ref[...]
    ).astype(jnp.bfloat16)
    rope_sum = summed[:, lat:]
    swapped = jnp.where(
        piece_lanes < rope // 2,
        pltpu.roll(rope_sum, width - lat - rope // 2, 1),
        pltpu.roll(rope_sum, rope // 2, 1),
    )
    new_tail = rope_sum * cosine + swapped * sine
    fresh[z, x, core, :, lat:] = jnp.where(
        piece_lanes == rope + context, 1.0, new_tail
    ).astype(jnp.bfloat16)

    twin_copy().start()
    for copy in own_copies(1):
        copy.start()
    stage(0, 2)
    twin_arrival().wait_recv()
    z_copy(1, 1, 0).start()
    own_arrived(1, 2)
    z_copy(1, 1, 1).start()
    for d in (1, 3):
        own_arrived(0, d)
    stage(0, 3)

    score_scale = float((nope + rope) ** (-0.5) * math.log2(math.e))

    def new_keys(place):
        count = 2 * n_x * PIECE
        return jnp.concatenate(
            [fresh[place].reshape(count, width), marks[place].reshape(count, tok)], axis=1
        )

    def prefix_keys(place):
        return prefix[place].reshape(n_x * PIECE, width)

    def attend(parts):
        key_rows = jnp.concatenate(parts, axis=0)
        tiles, depth = key_rows.shape[0] // 128, key_rows.shape[1]
        at_once = min(ROWS, heads * tok)
        for first in range(0, heads * tok, at_once):
            rows = pl.ds(first, at_once)
            scores = lax.dot_general(
                queries[rows, :depth],
                key_rows,
                (((1,), (1,)), ((), ())),
                preferred_element_type=jnp.float32,
            )
            scores = scores * score_scale
            old_top = top[rows, :]
            new_top = jnp.maximum(old_top, jnp.max(scores, axis=1, keepdims=True))
            top[rows, :] = new_top
            rescale = jnp.exp2(old_top - new_top)
            exponents = [
                jnp.exp2(scores[:, i * 128 : (i + 1) * 128] - new_top) for i in range(tiles)
            ]
            weight_sum[rows, :] = weight_sum[rows, :] * rescale + sum(exponents)
            weights = jnp.concatenate([e.astype(jnp.bfloat16) for e in exponents], axis=1)
            total[rows, :] = total[rows, :] * jnp.concatenate(
                [rescale] * (lat // 128), axis=1
            ) + jnp.dot(weights, key_rows[:, :lat], preferred_element_type=jnp.float32)


    def to_owners():
        for d in range(1, n_rep):
            y_copy(d).start()
        for place in range(n_lo):
            blocks[core, replica * n_lo + place] = fresh[z_hi * n_lo + place, x, core]

    def owners():
        for d in range(1, n_rep):
            y_arrival(d).wait_recv()
        yd_copy().start()

    def own_slot():
        for d in (1, 3):
            own_arrived(1, d)

    def iteration(s, carry):
        stage(1, s)
        stage(0, s + 3)
        pl.when(s == 2)(own_slot)
        pl.when(s == n_lo + 1)(to_owners)
        pl.when(s == half + 1)(owners)

        def attend_prefix():
            last = jnp.where(s + 1 == half, z, z_place(-s - 1))
            attend([prefix_keys(place) for place in (z_place(s), z_place(-s), z_place(s + 1), last)])

        pl.when(both(lax.rem(s, 2) == 1, s < half))(attend_prefix)
        pl.when(s >= 3)(
            lambda: attend(
                [
                    new_keys(z_place(s - 2)),
                    new_keys(jnp.where(s == half + 2, z, z_place(2 - s))),
                ]
            )
        )
        return carry

    lax.fori_loop(1, half + 3, iteration, 0)

    loaded("value")
    for head in range(heads):
        rows = pl.ds(head * tok, tok)
        row_sum = jnp.sum(weight_sum[rows, :], axis=1, keepdims=True)
        latent_out = (total[rows, :] / row_sum).astype(jnp.bfloat16)
        out_ref[:, head * value : (head + 1) * value] = jnp.dot(
            latent_out, w_uv[head], preferred_element_type=jnp.float32
        ).astype(jnp.bfloat16)

    yd_arrival().wait_recv()
    tile = lat // TILES
    per_block = BLOCK // (2 * PIECE)
    flat_scales = []
    scale_row = lax.broadcasted_iota(jnp.int32, (BLOCK, BLOCK * TILES), 0)
    scale_lane = lax.broadcasted_iota(jnp.int32, (BLOCK, BLOCK * TILES), 1)
    rope_lane = lax.broadcasted_iota(jnp.int32, (BLOCK, 2 * rope), 1)
    for slot in range(2):
        source = jnp.int32(0)
        for candidate in range(n_rep * 2):
            source = jnp.where(
                places_ref[0, candidate] == replica * 2 + slot, candidate, source
            )
        rows = jnp.concatenate(
            [
                blocks[who, source * per_block + place]
                for place in range(per_block)
                for who in range(2)
            ],
            axis=0,
        ).astype(jnp.float32)
        flat = jnp.zeros((BLOCK, BLOCK * TILES), jnp.float32)
        held = pl.ds(slot * BLOCK, BLOCK)
        for i in range(TILES):
            entries = rows[:, i * tile : (i + 1) * tile]
            scale = jnp.max(jnp.abs(entries), axis=1, keepdims=True) + SCALE_EPS
            scale = scale.astype(jnp.bfloat16).astype(jnp.float32)
            cache_lat_ref[slot, :, i * tile : (i + 1) * tile] = (entries / scale).astype(
                jnp.bfloat16
            )
            flat = jnp.where(scale_lane == scale_row * TILES + i, scale, flat)
        flat_scales.append(jnp.sum(flat, axis=0, keepdims=True))
        tail = rows[:, lat : lat + 2 * rope]
        following = pltpu.roll(pltpu.roll(tail, BLOCK - 1, 0), rope, 1)
        flat_rope[held, :] = jnp.where(rope_lane < rope, tail, following)
    for j in range(BLOCK // 2):
        cache_rope_ref[:, j * 2 * rope : (j + 1) * 2 * rope] = flat_rope[
            pl.ds(2 * j, 2, stride=BLOCK), :
        ].astype(jnp.bfloat16)
    cache_scale_ref[...] = jnp.concatenate(flat_scales, axis=0).astype(jnp.bfloat16)

    ra_copy().wait_send()
    for d in range(1, n_lo):
        rb_copy(d).wait_send()
    for d in range(1, n_rep):
        y_copy(d).wait_send()
    yd_copy().wait_send()

    twin_copy().wait_send()
    for flow in range(2):
        for copy in own_copies(flow):
            copy.wait_send()

    def sent(s, carry):
        for flow in range(2):
            for i in range(2):
                z_copy(flow, s, i).wait_send()
                x_copy(flow, s, i).wait_send()
            pl.when(s < half)(lambda: d_copy(flow, s).wait_send())
        return carry

    lax.fori_loop(1, half + 1, sent, 0)


def per_device(
    shape,
    hidden,
    q_nope,
    q_rope,
    w_latent,
    w_krope,
    kv_gain,
    w_uk,
    w_uv,
    prefix_latent,
    prefix_rope,
    prefix_lengths,
    placements,
):
    n_rep, n_x, n_hi, n_lo = shape
    n_z = n_hi * n_lo
    half = n_z // 2
    tok, depth = hidden.shape[1:]
    heads, nope, lat = w_uk.shape
    rope = w_krope.shape[1]
    value = w_uv.shape[2]
    width = -(-(lat + rope) // 128) * 128
    count = rope // 2
    powers = -(np.arange(count, dtype=np.float32) * np.float32(2.0)) / np.float32(rope)
    frequency = np.power(np.float64(ROPE_THETA), powers.astype(np.float64))
    frequency = np.resize(frequency, (1, width - lat)).astype(np.float32)
    vmem = pl.BlockSpec(memory_space=pltpu.VMEM)
    smem = pl.BlockSpec(memory_space=pltpu.SMEM)
    anywhere = pl.BlockSpec(memory_space=pl.ANY)
    bf16, f32 = jnp.bfloat16, jnp.float32
    dma = pltpu.SemaphoreType.DMA
    out = pl.pallas_call(
        functools.partial(kernel, shape),
        out_shape=(
            jax.ShapeDtypeStruct((tok, heads * value), bf16),
            jax.ShapeDtypeStruct((2, BLOCK, lat), bf16),
            jax.ShapeDtypeStruct((2, BLOCK * rope), bf16),
            jax.ShapeDtypeStruct((2, BLOCK * TILES), bf16),
        ),
        in_specs=[smem, smem, vmem, vmem] + [anywhere] * 9,
        out_specs=(vmem, vmem, vmem, vmem),
        scratch_shapes=[
            pltpu.VMEM((tok, depth), bf16),
            pltpu.VMEM((tok, heads * nope), bf16),
            pltpu.VMEM((tok, heads * rope), bf16),
            pltpu.VMEM((depth, lat), bf16),
            pltpu.VMEM((rope, depth), bf16),
            pltpu.VMEM((heads, nope, lat), bf16),
            pltpu.VMEM((heads, lat, value), bf16),
            pltpu.VMEM((PIECE, lat), bf16),
            pltpu.VMEM((PIECE, rope), bf16),
            pltpu.VMEM((2, n_lo, PIECE, width), f32),
            pltpu.VMEM((n_lo, PIECE, width), f32),
            pltpu.VMEM((n_lo, PIECE, width), f32),
            pltpu.VMEM((max(n_lo - 1, 1), PIECE, width), f32),
            pltpu.VMEM((n_z, n_x, 2, PIECE, width), bf16),
            pltpu.VMEM((n_z, n_x, PIECE, width), bf16),
            pltpu.VMEM((n_z, n_x, 2, PIECE, tok), bf16),
            pltpu.VMEM((2, n_rep * n_lo, PIECE, width), bf16),
            pltpu.VMEM((heads * tok, width + tok), bf16),
            pltpu.VMEM((heads * tok, lat), f32),
            pltpu.VMEM((heads * tok, 128), f32),
            pltpu.VMEM((heads * tok, 128), f32),
            pltpu.VMEM((2 * BLOCK, 2 * rope), f32),
            dma((6 + depth // 128 + 2 * heads,)),
            dma,
            dma,
            dma((max(n_lo - 1, 1),)),
            dma((max(n_lo - 1, 1),)),
            dma((2, n_x - 1, 2)),
            dma((2, n_x - 1, 2)),
            dma,
            dma,
            dma((2, half + 1, 2)),
            dma((2, half + 1, 2)),
            dma((2, half + 1, 2)),
            dma((2, half + 1, 2)),
            dma((2, half + 1)),
            dma((2, half + 1)),
            dma((max(n_rep - 1, 1),)),
            dma((max(n_rep - 1, 1),)),
            dma,
            dma,
        ],
        compiler_params=pltpu.CompilerParams(
            collective_id=0, has_side_effects=True, vmem_limit_bytes=56 * 1024 * 1024
        ),
    )(
        prefix_lengths,
        placements,
        jnp.asarray(frequency),
        kv_gain.reshape(1, lat),
        hidden[0],
        q_nope[0],
        q_rope[0],
        w_latent,
        w_krope.T,
        w_uk,
        w_uv,
        prefix_latent[0],
        prefix_rope[0],
    )
    return tuple(result.reshape(1, result.shape[0], -1) for result in out)


def program(mesh, shape):
    return jax.shard_map(
        functools.partial(per_device, shape),
        mesh=mesh,
        in_specs=(
            P("replica", "context", "tensor"),
            P("replica", "context", "tensor"),
            P("replica", "context", "tensor"),
            P("tensor", None),
            P("tensor", None),
            P(),
            P("tensor", None, None),
            P("tensor", None, None),
            P("replica", "context", None),
            P("replica", "context", None),
            P("replica"),
            P("context", None),
        ),
        out_specs=(
            P("replica", "context", "tensor"),
            P("replica", "context", None),
            P("replica", "context", None),
            P("replica", "context", None),
        ),
        check_vma=False,
    )


def solution(mesh):
    n_hi = 4
    return program(
        mesh,
        (
            mesh.shape["replica"],
            mesh.shape["context"] // n_hi,
            n_hi,
            mesh.shape["tensor"] // 2,
        ),
    )
```

```python
import functools
import math

import jax
import jax.numpy as jnp
import numpy as np
from jax import lax
from jax.experimental import pallas as pl
from jax.experimental.pallas import tpu as pltpu
from jax.sharding import PartitionSpec as P

MESH = pl.DeviceIdType.MESH
BLOCK = 64
TILES = 4
PIECE = 16
ROWS = 256
ROPE_THETA = 50000.0
NORM_EPS = 1e-06
SCALE_EPS = 1e-06
MASKED = -1e30
FLOOR = -1e28


def when(condition, action):
    if isinstance(condition, bool):
        if condition:
            action()
    else:
        pl.when(condition)(action)


def both(first, second):
    if isinstance(first, bool):
        return first and second
    return jnp.logical_and(first, second)


def sine_cosine(angle):
    turns = jnp.floor(angle * np.float32(1.0 / (2.0 * math.pi)) + 0.5)
    high = 6.28125
    middle = float(np.float32(0.0019350051879882812))
    low = 2.0 * math.pi - high - middle
    r = angle - turns * np.float32(high)
    r = r - turns * np.float32(middle)
    r = r - turns * np.float32(low)
    square = r * r
    sine = jnp.full_like(r, 1.0 / math.factorial(17))
    for n in (15, 13, 11, 9, 7, 5, 3, 1):
        sign = -1.0 if (n // 2) % 2 else 1.0
        sine = sine * square + sign / math.factorial(n)
    cosine = jnp.full_like(r, 1.0 / math.factorial(16))
    for n in (14, 12, 10, 8, 6, 4, 2, 0):
        sign = -1.0 if (n // 2) % 2 else 1.0
        cosine = cosine * square + sign / math.factorial(n)
    return sine * r, cosine


def kernel(
    shape,
    length_ref,
    places_ref,
    frequency_ref,
    gain_ref,
    hidden_hbm,
    q_nope_hbm,
    q_rope_hbm,
    w_latent_hbm,
    w_krope_hbm,
    w_uk_hbm,
    w_uv_hbm,
    pre_lat_hbm,
    pre_rope_hbm,
    out_ref,
    cache_lat_ref,
    cache_rope_ref,
    cache_scale_ref,
    hidden,
    q_nope,
    q_rope,
    w_latent,
    w_krope,
    w_uk,
    w_uv,
    pre_lat,
    pre_rope,
    partial,
    partner_part,
    chip_sum,
    group_part,
    fresh,
    prefix,
    marks,
    blocks,
    queries,
    total,
    top,
    weight_sum,
    flat_rope,
    in_sem,
    ra_send,
    ra_recv,
    rb_send,
    rb_recv,
    own_send,
    own_recv,
    twin_send,
    twin_recv,
    z_send,
    z_recv,
    x_send,
    x_recv,
    d_send,
    d_recv,
    y_send,
    y_recv,
):
    n_rep, n_x, n_hi, n_lo = shape
    n_z = n_hi * n_lo
    half = n_z // 2
    heads, nope, lat = w_uk.shape
    rope = pre_rope.shape[1]
    width = prefix.shape[-1]
    value = w_uv.shape[2]
    tok = hidden.shape[0]

    replica = lax.axis_index("replica")
    context = lax.axis_index("context")
    tensor = lax.axis_index("tensor")
    x = lax.div(context, n_hi)
    z_hi = lax.rem(context, n_hi)
    z_lo = lax.div(tensor, 2)
    core = lax.rem(tensor, 2)
    other = 1 - core
    z = z_hi * n_lo + z_lo
    sign = 1 - 2 * core

    def z_place(step):
        return lax.rem(z + step + n_z, n_z)

    def z_plus(step):
        place = z_place(step)
        return {
            "context": x * n_hi + lax.div(place, n_lo),
            "tensor": lax.rem(place, n_lo) * 2 + core,
        }

    def x_place(step):
        return lax.rem(x + step + n_x, n_x)

    def x_plus(step, who=core):
        return {"context": x_place(step) * n_hi + z_hi, "tensor": z_lo * 2 + who}

    def r_plus(step):
        return lax.rem(replica + step, n_rep)

    def group(step):
        return lax.rem(z_lo + step + n_lo, n_lo)

    partner = {"tensor": z_lo * 2 + other}

    peers = [partner, z_plus(1), z_plus(-1)]
    peers += [x_plus(d, who) for d in range(1, n_x) for who in (core, other)]
    peers += [{"tensor": group(d) * 2 + core} for d in range(1, n_lo)]
    peers += [
        {"replica": r_plus(d), "tensor": z_lo * 2 + who}
        for d in range(1, n_rep)
        for who in (core, other)
    ]
    barrier = pltpu.get_barrier_semaphore()
    for peer in peers:
        pl.semaphore_signal(barrier, inc=1, device_id=peer, device_id_type=MESH)

    own_pre = pl.multiple_of(z_lo * PIECE, PIECE)
    depth = hidden.shape[1]
    cuts = range(0, depth, 128)
    loads = {
        "prefix": [
            (pre_lat_hbm.at[pl.ds(own_pre, PIECE)], pre_lat),
            (pre_rope_hbm.at[pl.ds(own_pre, PIECE)], pre_rope),
        ],
        "hidden": [(hidden_hbm, hidden), (w_krope_hbm, w_krope)]
        + [
            (w_latent_hbm.at[pl.ds(first, 128)], w_latent.at[pl.ds(first, 128)])
            for first in cuts
        ],
        "query": [(q_nope_hbm, q_nope), (q_rope_hbm, q_rope)]
        + [(w_uk_hbm.at[head], w_uk.at[head]) for head in range(heads)],
        "value": [(w_uv_hbm.at[head], w_uv.at[head]) for head in range(heads)],
    }
    number = 0
    for name, pairs in loads.items():
        copies = []
        for source, target in pairs:
            copies.append(pltpu.make_async_copy(source, target, in_sem.at[number]))
            number += 1
        loads[name] = copies
    for name in ("hidden", "prefix", "query", "value"):
        for load in loads[name]:
            load.start()

    def loaded(name):
        for load in loads[name]:
            load.wait()

    def send(source, target, send_sem, recv_sem, device):
        return pltpu.make_async_remote_copy(
            src_ref=source,
            dst_ref=target,
            send_sem=send_sem,
            recv_sem=recv_sem,
            device_id=device,
            device_id_type=MESH,
        )

    def same(ref, send_sem, recv_sem, device):
        return send(ref, ref, send_sem, recv_sem, device)

    def ra_copy():
        return send(partial.at[other], partner_part, ra_send, ra_recv, partner)

    def rb_copy(d):
        to = lax.rem(z_lo + d, n_lo)
        return send(
            chip_sum.at[to],
            group_part.at[d - 1],
            rb_send.at[d - 1],
            rb_recv.at[d - 1],
            {"tensor": to * 2 + core},
        )

    def slots_of(flow):
        return fresh if flow else prefix

    def own_copies(flow):
        copies = []
        piece = fresh.at[z, x, core] if flow else prefix.at[z, x]
        for d in range(1, n_x):
            for i, who in enumerate((core, other) if flow else (core,)):
                copies.append(
                    same(
                        piece,
                        own_send.at[flow, d - 1, i],
                        own_recv.at[flow, d - 1, core],
                        x_plus(d, who),
                    )
                )
        return copies

    def own_arrival(flow, d, who):
        place = x_place(-d)
        piece = fresh.at[z, place, who] if flow else prefix.at[z, place]
        return same(piece, own_send.at[flow, d - 1, 0], own_recv.at[flow, d - 1, who], partner)

    def own_arrived(flow, d):
        own_arrival(flow, d, core).wait_recv()
        if flow:
            own_arrival(flow, d, other).wait_recv()

    def twin_copy():
        return same(fresh.at[z, x, core], twin_send, twin_recv, partner)

    def twin_arrival():
        return same(fresh.at[z, x, other], twin_send, twin_recv, partner)

    def z_copy(flow, s, i):
        return same(
            slots_of(flow).at[z_place(-sign * (s - 1)), x_place(2 * i)],
            z_send.at[flow, s, i],
            z_recv.at[flow, s, i],
            z_plus(sign),
        )

    def z_arrival(flow, s, i):
        return same(
            slots_of(flow).at[z_place(-sign * s), x_place(2 * i)],
            z_send.at[flow, s, i],
            z_recv.at[flow, s, i],
            partner,
        )

    def x_copy(flow, s, i, who):
        return same(
            slots_of(flow).at[z_place(-sign * s), x],
            x_send.at[flow, s, i, who],
            x_recv.at[flow, s, i, core],
            x_plus(1 - 2 * i, who),
        )

    def x_arrival(flow, s, i, who):
        return same(
            slots_of(flow).at[z_place((2 * who - 1) * s), x_place(2 * i - 1)],
            x_send.at[flow, s, i, who],
            x_recv.at[flow, s, i, who],
            partner,
        )

    def d_copy(flow, s, i):
        return same(
            slots_of(flow).at[z_place(-sign * s), x_place(2 * i)],
            d_send.at[flow, s, i],
            d_recv.at[flow, s, i],
            partner,
        )

    def d_arrival(flow, s, i):
        return same(
            slots_of(flow).at[z_place(sign * s), x_place(2 * i)],
            d_send.at[flow, s, i],
            d_recv.at[flow, s, i],
            partner,
        )

    def come(flow, s):
        def to_other_cores():
            for i in range(2):
                x_copy(flow, s, i, other).start()
            d_copy(flow, s, 0).start()

        z_arrival(flow, s, 0).wait_recv()
        when(s < half, lambda: z_copy(flow, s + 1, 0).start())
        for i in range(2):
            x_copy(flow, s, i, core).start()
        when(s < half, to_other_cores)
        z_arrival(flow, s, 1).wait_recv()
        when(s < half, lambda: z_copy(flow, s + 1, 1).start())
        when(s < half, lambda: d_copy(flow, s, 1).start())

    def settle(flow, s):
        for i in range(2):
            x_arrival(flow, s, i, core).wait_recv()

        def from_other_cores():
            for i in range(2):
                x_arrival(flow, s, i, other).wait_recv()
                d_arrival(flow, s, i).wait_recv()

        when(s < half, from_other_cores)

    def stage(flow, s):
        when(s <= half, lambda: come(flow, s))
        when(both(s >= 2, s <= half + 1), lambda: settle(flow, s - 1))

    def y_copy(d, who):
        return send(
            fresh.at[pl.ds(z_hi * n_lo, n_lo), x, core],
            blocks.at[core, pl.ds(replica * n_lo, n_lo)],
            y_send.at[d - 1, who],
            y_recv.at[d - 1, core],
            {"replica": r_plus(d), "tensor": z_lo * 2 + who},
        )

    def y_arrival(d, who):
        return send(
            fresh.at[pl.ds(z_hi * n_lo, n_lo), x, core],
            blocks.at[who, pl.ds(r_plus(n_rep - d) * n_lo, n_lo)],
            y_send.at[d - 1, who],
            y_recv.at[d - 1, who],
            partner,
        )

    loaded("hidden")
    lat_term = jnp.dot(hidden[...], w_latent[...], preferred_element_type=jnp.float32)
    rope_term = lax.dot_general(
        hidden[...], w_krope[...], (((1,), (1,)), ((), ())), preferred_element_type=jnp.float32
    )
    rope_term = jnp.concatenate(
        [rope_term, jnp.zeros((tok, width - lat - rope), jnp.float32)], axis=1
    )
    for place in range(n_lo):
        for who in range(2):
            first = (place * 2 + who) * PIECE
            partial[who, place, :, :lat] = lat_term[first : first + PIECE]
            partial[who, place, :, lat:] = rope_term[first : first + PIECE]
    loaded("prefix")
    prefix[z, x, :, :lat] = pre_lat[...]
    length = length_ref[0]
    n_context = n_x * n_hi
    piece_row = lax.broadcasted_iota(jnp.int32, (PIECE, width - lat), 0)
    piece_lanes = lax.broadcasted_iota(jnp.int32, (PIECE, width - lat), 1)
    pre_place = context * (n_lo * PIECE) + z_lo * PIECE + piece_row
    hidden_key = jnp.logical_and(piece_lanes == rope + n_context, pre_place >= length)
    pre_tail = jnp.concatenate(
        [
            pre_rope[...].astype(jnp.float32),
            jnp.zeros((PIECE, width - lat - rope), jnp.float32),
        ],
        axis=1,
    )
    prefix[z, x, :, lat:] = jnp.where(hidden_key, MASKED, pre_tail).astype(
        jnp.bfloat16
    )

    pl.semaphore_wait(barrier, len(peers))
    ra_copy().start()
    z_copy(0, 1, 0).start()
    for copy in own_copies(0):
        copy.start()

    loaded("query")
    lanes = lax.broadcasted_iota(jnp.int32, (tok, width - lat), 1)
    later = jnp.logical_and(lanes > rope + context, lanes < rope + n_context)
    masks = jnp.where(later, MASKED, jnp.where(lanes == rope + n_context, 1.0, 0.0))
    query_row = lax.broadcasted_iota(jnp.int32, (tok, tok), 0)
    key_lane = lax.broadcasted_iota(jnp.int32, (tok, tok), 1)
    triangle = jnp.where(key_lane > query_row, MASKED, 0.0).astype(jnp.bfloat16)
    marks[...] = jnp.zeros_like(marks)
    mark_row = lax.broadcasted_iota(jnp.int32, (PIECE, tok), 0)
    mark_lane = lax.broadcasted_iota(jnp.int32, (PIECE, tok), 1)
    for place in range(n_lo):
        for who in range(2):
            first = (place * 2 + who) * PIECE
            marks[z_hi * n_lo + place, x, who] = jnp.where(
                mark_lane == first + mark_row, 1.0, 0.0
            ).astype(jnp.bfloat16)

    def absorb(first, last):
        for head in range(first, last):
            rows = pl.ds(head * tok, tok)
            queries[rows, :lat] = jnp.dot(
                q_nope[:, head * nope : (head + 1) * nope],
                w_uk[head],
                preferred_element_type=jnp.float32,
            ).astype(jnp.bfloat16)
            pair = q_rope[:, (head // 2) * 2 * rope : (head // 2 + 1) * 2 * rope]
            pair = pair.astype(jnp.float32)
            if head % 2:
                pair = pltpu.roll(pair, rope, 1)
            queries[rows, lat:width] = jnp.where(lanes < rope, pair, masks).astype(jnp.bfloat16)
            queries[rows, width:] = triangle

    absorb(0, heads // 2)

    ra_copy().wait_recv()
    chip_sum[...] = partial[core] + partner_part[...]
    for d in range(1, n_lo):
        rb_copy(d).start()

    own_arrived(0, 2)
    z_copy(0, 1, 1).start()
    absorb(heads // 2, heads)

    position = (
        length
        + context * tok
        + tensor * PIECE
        + piece_row
    )
    sine, cosine = sine_cosine(position.astype(jnp.float32) * frequency_ref[...])
    sine = jnp.where(piece_lanes < rope // 2, -sine, sine)
    sine = jnp.where(piece_lanes < rope, sine, 0.0)

    top[...] = jnp.full_like(top, FLOOR)
    weight_sum[...] = jnp.zeros_like(weight_sum)
    total[...] = jnp.zeros_like(total)

    stage(0, 1)
    for d in range(1, n_lo):
        rb_copy(d).wait_recv()
    summed = chip_sum[z_lo]
    for d in range(1, n_lo):
        summed = summed + group_part[d - 1]
    lat_sum = summed[:, :lat]
    mean_square = jnp.mean(lat_sum * lat_sum, axis=1, keepdims=True)
    fresh[z, x, core, :, :lat] = (
        lat_sum * lax.rsqrt(mean_square + NORM_EPS) * gain_ref[...]
    ).astype(jnp.bfloat16)
    rope_sum = summed[:, lat:]
    swapped = jnp.where(
        piece_lanes < rope // 2,
        pltpu.roll(rope_sum, width - lat - rope // 2, 1),
        pltpu.roll(rope_sum, rope // 2, 1),
    )
    new_tail = rope_sum * cosine + swapped * sine
    fresh[z, x, core, :, lat:] = jnp.where(
        piece_lanes == rope + context, 1.0, new_tail
    ).astype(jnp.bfloat16)

    twin_copy().start()
    for copy in own_copies(1):
        copy.start()
    stage(0, 2)
    twin_arrival().wait_recv()
    z_copy(1, 1, 0).start()
    own_arrived(1, 2)
    z_copy(1, 1, 1).start()
    for d in (1, 3):
        own_arrived(0, d)
    stage(0, 3)

    score_scale = float((nope + rope) ** (-0.5) * math.log2(math.e))

    zeros = jnp.zeros((n_x * PIECE, tok), jnp.bfloat16)

    def attend(slots):
        count = n_x * PIECE
        parts = []
        for place in slots:
            parts.append((fresh[place].reshape(2 * count, width), marks[place].reshape(2 * count, tok)))
            parts.append((prefix[place].reshape(count, width), zeros))
        key_rows = jnp.concatenate(
            [jnp.concatenate(part, axis=1) for part in parts], axis=0
        )
        tiles = len(slots) * 3 * count // 128
        at_once = min(ROWS, heads * tok)
        for first in range(0, heads * tok, at_once):
            rows = pl.ds(first, at_once)
            scores = lax.dot_general(
                queries[rows, :],
                key_rows,
                (((1,), (1,)), ((), ())),
                preferred_element_type=jnp.float32,
            )
            scores = scores * score_scale
            old_top = top[rows, :]
            new_top = jnp.maximum(old_top, jnp.max(scores, axis=1, keepdims=True))
            top[rows, :] = new_top
            rescale = jnp.exp2(old_top - new_top)
            exponents = [
                jnp.exp2(scores[:, i * 128 : (i + 1) * 128] - new_top) for i in range(tiles)
            ]
            weight_sum[rows, :] = weight_sum[rows, :] * rescale + sum(exponents)
            weights = jnp.concatenate([e.astype(jnp.bfloat16) for e in exponents], axis=1)
            total[rows, :] = total[rows, :] * jnp.concatenate(
                [rescale] * (lat // 128), axis=1
            ) + jnp.dot(weights, key_rows[:, :lat], preferred_element_type=jnp.float32)


    def to_owners():
        for d in range(1, n_rep):
            for who in (core, other):
                y_copy(d, who).start()
        for place in range(n_lo):
            for who in range(2):
                blocks[who, replica * n_lo + place] = fresh[z_hi * n_lo + place, x, who]

    def own_slot():
        for d in (1, 3):
            own_arrived(1, d)

    def iteration(s, carry):
        stage(1, s)
        stage(0, s + 3)
        pl.when(s == 2)(own_slot)
        pl.when(s == n_lo)(to_owners)
        pl.when(s >= 2)(
            lambda: attend(
                [z_place(s - 1), jnp.where(s == half + 1, z, z_place(1 - s))]
            )
        )
        return carry

    lax.fori_loop(1, half + 2, iteration, 0)

    loaded("value")
    for head in range(heads):
        rows = pl.ds(head * tok, tok)
        row_sum = jnp.sum(weight_sum[rows, :], axis=1, keepdims=True)
        latent_out = (total[rows, :] / row_sum).astype(jnp.bfloat16)
        out_ref[:, head * value : (head + 1) * value] = jnp.dot(
            latent_out, w_uv[head], preferred_element_type=jnp.float32
        ).astype(jnp.bfloat16)

    for d in range(1, n_rep):
        for who in (core, other):
            y_arrival(d, who).wait_recv()
    tile = lat // TILES
    per_block = BLOCK // (2 * PIECE)
    flat_scales = []
    scale_row = lax.broadcasted_iota(jnp.int32, (BLOCK, BLOCK * TILES), 0)
    scale_lane = lax.broadcasted_iota(jnp.int32, (BLOCK, BLOCK * TILES), 1)
    rope_lane = lax.broadcasted_iota(jnp.int32, (BLOCK, 2 * rope), 1)
    for slot in range(2):
        source = jnp.int32(0)
        for candidate in range(n_rep * 2):
            source = jnp.where(
                places_ref[0, candidate] == replica * 2 + slot, candidate, source
            )
        rows = jnp.concatenate(
            [
                blocks[who, source * per_block + place]
                for place in range(per_block)
                for who in range(2)
            ],
            axis=0,
        ).astype(jnp.float32)
        flat = jnp.zeros((BLOCK, BLOCK * TILES), jnp.float32)
        held = pl.ds(slot * BLOCK, BLOCK)
        for i in range(TILES):
            entries = rows[:, i * tile : (i + 1) * tile]
            scale = jnp.max(jnp.abs(entries), axis=1, keepdims=True) + SCALE_EPS
            scale = scale.astype(jnp.bfloat16).astype(jnp.float32)
            cache_lat_ref[slot, :, i * tile : (i + 1) * tile] = (entries / scale).astype(
                jnp.bfloat16
            )
            flat = jnp.where(scale_lane == scale_row * TILES + i, scale, flat)
        flat_scales.append(jnp.sum(flat, axis=0, keepdims=True))
        tail = rows[:, lat : lat + 2 * rope]
        following = pltpu.roll(pltpu.roll(tail, BLOCK - 1, 0), rope, 1)
        flat_rope[held, :] = jnp.where(rope_lane < rope, tail, following)
    for j in range(BLOCK // 2):
        cache_rope_ref[:, j * 2 * rope : (j + 1) * 2 * rope] = flat_rope[
            pl.ds(2 * j, 2, stride=BLOCK), :
        ].astype(jnp.bfloat16)
    cache_scale_ref[...] = jnp.concatenate(flat_scales, axis=0).astype(jnp.bfloat16)

    ra_copy().wait_send()
    for d in range(1, n_lo):
        rb_copy(d).wait_send()
    for d in range(1, n_rep):
        for who in (core, other):
            y_copy(d, who).wait_send()

    twin_copy().wait_send()
    for flow in range(2):
        for copy in own_copies(flow):
            copy.wait_send()

    def sent(s, carry):
        for flow in range(2):
            for i in range(2):
                z_copy(flow, s, i).wait_send()
                x_copy(flow, s, i, core).wait_send()

            def to_other_cores():
                for i in range(2):
                    x_copy(flow, s, i, other).wait_send()
                    d_copy(flow, s, i).wait_send()

            pl.when(s < half)(to_other_cores)
        return carry

    lax.fori_loop(1, half + 1, sent, 0)


def per_device(
    shape,
    hidden,
    q_nope,
    q_rope,
    w_latent,
    w_krope,
    kv_gain,
    w_uk,
    w_uv,
    prefix_latent,
    prefix_rope,
    prefix_lengths,
    placements,
):
    n_rep, n_x, n_hi, n_lo = shape
    n_z = n_hi * n_lo
    half = n_z // 2
    tok, depth = hidden.shape[1:]
    heads, nope, lat = w_uk.shape
    rope = w_krope.shape[1]
    value = w_uv.shape[2]
    width = -(-(lat + rope) // 128) * 128
    count = rope // 2
    powers = -(np.arange(count, dtype=np.float32) * np.float32(2.0)) / np.float32(rope)
    frequency = np.power(np.float64(ROPE_THETA), powers.astype(np.float64))
    frequency = np.resize(frequency, (1, width - lat)).astype(np.float32)
    vmem = pl.BlockSpec(memory_space=pltpu.VMEM)
    smem = pl.BlockSpec(memory_space=pltpu.SMEM)
    anywhere = pl.BlockSpec(memory_space=pl.ANY)
    bf16, f32 = jnp.bfloat16, jnp.float32
    dma = pltpu.SemaphoreType.DMA
    out = pl.pallas_call(
        functools.partial(kernel, shape),
        out_shape=(
            jax.ShapeDtypeStruct((tok, heads * value), bf16),
            jax.ShapeDtypeStruct((2, BLOCK, lat), bf16),
            jax.ShapeDtypeStruct((2, BLOCK * rope), bf16),
            jax.ShapeDtypeStruct((2, BLOCK * TILES), bf16),
        ),
        in_specs=[smem, smem, vmem, vmem] + [anywhere] * 9,
        out_specs=(vmem, vmem, vmem, vmem),
        scratch_shapes=[
            pltpu.VMEM((tok, depth), bf16),
            pltpu.VMEM((tok, heads * nope), bf16),
            pltpu.VMEM((tok, heads * rope), bf16),
            pltpu.VMEM((depth, lat), bf16),
            pltpu.VMEM((rope, depth), bf16),
            pltpu.VMEM((heads, nope, lat), bf16),
            pltpu.VMEM((heads, lat, value), bf16),
            pltpu.VMEM((PIECE, lat), bf16),
            pltpu.VMEM((PIECE, rope), bf16),
            pltpu.VMEM((2, n_lo, PIECE, width), f32),
            pltpu.VMEM((n_lo, PIECE, width), f32),
            pltpu.VMEM((n_lo, PIECE, width), f32),
            pltpu.VMEM((max(n_lo - 1, 1), PIECE, width), f32),
            pltpu.VMEM((n_z, n_x, 2, PIECE, width), bf16),
            pltpu.VMEM((n_z, n_x, PIECE, width), bf16),
            pltpu.VMEM((n_z, n_x, 2, PIECE, tok), bf16),
            pltpu.VMEM((2, n_rep * n_lo, PIECE, width), bf16),
            pltpu.VMEM((heads * tok, width + tok), bf16),
            pltpu.VMEM((heads * tok, lat), f32),
            pltpu.VMEM((heads * tok, 128), f32),
            pltpu.VMEM((heads * tok, 128), f32),
            pltpu.VMEM((2 * BLOCK, 2 * rope), f32),
            dma((6 + depth // 128 + 2 * heads,)),
            dma,
            dma,
            dma((max(n_lo - 1, 1),)),
            dma((max(n_lo - 1, 1),)),
            dma((2, n_x - 1, 2)),
            dma((2, n_x - 1, 2)),
            dma,
            dma,
            dma((2, half + 1, 2)),
            dma((2, half + 1, 2)),
            dma((2, half + 1, 2, 2)),
            dma((2, half + 1, 2, 2)),
            dma((2, half + 1, 2)),
            dma((2, half + 1, 2)),
            dma((max(n_rep - 1, 1), 2)),
            dma((max(n_rep - 1, 1), 2)),
        ],
        compiler_params=pltpu.CompilerParams(
            collective_id=0, has_side_effects=True, vmem_limit_bytes=56 * 1024 * 1024
        ),
    )(
        prefix_lengths,
        placements,
        jnp.asarray(frequency),
        kv_gain.reshape(1, lat),
        hidden[0],
        q_nope[0],
        q_rope[0],
        w_latent,
        w_krope.T,
        w_uk,
        w_uv,
        prefix_latent[0],
        prefix_rope[0],
    )
    return tuple(result.reshape(1, result.shape[0], -1) for result in out)


def program(mesh, shape):
    return jax.shard_map(
        functools.partial(per_device, shape),
        mesh=mesh,
        in_specs=(
            P("replica", "context", "tensor"),
            P("replica", "context", "tensor"),
            P("replica", "context", "tensor"),
            P("tensor", None),
            P("tensor", None),
            P(),
            P("tensor", None, None),
            P("tensor", None, None),
            P("replica", "context", None),
            P("replica", "context", None),
            P("replica"),
            P("context", None),
        ),
        out_specs=(
            P("replica", "context", "tensor"),
            P("replica", "context", None),
            P("replica", "context", None),
            P("replica", "context", None),
        ),
        check_vma=False,
    )


def solution(mesh):
    n_hi = 4
    return program(
        mesh,
        (
            mesh.shape["replica"],
            mesh.shape["context"] // n_hi,
            n_hi,
            mesh.shape["tensor"] // 2,
        ),
    )
```

```python
import functools
import math

import jax
import jax.numpy as jnp
import numpy as np
from jax import lax
from jax.experimental import pallas as pl
from jax.experimental.pallas import tpu as pltpu
from jax.sharding import PartitionSpec as P

MESH = pl.DeviceIdType.MESH
BLOCK = 64
TILES = 4
PIECE = 16
COLUMNS = 512
ROPE_THETA = 50000.0
NORM_EPS = 1e-06
SCALE_EPS = 1e-06
MASKED = -1e30
FLOOR = -1e28


def when(condition, action):
    if isinstance(condition, bool):
        if condition:
            action()
    else:
        pl.when(condition)(action)


def both(*conditions):
    static = [c for c in conditions if isinstance(c, bool)]
    traced = [c for c in conditions if not isinstance(c, bool)]
    if not all(static):
        return False
    if not traced:
        return True
    out = traced[0]
    for c in traced[1:]:
        out = jnp.logical_and(out, c)
    return out


def sine_cosine(angle):
    turns = jnp.floor(angle * np.float32(1.0 / (2.0 * math.pi)) + 0.5)
    high = 6.28125
    middle = float(np.float32(0.0019350051879882812))
    low = 2.0 * math.pi - high - middle
    r = angle - turns * np.float32(high)
    r = r - turns * np.float32(middle)
    r = r - turns * np.float32(low)
    square = r * r
    sine = jnp.full_like(r, 1.0 / math.factorial(17))
    for n in (15, 13, 11, 9, 7, 5, 3, 1):
        sign = -1.0 if (n // 2) % 2 else 1.0
        sine = sine * square + sign / math.factorial(n)
    cosine = jnp.full_like(r, 1.0 / math.factorial(16))
    for n in (14, 12, 10, 8, 6, 4, 2, 0):
        sign = -1.0 if (n // 2) % 2 else 1.0
        cosine = cosine * square + sign / math.factorial(n)
    return sine * r, cosine


def kernel(
    shape,
    length_ref,
    places_ref,
    frequency_ref,
    gain_ref,
    hidden_hbm,
    q_nope_hbm,
    q_rope_hbm,
    w_latent_hbm,
    w_krope_hbm,
    w_uk_hbm,
    w_uv_hbm,
    pre_lat_hbm,
    pre_rope_hbm,
    out_ref,
    cache_lat_ref,
    cache_rope_ref,
    cache_scale_ref,
    hidden,
    q_nope,
    q_rope,
    w_latent,
    w_krope,
    w_uk,
    w_uv,
    pre_lat,
    pre_rope,
    partial,
    partner_part,
    chip_sum,
    group_part,
    keys,
    marks,
    blocks,
    queries,
    total,
    top,
    weight_sum,
    in_sem,
    ra_send,
    ra_recv,
    rb_send,
    rb_recv,
    px_send,
    px_recv,
    pz_send,
    pz_recv,
    pd_send,
    pd_recv,
    nx_send,
    nx_recv,
    no_send,
    no_recv,
    nz_send,
    nz_recv,
    nd_send,
    nd_recv,
    y_send,
    y_recv,
    yd_send,
    yd_recv,
):
    n_rep, n_x, n_hi, n_lo = shape
    n_z = n_hi * n_lo
    half = n_z // 2
    heads, nope, lat = w_uk.shape
    rope = pre_rope.shape[1]
    width = keys.shape[-1]
    value = w_uv.shape[2]
    tok = hidden.shape[0]

    replica = lax.axis_index("replica")
    context = lax.axis_index("context")
    tensor = lax.axis_index("tensor")
    x = lax.div(context, n_hi)
    z_hi = lax.rem(context, n_hi)
    z_lo = lax.div(tensor, 2)
    core = lax.rem(tensor, 2)
    other = 1 - core
    z = z_hi * n_lo + z_lo
    sign = 1 - 2 * core

    def wrap(place):
        return lax.rem(place + 2 * n_z, n_z)

    def at_z(place):
        return {
            "context": x * n_hi + lax.div(place, n_lo),
            "tensor": lax.rem(place, n_lo) * 2 + core,
        }

    def at_x(place):
        return {"context": place * n_hi + z_hi}

    def x_plus(step):
        return lax.rem(x + step, n_x)

    def r_plus(step):
        return lax.rem(replica + step, n_rep)

    partner = {"tensor": z_lo * 2 + other}
    z_next = at_z(wrap(z + sign))
    z_behind = at_z(wrap(z - sign))

    peers = [z_next, z_behind, partner]
    peers += [at_x(x_plus(d)) for d in range(1, n_x)]
    peers += [{"tensor": lax.rem(z_lo + d, n_lo) * 2 + core} for d in range(1, n_lo)]
    peers += [{"replica": r_plus(d)} for d in range(1, n_rep)]
    barrier = pltpu.get_barrier_semaphore()
    for peer in peers:
        pl.semaphore_signal(barrier, inc=1, device_id=peer, device_id_type=MESH)

    own_pre = pl.multiple_of(z_lo * PIECE, PIECE)
    loads = [
        (hidden_hbm, hidden),
        (w_latent_hbm, w_latent),
        (w_krope_hbm, w_krope),
        (pre_lat_hbm.at[pl.ds(own_pre, PIECE)], pre_lat),
        (pre_rope_hbm.at[pl.ds(own_pre, PIECE)], pre_rope),
        (q_nope_hbm, q_nope),
        (q_rope_hbm, q_rope),
        (w_uk_hbm, w_uk),
        (w_uv_hbm, w_uv),
    ]
    loads = [
        pltpu.make_async_copy(source, target, in_sem.at[i])
        for i, (source, target) in enumerate(loads)
    ]
    for load in loads:
        load.start()

    def send(source, target, send_sem, recv_sem, device):
        return pltpu.make_async_remote_copy(
            src_ref=source,
            dst_ref=target,
            send_sem=send_sem,
            recv_sem=recv_sem,
            device_id=device,
            device_id_type=MESH,
        )

    def same(ref, send_sem, recv_sem, device):
        return send(ref, ref, send_sem, recv_sem, device)

    def ra_copy():
        return send(partial.at[other], partner_part, ra_send, ra_recv, partner)

    def rb_copy(d):
        to = lax.rem(z_lo + d, n_lo)
        return send(
            chip_sum.at[to],
            group_part.at[d - 1],
            rb_send.at[d - 1],
            rb_recv.at[d - 1],
            {"tensor": to * 2 + core},
        )

    def pz_copy(p):
        return same(
            keys.at[0, wrap(z - sign * (p - 1)), x], pz_send.at[p], pz_recv.at[p], z_next
        )

    def pz_arrival(p):
        return same(keys.at[0, wrap(z - sign * p), x], pz_send.at[p], pz_recv.at[p], z_next)

    def px_copy(p, d):
        return same(
            keys.at[0, wrap(z - sign * p), x],
            px_send.at[p, d - 1],
            px_recv.at[p, d - 1],
            at_x(x_plus(d)),
        )

    def px_arrival(p, d):
        return same(
            keys.at[0, wrap(z - sign * p), x_plus(n_x - d)],
            px_send.at[p, d - 1],
            px_recv.at[p, d - 1],
            partner,
        )

    def pd_copy(p):
        return same(keys.at[0, wrap(z - sign * p)], pd_send.at[p], pd_recv.at[p], partner)

    def pd_arrival(p):
        return same(keys.at[0, wrap(z + sign * p)], pd_send.at[p], pd_recv.at[p], partner)

    def prefix_step(p):
        def first():
            pz_arrival(p).wait_recv()
            when(p < half, lambda: pz_copy(p + 1).start())
            for d in range(1, n_x):
                px_copy(p, d).start()

        def second():
            for d in range(1, n_x):
                px_arrival(p - 1, d).wait_recv()
            when(both(p - 1 >= 1, p - 1 < half), lambda: pd_copy(p - 1).start())

        def third():
            pd_arrival(p - 2).wait_recv()

        when(p <= half, first)
        when(p - 1 <= half, second)
        when(both(p - 2 >= 1, p - 2 < half), third)

    own_kind = 1 + core

    def nx_copy(d):
        return same(
            keys.at[own_kind, z, x], nx_send.at[d - 1], nx_recv.at[d - 1], at_x(x_plus(d))
        )

    def nx_arrival(d):
        return same(
            keys.at[own_kind, z, x_plus(n_x - d)],
            nx_send.at[d - 1],
            nx_recv.at[d - 1],
            partner,
        )

    def no_copy():
        return same(keys.at[own_kind, z], no_send, no_recv, partner)

    def no_arrival():
        return same(keys.at[2 - core, z], no_send, no_recv, partner)

    def half_x(who):
        return pl.ds(who * (n_x // 2), n_x // 2)

    def nz_copy(kind, s):
        return same(
            keys.at[kind, wrap(z - sign * (s - 1))],
            nz_send.at[kind - 1, s],
            nz_recv.at[kind - 1, s],
            z_next,
        )

    def nz_arrival(kind, s):
        return same(
            keys.at[kind, wrap(z - sign * s)],
            nz_send.at[kind - 1, s],
            nz_recv.at[kind - 1, s],
            z_next,
        )

    def nz_last_copy(kind):
        return same(
            keys.at[kind, wrap(z - sign * (half - 1)), half_x(core)],
            nz_send.at[kind - 1, half],
            nz_recv.at[kind - 1, half],
            z_next,
        )

    def nz_last_arrival(kind):
        return same(
            keys.at[kind, wrap(z + half), half_x(core)],
            nz_send.at[kind - 1, half],
            nz_recv.at[kind - 1, half],
            z_next,
        )

    def nd_copy(kind, s):
        return same(
            keys.at[kind, wrap(z - sign * s)],
            nd_send.at[kind - 1, s],
            nd_recv.at[kind - 1, s],
            partner,
        )

    def nd_arrival(kind, s):
        return same(
            keys.at[kind, wrap(z + sign * s)],
            nd_send.at[kind - 1, s],
            nd_recv.at[kind - 1, s],
            partner,
        )

    def nd_last_copy(kind):
        return same(
            keys.at[kind, wrap(z + half), half_x(core)],
            nd_send.at[kind - 1, half],
            nd_recv.at[kind - 1, half],
            partner,
        )

    def nd_last_arrival(kind):
        return same(
            keys.at[kind, wrap(z + half), half_x(other)],
            nd_send.at[kind - 1, half],
            nd_recv.at[kind - 1, half],
            partner,
        )

    def new_step(s):
        def middle():
            for kind in (1, 2):
                nz_arrival(kind, s).wait_recv()
                when(s + 1 < half, lambda: nz_copy(kind, s + 1).start())
                when(s + 1 == half, lambda: nz_last_copy(kind).start())
                nd_copy(kind, s).start()

        def last():
            for kind in (1, 2):
                nz_last_arrival(kind).wait_recv()
                nd_last_copy(kind).start()

        when(s < half, middle)
        when(s == half, last)

    def y_copy(d):
        return send(
            keys.at[own_kind, pl.ds(z_hi * n_lo, n_lo), x],
            blocks.at[core, pl.ds(replica * n_lo, n_lo)],
            y_send.at[d - 1],
            y_recv.at[d - 1],
            {"replica": r_plus(d)},
        )

    def y_arrival(d):
        return send(
            keys.at[own_kind, pl.ds(z_hi * n_lo, n_lo), x],
            blocks.at[core, pl.ds(r_plus(n_rep - d) * n_lo, n_lo)],
            y_send.at[d - 1],
            y_recv.at[d - 1],
            partner,
        )

    def yd_copy():
        return same(blocks.at[core], yd_send, yd_recv, partner)

    def yd_arrival():
        return same(blocks.at[other], yd_send, yd_recv, partner)

    loads[0].wait()
    loads[1].wait()
    loads[2].wait()
    lat_term = jnp.dot(hidden[...], w_latent[...], preferred_element_type=jnp.float32)
    rope_term = lax.dot_general(
        hidden[...], w_krope[...], (((1,), (1,)), ((), ())), preferred_element_type=jnp.float32
    )
    rope_term = jnp.concatenate(
        [rope_term, jnp.zeros((tok, width - lat - rope), jnp.float32)], axis=1
    )
    for place in range(n_lo):
        for who in range(2):
            first = (place * 2 + who) * PIECE
            partial[who, place, :, :lat] = lat_term[first : first + PIECE]
            partial[who, place, :, lat:] = rope_term[first : first + PIECE]
    loads[3].wait()
    loads[4].wait()
    keys[0, z, x, :, :lat] = pre_lat[...]
    length = length_ref[0]
    n_context = n_x * n_hi
    piece_row = lax.broadcasted_iota(jnp.int32, (PIECE, width - lat), 0)
    piece_lanes = lax.broadcasted_iota(jnp.int32, (PIECE, width - lat), 1)
    pre_place = context * (n_lo * PIECE) + z_lo * PIECE + piece_row
    hidden_key = jnp.logical_and(piece_lanes == rope + n_context, pre_place >= length)
    pre_tail = jnp.concatenate(
        [
            pre_rope[...].astype(jnp.float32),
            jnp.zeros((PIECE, width - lat - rope), jnp.float32),
        ],
        axis=1,
    )
    keys[0, z, x, :, lat:] = jnp.where(hidden_key, MASKED, pre_tail).astype(jnp.bfloat16)

    pl.semaphore_wait(barrier, len(peers))
    ra_copy().start()
    pz_copy(1).start()
    for d in range(1, n_x):
        px_copy(0, d).start()

    loads[5].wait()
    loads[6].wait()
    loads[7].wait()
    lanes = lax.broadcasted_iota(jnp.int32, (tok, width - lat), 1)
    later = jnp.logical_and(lanes > rope + context, lanes < rope + n_context)
    masks = jnp.where(later, MASKED, jnp.where(lanes == rope + n_context, 1.0, 0.0))
    key_row = lax.broadcasted_iota(jnp.int32, (tok, tok), 0)
    query_lane = lax.broadcasted_iota(jnp.int32, (tok, tok), 1)
    triangle = jnp.where(key_row > query_lane, MASKED, 0.0).astype(jnp.bfloat16)
    marks[...] = jnp.zeros_like(marks)
    mark_row = lax.broadcasted_iota(jnp.int32, (PIECE, tok), 0)
    mark_lane = lax.broadcasted_iota(jnp.int32, (PIECE, tok), 1)
    for place in range(n_lo):
        for who in range(2):
            first = (place * 2 + who) * PIECE
            marks[1 + who, z_hi * n_lo + place, x] = jnp.where(
                mark_lane == first + mark_row, 1.0, 0.0
            ).astype(jnp.bfloat16)

    def absorb(first, last):
        for head in range(first, last):
            columns = pl.ds(head * tok, tok)
            absorbed = jnp.dot(
                q_nope[:, head * nope : (head + 1) * nope],
                w_uk[head],
                preferred_element_type=jnp.float32,
            )
            queries[:lat, columns] = absorbed.T.astype(jnp.bfloat16)
            pair = q_rope[:, (head // 2) * 2 * rope : (head // 2 + 1) * 2 * rope]
            pair = pair.astype(jnp.float32)
            if head % 2:
                pair = pltpu.roll(pair, rope, 1)
            queries[lat:width, columns] = jnp.where(lanes < rope, pair, masks).T.astype(jnp.bfloat16)
            queries[width:, columns] = triangle

    absorb(0, heads // 2)

    ra_copy().wait_recv()
    chip_sum[...] = partial[core] + partner_part[...]
    for d in range(1, n_lo):
        rb_copy(d).start()

    if half >= 1:
        prefix_step(1)
    absorb(heads // 2, heads)

    position = (
        length
        + context * tok
        + tensor * PIECE
        + piece_row
    )
    sine, cosine = sine_cosine(position.astype(jnp.float32) * frequency_ref[...])
    sine = jnp.where(piece_lanes < rope // 2, -sine, sine)
    sine = jnp.where(piece_lanes < rope, sine, 0.0)

    top[...] = jnp.full_like(top, FLOOR)
    weight_sum[...] = jnp.zeros_like(weight_sum)
    total[...] = jnp.zeros_like(total)

    for d in range(1, n_lo):
        rb_copy(d).wait_recv()
    summed = chip_sum[z_lo]
    for d in range(1, n_lo):
        summed = summed + group_part[d - 1]
    lat_sum = summed[:, :lat]
    mean_square = jnp.mean(lat_sum * lat_sum, axis=1, keepdims=True)
    keys[own_kind, z, x, :, :lat] = (
        lat_sum * lax.rsqrt(mean_square + NORM_EPS) * gain_ref[...]
    ).astype(jnp.bfloat16)
    rope_sum = summed[:, lat:]
    swapped = jnp.where(
        piece_lanes < rope // 2,
        pltpu.roll(rope_sum, width - lat - rope // 2, 1),
        pltpu.roll(rope_sum, rope // 2, 1),
    )
    new_tail = rope_sum * cosine + swapped * sine
    keys[own_kind, z, x, :, lat:] = jnp.where(
        piece_lanes == rope + context, 1.0, new_tail
    ).astype(jnp.bfloat16)

    for d in range(1, n_x):
        nx_copy(d).start()
    prefix_step(2)
    for d in range(1, n_x):
        nx_arrival(d).wait_recv()
    no_copy().start()

    def start_ring(kind):
        if half > 1:
            nz_copy(kind, 1).start()
        else:
            nz_last_copy(kind).start()

    pl.when(core == 0)(lambda: start_ring(1))
    pl.when(core == 1)(lambda: start_ring(2))
    prefix_step(3)
    no_arrival().wait_recv()
    pl.when(core == 1)(lambda: start_ring(1))
    pl.when(core == 0)(lambda: start_ring(2))

    score_scale = float((nope + rope) ** (-0.5) * math.log2(math.e))

    def attend(slots):
        block = n_x * PIECE
        key_rows = jnp.concatenate(
            [
                jnp.concatenate(
                    [
                        keys[kind, place].reshape(block, width),
                        marks[kind, place].reshape(block, tok),
                    ],
                    axis=1,
                )
                for place in slots
                for kind in range(3)
            ],
            axis=0,
        )
        latents = key_rows[:, :lat].T
        at_once = min(COLUMNS, heads * tok)
        for first in range(0, heads * tok, at_once):
            columns = pl.ds(first, at_once)
            scores = jnp.dot(key_rows, queries[:, columns], preferred_element_type=jnp.float32)
            scores = scores * score_scale
            old_top = top[:, columns]
            new_top = jnp.maximum(old_top, jnp.max(scores, axis=0, keepdims=True))
            top[:, columns] = new_top
            rescale = jnp.exp2(old_top - new_top)
            exponents = jnp.exp2(scores - new_top)
            weight_sum[:, columns] = weight_sum[:, columns] * rescale + jnp.sum(
                exponents, axis=0, keepdims=True
            )
            total[:, columns] = total[:, columns] * rescale + jnp.dot(
                latents, exponents.astype(jnp.bfloat16), preferred_element_type=jnp.float32
            )

    def iteration(s, carry):
        new_step(s)
        prefix_step(s + 3)

        def from_partner():
            for kind in (1, 2):
                nd_arrival(kind, s - 1).wait_recv()

        pl.when(s > 1)(from_partner)

        def to_owners():
            for place in range(n_lo):
                blocks[core, replica * n_lo + place] = keys[own_kind, z_hi * n_lo + place, x]
            for d in range(1, n_rep):
                y_copy(d).start()

        pl.when(s == n_lo)(to_owners)

        def owners_done():
            for d in range(1, n_rep):
                y_arrival(d).wait_recv()
            yd_copy().start()

        pl.when(s == half)(owners_done)

        pl.when(s > 1)(lambda: attend([wrap(z - (s - 1)), wrap(z + (s - 1))]))
        return carry

    attend([z])
    lax.fori_loop(1, half + 1, iteration, 0)
    for kind in (1, 2):
        nd_last_arrival(kind).wait_recv()
    attend([wrap(z + half)])

    loads[8].wait()
    for head in range(heads):
        columns = pl.ds(head * tok, tok)
        latent_out = (total[:, columns] / weight_sum[:, columns]).astype(jnp.bfloat16)
        out_ref[:, head * value : (head + 1) * value] = jnp.dot(
            latent_out.T, w_uv[head], preferred_element_type=jnp.float32
        ).astype(jnp.bfloat16)

    yd_arrival().wait_recv()
    tile = lat // TILES
    per_block = BLOCK // (2 * PIECE)
    stored, ropes, flat_scales = [], [], []
    scale_row = lax.broadcasted_iota(jnp.int32, (BLOCK, BLOCK * TILES), 0)
    scale_lane = lax.broadcasted_iota(jnp.int32, (BLOCK, BLOCK * TILES), 1)
    rope_lane = lax.broadcasted_iota(jnp.int32, (BLOCK, 2 * rope), 1)
    for slot in range(2):
        source = jnp.int32(0)
        for candidate in range(n_rep * 2):
            source = jnp.where(
                places_ref[0, candidate] == replica * 2 + slot, candidate, source
            )
        rows = jnp.concatenate(
            [
                blocks[who, source * per_block + place]
                for place in range(per_block)
                for who in range(2)
            ],
            axis=0,
        ).astype(jnp.float32)
        flat = jnp.zeros((BLOCK, BLOCK * TILES), jnp.float32)
        tiles = []
        for i in range(TILES):
            entries = rows[:, i * tile : (i + 1) * tile]
            scale = jnp.max(jnp.abs(entries), axis=1, keepdims=True) + SCALE_EPS
            scale = scale.astype(jnp.bfloat16).astype(jnp.float32)
            tiles.append(entries / scale)
            flat = jnp.where(scale_lane == scale_row * TILES + i, scale, flat)
        stored.append(jnp.concatenate(tiles, axis=1))
        flat_scales.append(jnp.sum(flat, axis=0, keepdims=True))
        tail = rows[:, lat : lat + 2 * rope]
        following = pltpu.roll(pltpu.roll(tail, BLOCK - 1, 0), rope, 1)
        ropes.append(jnp.where(rope_lane < rope, tail, following))
    for j in range(BLOCK):
        cache_lat_ref[:, j * lat : (j + 1) * lat] = jnp.concatenate(
            [stored[0][j : j + 1], stored[1][j : j + 1]], axis=0
        ).astype(jnp.bfloat16)
    for j in range(BLOCK // 2):
        cache_rope_ref[:, j * 2 * rope : (j + 1) * 2 * rope] = jnp.concatenate(
            [ropes[0][2 * j : 2 * j + 1], ropes[1][2 * j : 2 * j + 1]], axis=0
        ).astype(jnp.bfloat16)
    cache_scale_ref[...] = jnp.concatenate(flat_scales, axis=0).astype(jnp.bfloat16)

    ra_copy().wait_send()
    for d in range(1, n_lo):
        rb_copy(d).wait_send()
    for d in range(1, n_x):
        nx_copy(d).wait_send()
    for d in range(1, n_rep):
        y_copy(d).wait_send()
    no_copy().wait_send()
    yd_copy().wait_send()

    def sent(s, carry):
        pz_copy(s).wait_send()

        def middle():
            pd_copy(s).wait_send()
            for kind in (1, 2):
                nz_copy(kind, s).wait_send()
                nd_copy(kind, s).wait_send()

        def last():
            for kind in (1, 2):
                nz_last_copy(kind).wait_send()
                nd_last_copy(kind).wait_send()

        pl.when(s < half)(middle)
        pl.when(s == half)(last)
        return carry

    lax.fori_loop(1, half + 1, sent, 0)

    def pushed(p, carry):
        for d in range(1, n_x):
            px_copy(p, d).wait_send()
        return carry

    lax.fori_loop(0, half + 1, pushed, 0)


def per_device(
    shape,
    hidden,
    q_nope,
    q_rope,
    w_latent,
    w_krope,
    kv_gain,
    w_uk,
    w_uv,
    prefix_latent,
    prefix_rope,
    prefix_lengths,
    placements,
):
    n_rep, n_x, n_hi, n_lo = shape
    n_z = n_hi * n_lo
    half = n_z // 2
    tok, depth = hidden.shape[1:]
    heads, nope, lat = w_uk.shape
    rope = w_krope.shape[1]
    value = w_uv.shape[2]
    width = -(-(lat + rope) // 128) * 128
    count = rope // 2
    powers = -(np.arange(count, dtype=np.float32) * np.float32(2.0)) / np.float32(rope)
    frequency = np.power(np.float64(ROPE_THETA), powers.astype(np.float64))
    frequency = np.resize(frequency, (1, width - lat)).astype(np.float32)
    vmem = pl.BlockSpec(memory_space=pltpu.VMEM)
    smem = pl.BlockSpec(memory_space=pltpu.SMEM)
    anywhere = pl.BlockSpec(memory_space=pl.ANY)
    bf16, f32 = jnp.bfloat16, jnp.float32
    dma = pltpu.SemaphoreType.DMA
    out = pl.pallas_call(
        functools.partial(kernel, shape),
        out_shape=(
            jax.ShapeDtypeStruct((tok, heads * value), bf16),
            jax.ShapeDtypeStruct((2, BLOCK * lat), bf16),
            jax.ShapeDtypeStruct((2, BLOCK * rope), bf16),
            jax.ShapeDtypeStruct((2, BLOCK * TILES), bf16),
        ),
        in_specs=[smem, smem, vmem, vmem] + [anywhere] * 9,
        out_specs=(vmem, vmem, vmem, vmem),
        scratch_shapes=[
            pltpu.VMEM((tok, depth), bf16),
            pltpu.VMEM((tok, heads * nope), bf16),
            pltpu.VMEM((tok, heads * rope), bf16),
            pltpu.VMEM((depth, lat), bf16),
            pltpu.VMEM((rope, depth), bf16),
            pltpu.VMEM((heads, nope, lat), bf16),
            pltpu.VMEM((heads, lat, value), bf16),
            pltpu.VMEM((PIECE, lat), bf16),
            pltpu.VMEM((PIECE, rope), bf16),
            pltpu.VMEM((2, n_lo, PIECE, width), f32),
            pltpu.VMEM((n_lo, PIECE, width), f32),
            pltpu.VMEM((n_lo, PIECE, width), f32),
            pltpu.VMEM((max(n_lo - 1, 1), PIECE, width), f32),
            pltpu.VMEM((3, n_z, n_x, PIECE, width), bf16),
            pltpu.VMEM((3, n_z, n_x, PIECE, tok), bf16),
            pltpu.VMEM((2, n_rep * n_lo, PIECE, width), bf16),
            pltpu.VMEM((width + tok, heads * tok), bf16),
            pltpu.VMEM((lat, heads * tok), f32),
            pltpu.VMEM((1, heads * tok), f32),
            pltpu.VMEM((1, heads * tok), f32),
            dma((9,)),
            dma,
            dma,
            dma((max(n_lo - 1, 1),)),
            dma((max(n_lo - 1, 1),)),
            dma((half + 1, max(n_x - 1, 1))),
            dma((half + 1, max(n_x - 1, 1))),
            dma((half + 1,)),
            dma((half + 1,)),
            dma((half + 1,)),
            dma((half + 1,)),
            dma((max(n_x - 1, 1),)),
            dma((max(n_x - 1, 1),)),
            dma,
            dma,
            dma((2, half + 1)),
            dma((2, half + 1)),
            dma((2, half + 1)),
            dma((2, half + 1)),
            dma((max(n_rep - 1, 1),)),
            dma((max(n_rep - 1, 1),)),
            dma,
            dma,
        ],
        compiler_params=pltpu.CompilerParams(
            collective_id=0, has_side_effects=True, vmem_limit_bytes=56 * 1024 * 1024
        ),
    )(
        prefix_lengths,
        placements,
        jnp.asarray(frequency),
        kv_gain.reshape(1, lat),
        hidden[0],
        q_nope[0],
        q_rope[0],
        w_latent,
        w_krope.T,
        w_uk,
        w_uv,
        prefix_latent[0],
        prefix_rope[0],
    )
    return tuple(result[None] for result in out)


def program(mesh, shape):
    return jax.shard_map(
        functools.partial(per_device, shape),
        mesh=mesh,
        in_specs=(
            P("replica", "context", "tensor"),
            P("replica", "context", "tensor"),
            P("replica", "context", "tensor"),
            P("tensor", None),
            P("tensor", None),
            P(),
            P("tensor", None, None),
            P("tensor", None, None),
            P("replica", "context", None),
            P("replica", "context", None),
            P("replica"),
            P("context", None),
        ),
        out_specs=(
            P("replica", "context", "tensor"),
            P("replica", "context", None),
            P("replica", "context", None),
            P("replica", "context", None),
        ),
        check_vma=False,
    )


def solution(mesh):
    n_hi = 4
    return program(
        mesh,
        (
            mesh.shape["replica"],
            mesh.shape["context"] // n_hi,
            n_hi,
            mesh.shape["tensor"] // 2,
        ),
    )
```

```python
import functools
import math

import jax
import jax.numpy as jnp
import numpy as np
from jax import lax
from jax.experimental import pallas as pl
from jax.experimental.pallas import tpu as pltpu
from jax.sharding import PartitionSpec as P

MESH = pl.DeviceIdType.MESH
BLOCK = 64
TILES = 4
PIECE = 16
COLUMNS = 512
ROPE_THETA = 50000.0
NORM_EPS = 1e-06
SCALE_EPS = 1e-06
MASKED = -1e30
FLOOR = -1e28


def when(condition, action):
    if isinstance(condition, bool):
        if condition:
            action()
    else:
        pl.when(condition)(action)


def both(*conditions):
    static = [c for c in conditions if isinstance(c, bool)]
    traced = [c for c in conditions if not isinstance(c, bool)]
    if not all(static):
        return False
    if not traced:
        return True
    out = traced[0]
    for c in traced[1:]:
        out = jnp.logical_and(out, c)
    return out


def sine_cosine(angle):
    turns = jnp.floor(angle * np.float32(1.0 / (2.0 * math.pi)) + 0.5)
    high = 6.28125
    middle = float(np.float32(0.0019350051879882812))
    low = 2.0 * math.pi - high - middle
    r = angle - turns * np.float32(high)
    r = r - turns * np.float32(middle)
    r = r - turns * np.float32(low)
    square = r * r
    sine = jnp.full_like(r, 1.0 / math.factorial(17))
    for n in (15, 13, 11, 9, 7, 5, 3, 1):
        sign = -1.0 if (n // 2) % 2 else 1.0
        sine = sine * square + sign / math.factorial(n)
    cosine = jnp.full_like(r, 1.0 / math.factorial(16))
    for n in (14, 12, 10, 8, 6, 4, 2, 0):
        sign = -1.0 if (n // 2) % 2 else 1.0
        cosine = cosine * square + sign / math.factorial(n)
    return sine * r, cosine


def kernel(
    shape,
    length_ref,
    places_ref,
    frequency_ref,
    gain_ref,
    hidden_hbm,
    q_nope_hbm,
    q_rope_hbm,
    w_latent_hbm,
    w_krope_hbm,
    w_uk_hbm,
    w_uv_hbm,
    pre_lat_hbm,
    pre_rope_hbm,
    out_ref,
    cache_lat_ref,
    cache_rope_ref,
    cache_scale_ref,
    hidden,
    q_nope,
    q_rope,
    w_latent,
    w_krope,
    w_uk,
    w_uv,
    pre_lat,
    pre_rope,
    partial,
    partner_part,
    chip_sum,
    group_part,
    keys,
    marks,
    blocks,
    queries,
    total,
    top,
    weight_sum,
    in_sem,
    ra_send,
    ra_recv,
    rb_send,
    rb_recv,
    px_send,
    px_recv,
    pz_send,
    pz_recv,
    pd_send,
    pd_recv,
    nx_send,
    nx_recv,
    no_send,
    no_recv,
    nz_send,
    nz_recv,
    nd_send,
    nd_recv,
    y_send,
    y_recv,
    yd_send,
    yd_recv,
):
    n_rep, n_x, n_hi, n_lo = shape
    n_z = n_hi * n_lo
    half = n_z // 2
    heads, nope, lat = w_uk.shape
    rope = pre_rope.shape[1]
    width = keys.shape[-1]
    value = w_uv.shape[2]
    tok = hidden.shape[0]

    replica = lax.axis_index("replica")
    context = lax.axis_index("context")
    tensor = lax.axis_index("tensor")
    x = lax.div(context, n_hi)
    z_hi = lax.rem(context, n_hi)
    z_lo = lax.div(tensor, 2)
    core = lax.rem(tensor, 2)
    other = 1 - core
    z = z_hi * n_lo + z_lo
    sign = 1 - 2 * core

    def wrap(place):
        return lax.rem(place + 2 * n_z, n_z)

    def at_z(place):
        return {
            "context": x * n_hi + lax.div(place, n_lo),
            "tensor": lax.rem(place, n_lo) * 2 + core,
        }

    def at_x(place):
        return {"context": place * n_hi + z_hi}

    def x_plus(step):
        return lax.rem(x + step, n_x)

    def r_plus(step):
        return lax.rem(replica + step, n_rep)

    partner = {"tensor": z_lo * 2 + other}
    z_next = at_z(wrap(z + sign))
    z_behind = at_z(wrap(z - sign))

    peers = [z_next, z_behind, partner]
    peers += [at_x(x_plus(d)) for d in range(1, n_x)]
    peers += [{"tensor": lax.rem(z_lo + d, n_lo) * 2 + core} for d in range(1, n_lo)]
    peers += [{"replica": r_plus(d)} for d in range(1, n_rep)]
    barrier = pltpu.get_barrier_semaphore()
    for peer in peers:
        pl.semaphore_signal(barrier, inc=1, device_id=peer, device_id_type=MESH)

    own_pre = pl.multiple_of(z_lo * PIECE, PIECE)
    loads = [
        (hidden_hbm, hidden),
        (w_latent_hbm, w_latent),
        (w_krope_hbm, w_krope),
        (pre_lat_hbm.at[pl.ds(own_pre, PIECE)], pre_lat),
        (pre_rope_hbm.at[pl.ds(own_pre, PIECE)], pre_rope),
        (q_nope_hbm, q_nope),
        (q_rope_hbm, q_rope),
        (w_uk_hbm, w_uk),
        (w_uv_hbm, w_uv),
    ]
    loads = [
        pltpu.make_async_copy(source, target, in_sem.at[i])
        for i, (source, target) in enumerate(loads)
    ]
    for load in loads:
        load.start()

    def send(source, target, send_sem, recv_sem, device):
        return pltpu.make_async_remote_copy(
            src_ref=source,
            dst_ref=target,
            send_sem=send_sem,
            recv_sem=recv_sem,
            device_id=device,
            device_id_type=MESH,
        )

    def same(ref, send_sem, recv_sem, device):
        return send(ref, ref, send_sem, recv_sem, device)

    def ra_copy():
        return send(partial.at[other], partner_part, ra_send, ra_recv, partner)

    def rb_copy(d):
        to = lax.rem(z_lo + d, n_lo)
        return send(
            chip_sum.at[to],
            group_part.at[d - 1],
            rb_send.at[d - 1],
            rb_recv.at[d - 1],
            {"tensor": to * 2 + core},
        )

    def pz_copy(p):
        return same(
            keys.at[0, wrap(z - sign * (p - 1)), x], pz_send.at[p], pz_recv.at[p], z_next
        )

    def pz_arrival(p):
        return same(keys.at[0, wrap(z - sign * p), x], pz_send.at[p], pz_recv.at[p], z_next)

    def px_copy(p, d):
        return same(
            keys.at[0, wrap(z - sign * p), x],
            px_send.at[p, d - 1],
            px_recv.at[p, d - 1],
            at_x(x_plus(d)),
        )

    def px_arrival(p, d):
        return same(
            keys.at[0, wrap(z - sign * p), x_plus(n_x - d)],
            px_send.at[p, d - 1],
            px_recv.at[p, d - 1],
            partner,
        )

    def pd_copy(p):
        return same(keys.at[0, wrap(z - sign * p)], pd_send.at[p], pd_recv.at[p], partner)

    def pd_arrival(p):
        return same(keys.at[0, wrap(z + sign * p)], pd_send.at[p], pd_recv.at[p], partner)

    def prefix_step(p):
        def first():
            pz_arrival(p).wait_recv()
            when(p < half, lambda: pz_copy(p + 1).start())
            for d in range(1, n_x):
                px_copy(p, d).start()

        def second():
            for d in range(1, n_x):
                px_arrival(p - 1, d).wait_recv()
            when(both(p - 1 >= 1, p - 1 < half), lambda: pd_copy(p - 1).start())

        def third():
            pd_arrival(p - 2).wait_recv()

        when(p <= half, first)
        when(p - 1 <= half, second)
        when(both(p - 2 >= 1, p - 2 < half), third)

    own_kind = 1 + core

    def nx_copy(d):
        return same(
            keys.at[own_kind, z, x], nx_send.at[d - 1], nx_recv.at[d - 1], at_x(x_plus(d))
        )

    def nx_arrival(d):
        return same(
            keys.at[own_kind, z, x_plus(n_x - d)],
            nx_send.at[d - 1],
            nx_recv.at[d - 1],
            partner,
        )

    def no_copy():
        return same(keys.at[own_kind, z], no_send, no_recv, partner)

    def no_arrival():
        return same(keys.at[2 - core, z], no_send, no_recv, partner)

    def half_x(who):
        return pl.ds(who * (n_x // 2), n_x // 2)

    def nz_copy(kind, s):
        return same(
            keys.at[kind, wrap(z - sign * (s - 1))],
            nz_send.at[kind - 1, s],
            nz_recv.at[kind - 1, s],
            z_next,
        )

    def nz_arrival(kind, s):
        return same(
            keys.at[kind, wrap(z - sign * s)],
            nz_send.at[kind - 1, s],
            nz_recv.at[kind - 1, s],
            z_next,
        )

    def nz_last_copy(kind):
        return same(
            keys.at[kind, wrap(z - sign * (half - 1)), half_x(core)],
            nz_send.at[kind - 1, half],
            nz_recv.at[kind - 1, half],
            z_next,
        )

    def nz_last_arrival(kind):
        return same(
            keys.at[kind, wrap(z + half), half_x(core)],
            nz_send.at[kind - 1, half],
            nz_recv.at[kind - 1, half],
            z_next,
        )

    def nd_copy(kind, s):
        return same(
            keys.at[kind, wrap(z - sign * s)],
            nd_send.at[kind - 1, s],
            nd_recv.at[kind - 1, s],
            partner,
        )

    def nd_arrival(kind, s):
        return same(
            keys.at[kind, wrap(z + sign * s)],
            nd_send.at[kind - 1, s],
            nd_recv.at[kind - 1, s],
            partner,
        )

    def nd_last_copy(kind):
        return same(
            keys.at[kind, wrap(z + half), half_x(core)],
            nd_send.at[kind - 1, half],
            nd_recv.at[kind - 1, half],
            partner,
        )

    def nd_last_arrival(kind):
        return same(
            keys.at[kind, wrap(z + half), half_x(other)],
            nd_send.at[kind - 1, half],
            nd_recv.at[kind - 1, half],
            partner,
        )

    def new_step(s):
        def middle():
            for kind in (1, 2):
                nz_arrival(kind, s).wait_recv()
                when(s + 1 < half, lambda: nz_copy(kind, s + 1).start())
                when(s + 1 == half, lambda: nz_last_copy(kind).start())
                nd_copy(kind, s).start()

        def last():
            for kind in (1, 2):
                nz_last_arrival(kind).wait_recv()
                nd_last_copy(kind).start()

        when(s < half, middle)
        when(s == half, last)

    def y_copy(d):
        return send(
            keys.at[own_kind, pl.ds(z_hi * n_lo, n_lo), x],
            blocks.at[core, pl.ds(replica * n_lo, n_lo)],
            y_send.at[d - 1],
            y_recv.at[d - 1],
            {"replica": r_plus(d)},
        )

    def y_arrival(d):
        return send(
            keys.at[own_kind, pl.ds(z_hi * n_lo, n_lo), x],
            blocks.at[core, pl.ds(r_plus(n_rep - d) * n_lo, n_lo)],
            y_send.at[d - 1],
            y_recv.at[d - 1],
            partner,
        )

    def yd_copy():
        return same(blocks.at[core], yd_send, yd_recv, partner)

    def yd_arrival():
        return same(blocks.at[other], yd_send, yd_recv, partner)

    loads[0].wait()
    loads[1].wait()
    loads[2].wait()
    lat_term = jnp.dot(hidden[...], w_latent[...], preferred_element_type=jnp.float32)
    rope_term = lax.dot_general(
        hidden[...], w_krope[...], (((1,), (1,)), ((), ())), preferred_element_type=jnp.float32
    )
    rope_term = jnp.concatenate(
        [rope_term, jnp.zeros((tok, width - lat - rope), jnp.float32)], axis=1
    )
    for place in range(n_lo):
        for who in range(2):
            first = (place * 2 + who) * PIECE
            partial[who, place, :, :lat] = lat_term[first : first + PIECE]
            partial[who, place, :, lat:] = rope_term[first : first + PIECE]
    loads[3].wait()
    loads[4].wait()
    keys[0, z, x, :, :lat] = pre_lat[...]
    length = length_ref[0]
    n_context = n_x * n_hi
    piece_row = lax.broadcasted_iota(jnp.int32, (PIECE, width - lat), 0)
    piece_lanes = lax.broadcasted_iota(jnp.int32, (PIECE, width - lat), 1)
    pre_place = context * (n_lo * PIECE) + z_lo * PIECE + piece_row
    hidden_key = jnp.logical_and(piece_lanes == rope + n_context, pre_place >= length)
    pre_tail = jnp.concatenate(
        [
            pre_rope[...].astype(jnp.float32),
            jnp.zeros((PIECE, width - lat - rope), jnp.float32),
        ],
        axis=1,
    )
    keys[0, z, x, :, lat:] = jnp.where(hidden_key, MASKED, pre_tail).astype(jnp.bfloat16)

    pl.semaphore_wait(barrier, len(peers))
    ra_copy().start()
    pz_copy(1).start()
    for d in range(1, n_x):
        px_copy(0, d).start()

    ra_copy().wait_recv()
    chip_sum[...] = partial[core] + partner_part[...]
    for d in range(1, n_lo):
        rb_copy(d).start()

    loads[5].wait()
    loads[6].wait()
    loads[7].wait()
    lanes = lax.broadcasted_iota(jnp.int32, (tok, width - lat), 1)
    later = jnp.logical_and(lanes > rope + context, lanes < rope + n_context)
    masks = jnp.where(later, MASKED, jnp.where(lanes == rope + n_context, 1.0, 0.0))
    key_row = lax.broadcasted_iota(jnp.int32, (tok, tok), 0)
    query_lane = lax.broadcasted_iota(jnp.int32, (tok, tok), 1)
    triangle = jnp.where(key_row > query_lane, MASKED, 0.0).astype(jnp.bfloat16)
    marks[...] = jnp.zeros_like(marks)
    mark_row = lax.broadcasted_iota(jnp.int32, (PIECE, tok), 0)
    mark_lane = lax.broadcasted_iota(jnp.int32, (PIECE, tok), 1)
    for place in range(n_lo):
        for who in range(2):
            first = (place * 2 + who) * PIECE
            marks[1 + who, z_hi * n_lo + place, x] = jnp.where(
                mark_lane == first + mark_row, 1.0, 0.0
            ).astype(jnp.bfloat16)

    def absorb(first, last):
        for head in range(first, last):
            columns = pl.ds(head * tok, tok)
            absorbed = jnp.dot(
                q_nope[:, head * nope : (head + 1) * nope],
                w_uk[head],
                preferred_element_type=jnp.float32,
            )
            queries[:lat, columns] = absorbed.T.astype(jnp.bfloat16)
            pair = q_rope[:, (head // 2) * 2 * rope : (head // 2 + 1) * 2 * rope]
            pair = pair.astype(jnp.float32)
            if head % 2:
                pair = pltpu.roll(pair, rope, 1)
            queries[lat:width, columns] = jnp.where(lanes < rope, pair, masks).T.astype(jnp.bfloat16)
            queries[width:, columns] = triangle

    absorb(0, heads // 2)

    if half >= 1:
        prefix_step(1)
    absorb(heads // 2, heads)

    position = (
        length
        + context * tok
        + tensor * PIECE
        + piece_row
    )
    sine, cosine = sine_cosine(position.astype(jnp.float32) * frequency_ref[...])
    sine = jnp.where(piece_lanes < rope // 2, -sine, sine)
    sine = jnp.where(piece_lanes < rope, sine, 0.0)

    top[...] = jnp.full_like(top, FLOOR)
    weight_sum[...] = jnp.zeros_like(weight_sum)
    total[...] = jnp.zeros_like(total)

    for d in range(1, n_lo):
        rb_copy(d).wait_recv()
    summed = chip_sum[z_lo]
    for d in range(1, n_lo):
        summed = summed + group_part[d - 1]
    lat_sum = summed[:, :lat]
    mean_square = jnp.mean(lat_sum * lat_sum, axis=1, keepdims=True)
    keys[own_kind, z, x, :, :lat] = (
        lat_sum * lax.rsqrt(mean_square + NORM_EPS) * gain_ref[...]
    ).astype(jnp.bfloat16)
    rope_sum = summed[:, lat:]
    swapped = jnp.where(
        piece_lanes < rope // 2,
        pltpu.roll(rope_sum, width - lat - rope // 2, 1),
        pltpu.roll(rope_sum, rope // 2, 1),
    )
    new_tail = rope_sum * cosine + swapped * sine
    keys[own_kind, z, x, :, lat:] = jnp.where(
        piece_lanes == rope + context, 1.0, new_tail
    ).astype(jnp.bfloat16)

    for d in range(1, n_x):
        nx_copy(d).start()
    prefix_step(2)
    for d in range(1, n_x):
        nx_arrival(d).wait_recv()
    no_copy().start()

    def start_ring(kind):
        if half > 1:
            nz_copy(kind, 1).start()
        else:
            nz_last_copy(kind).start()

    pl.when(core == 0)(lambda: start_ring(1))
    pl.when(core == 1)(lambda: start_ring(2))
    prefix_step(3)
    no_arrival().wait_recv()
    pl.when(core == 1)(lambda: start_ring(1))
    pl.when(core == 0)(lambda: start_ring(2))

    score_scale = float((nope + rope) ** (-0.5) * math.log2(math.e))

    def attend(slots):
        block = n_x * PIECE
        key_rows = jnp.concatenate(
            [
                jnp.concatenate(
                    [
                        keys[kind, place].reshape(block, width),
                        marks[kind, place].reshape(block, tok),
                    ],
                    axis=1,
                )
                for place in slots
                for kind in range(3)
            ],
            axis=0,
        )
        latents = key_rows[:, :lat].T
        at_once = min(COLUMNS, heads * tok)
        for first in range(0, heads * tok, at_once):
            columns = pl.ds(first, at_once)
            scores = jnp.dot(key_rows, queries[:, columns], preferred_element_type=jnp.float32)
            scores = scores * score_scale
            old_top = top[:, columns]
            new_top = jnp.maximum(old_top, jnp.max(scores, axis=0, keepdims=True))
            top[:, columns] = new_top
            rescale = jnp.exp2(old_top - new_top)
            exponents = jnp.exp2(scores - new_top)
            weight_sum[:, columns] = weight_sum[:, columns] * rescale + jnp.sum(
                exponents, axis=0, keepdims=True
            )
            total[:, columns] = total[:, columns] * rescale + jnp.dot(
                latents, exponents.astype(jnp.bfloat16), preferred_element_type=jnp.float32
            )

    def iteration(s, carry):
        new_step(s)
        prefix_step(s + 3)

        def from_partner():
            for kind in (1, 2):
                nd_arrival(kind, s - 1).wait_recv()

        pl.when(s > 1)(from_partner)

        def to_owners():
            for place in range(n_lo):
                blocks[core, replica * n_lo + place] = keys[own_kind, z_hi * n_lo + place, x]
            for d in range(1, n_rep):
                y_copy(d).start()

        pl.when(s == n_lo)(to_owners)

        def owners_done():
            for d in range(1, n_rep):
                y_arrival(d).wait_recv()
            yd_copy().start()

        pl.when(s == half)(owners_done)

        pl.when(s == 1)(lambda: attend([z]))
        pl.when(s > 1)(lambda: attend([wrap(z - (s - 1)), wrap(z + (s - 1))]))
        return carry

    lax.fori_loop(1, half + 1, iteration, 0)
    for kind in (1, 2):
        nd_last_arrival(kind).wait_recv()
    attend([wrap(z + half)])

    loads[8].wait()
    for head in range(heads):
        columns = pl.ds(head * tok, tok)
        latent_out = (total[:, columns] / weight_sum[:, columns]).astype(jnp.bfloat16)
        out_ref[:, head * value : (head + 1) * value] = jnp.dot(
            latent_out.T, w_uv[head], preferred_element_type=jnp.float32
        ).astype(jnp.bfloat16)

    yd_arrival().wait_recv()
    tile = lat // TILES
    per_block = BLOCK // (2 * PIECE)
    stored, ropes, flat_scales = [], [], []
    scale_row = lax.broadcasted_iota(jnp.int32, (BLOCK, BLOCK * TILES), 0)
    scale_lane = lax.broadcasted_iota(jnp.int32, (BLOCK, BLOCK * TILES), 1)
    rope_lane = lax.broadcasted_iota(jnp.int32, (BLOCK, 2 * rope), 1)
    for slot in range(2):
        source = jnp.int32(0)
        for candidate in range(n_rep * 2):
            source = jnp.where(
                places_ref[0, candidate] == replica * 2 + slot, candidate, source
            )
        rows = jnp.concatenate(
            [
                blocks[who, source * per_block + place]
                for place in range(per_block)
                for who in range(2)
            ],
            axis=0,
        ).astype(jnp.float32)
        flat = jnp.zeros((BLOCK, BLOCK * TILES), jnp.float32)
        tiles = []
        for i in range(TILES):
            entries = rows[:, i * tile : (i + 1) * tile]
            scale = jnp.max(jnp.abs(entries), axis=1, keepdims=True) + SCALE_EPS
            scale = scale.astype(jnp.bfloat16).astype(jnp.float32)
            tiles.append(entries / scale)
            flat = jnp.where(scale_lane == scale_row * TILES + i, scale, flat)
        stored.append(jnp.concatenate(tiles, axis=1))
        flat_scales.append(jnp.sum(flat, axis=0, keepdims=True))
        tail = rows[:, lat : lat + 2 * rope]
        following = pltpu.roll(pltpu.roll(tail, BLOCK - 1, 0), rope, 1)
        ropes.append(jnp.where(rope_lane < rope, tail, following))
    for j in range(BLOCK):
        cache_lat_ref[:, j * lat : (j + 1) * lat] = jnp.concatenate(
            [stored[0][j : j + 1], stored[1][j : j + 1]], axis=0
        ).astype(jnp.bfloat16)
    for j in range(BLOCK // 2):
        cache_rope_ref[:, j * 2 * rope : (j + 1) * 2 * rope] = jnp.concatenate(
            [ropes[0][2 * j : 2 * j + 1], ropes[1][2 * j : 2 * j + 1]], axis=0
        ).astype(jnp.bfloat16)
    cache_scale_ref[...] = jnp.concatenate(flat_scales, axis=0).astype(jnp.bfloat16)

    ra_copy().wait_send()
    for d in range(1, n_lo):
        rb_copy(d).wait_send()
    for d in range(1, n_x):
        nx_copy(d).wait_send()
    for d in range(1, n_rep):
        y_copy(d).wait_send()
    no_copy().wait_send()
    yd_copy().wait_send()

    def sent(s, carry):
        pz_copy(s).wait_send()

        def middle():
            pd_copy(s).wait_send()
            for kind in (1, 2):
                nz_copy(kind, s).wait_send()
                nd_copy(kind, s).wait_send()

        def last():
            for kind in (1, 2):
                nz_last_copy(kind).wait_send()
                nd_last_copy(kind).wait_send()

        pl.when(s < half)(middle)
        pl.when(s == half)(last)
        return carry

    lax.fori_loop(1, half + 1, sent, 0)

    def pushed(p, carry):
        for d in range(1, n_x):
            px_copy(p, d).wait_send()
        return carry

    lax.fori_loop(0, half + 1, pushed, 0)


def per_device(
    shape,
    hidden,
    q_nope,
    q_rope,
    w_latent,
    w_krope,
    kv_gain,
    w_uk,
    w_uv,
    prefix_latent,
    prefix_rope,
    prefix_lengths,
    placements,
):
    n_rep, n_x, n_hi, n_lo = shape
    n_z = n_hi * n_lo
    half = n_z // 2
    tok, depth = hidden.shape[1:]
    heads, nope, lat = w_uk.shape
    rope = w_krope.shape[1]
    value = w_uv.shape[2]
    width = -(-(lat + rope) // 128) * 128
    count = rope // 2
    powers = -(np.arange(count, dtype=np.float32) * np.float32(2.0)) / np.float32(rope)
    frequency = np.power(np.float64(ROPE_THETA), powers.astype(np.float64))
    frequency = np.resize(frequency, (1, width - lat)).astype(np.float32)
    vmem = pl.BlockSpec(memory_space=pltpu.VMEM)
    smem = pl.BlockSpec(memory_space=pltpu.SMEM)
    anywhere = pl.BlockSpec(memory_space=pl.ANY)
    bf16, f32 = jnp.bfloat16, jnp.float32
    dma = pltpu.SemaphoreType.DMA
    out = pl.pallas_call(
        functools.partial(kernel, shape),
        out_shape=(
            jax.ShapeDtypeStruct((tok, heads * value), bf16),
            jax.ShapeDtypeStruct((2, BLOCK * lat), bf16),
            jax.ShapeDtypeStruct((2, BLOCK * rope), bf16),
            jax.ShapeDtypeStruct((2, BLOCK * TILES), bf16),
        ),
        in_specs=[smem, smem, vmem, vmem] + [anywhere] * 9,
        out_specs=(vmem, vmem, vmem, vmem),
        scratch_shapes=[
            pltpu.VMEM((tok, depth), bf16),
            pltpu.VMEM((tok, heads * nope), bf16),
            pltpu.VMEM((tok, heads * rope), bf16),
            pltpu.VMEM((depth, lat), bf16),
            pltpu.VMEM((rope, depth), bf16),
            pltpu.VMEM((heads, nope, lat), bf16),
            pltpu.VMEM((heads, lat, value), bf16),
            pltpu.VMEM((PIECE, lat), bf16),
            pltpu.VMEM((PIECE, rope), bf16),
            pltpu.VMEM((2, n_lo, PIECE, width), f32),
            pltpu.VMEM((n_lo, PIECE, width), f32),
            pltpu.VMEM((n_lo, PIECE, width), f32),
            pltpu.VMEM((max(n_lo - 1, 1), PIECE, width), f32),
            pltpu.VMEM((3, n_z, n_x, PIECE, width), bf16),
            pltpu.VMEM((3, n_z, n_x, PIECE, tok), bf16),
            pltpu.VMEM((2, n_rep * n_lo, PIECE, width), bf16),
            pltpu.VMEM((width + tok, heads * tok), bf16),
            pltpu.VMEM((lat, heads * tok), f32),
            pltpu.VMEM((1, heads * tok), f32),
            pltpu.VMEM((1, heads * tok), f32),
            dma((9,)),
            dma,
            dma,
            dma((max(n_lo - 1, 1),)),
            dma((max(n_lo - 1, 1),)),
            dma((half + 1, max(n_x - 1, 1))),
            dma((half + 1, max(n_x - 1, 1))),
            dma((half + 1,)),
            dma((half + 1,)),
            dma((half + 1,)),
            dma((half + 1,)),
            dma((max(n_x - 1, 1),)),
            dma((max(n_x - 1, 1),)),
            dma,
            dma,
            dma((2, half + 1)),
            dma((2, half + 1)),
            dma((2, half + 1)),
            dma((2, half + 1)),
            dma((max(n_rep - 1, 1),)),
            dma((max(n_rep - 1, 1),)),
            dma,
            dma,
        ],
        compiler_params=pltpu.CompilerParams(
            collective_id=0, has_side_effects=True, vmem_limit_bytes=56 * 1024 * 1024
        ),
    )(
        prefix_lengths,
        placements,
        jnp.asarray(frequency),
        kv_gain.reshape(1, lat),
        hidden[0],
        q_nope[0],
        q_rope[0],
        w_latent,
        w_krope.T,
        w_uk,
        w_uv,
        prefix_latent[0],
        prefix_rope[0],
    )
    return tuple(result[None] for result in out)


def program(mesh, shape):
    return jax.shard_map(
        functools.partial(per_device, shape),
        mesh=mesh,
        in_specs=(
            P("replica", "context", "tensor"),
            P("replica", "context", "tensor"),
            P("replica", "context", "tensor"),
            P("tensor", None),
            P("tensor", None),
            P(),
            P("tensor", None, None),
            P("tensor", None, None),
            P("replica", "context", None),
            P("replica", "context", None),
            P("replica"),
            P("context", None),
        ),
        out_specs=(
            P("replica", "context", "tensor"),
            P("replica", "context", None),
            P("replica", "context", None),
            P("replica", "context", None),
        ),
        check_vma=False,
    )


def solution(mesh):
    n_hi = 4
    return program(
        mesh,
        (
            mesh.shape["replica"],
            mesh.shape["context"] // n_hi,
            n_hi,
            mesh.shape["tensor"] // 2,
        ),
    )
```
